256 devices in a mesh: gx: 8 (over z_hi, core), gy: 8 (over y, z_lo), gz: 4 (over x).
Axes of the slice: x: 4, y: 4, z: 8 (z_hi: 4, z_lo: 2; z = z_hi * 2 + z_lo), core: 2. Of those that a mesh axis runs over, the one named last changes fastest.
Arguments:
- displacement: float32 [3, 64, 128, 512], P(None, 'gx', 'gy', 'gz'), may hold values from -0.16 to 0.16
- velocity: float32 [3, 64, 128, 512], P(None, 'gx', 'gy', 'gz'), may hold values from -1.2 to 1.2
- stiffness: float32 [64, 128, 512], P('gx', 'gy', 'gz'), may hold values from 0.5 to 2
- broken: int32 [61, 64, 128, 512], P(None, 'gx', 'gy', 'gz'), may hold values 0 or 1
- borehole_id: int32 [64, 128, 512], P('gx', 'gy', 'gz'), may hold values from 0 to 7
- flags: int32 [64, 128, 512], P('gx', 'gy', 'gz'), may hold values 0 or 1
- pressure: float32 [8], replicated, may hold values from 0.5 to 4
Outputs:
- displacement_out: float32 [3, 64, 128, 512], P(None, 'gx', 'gy', 'gz')
- velocity_out: float32 [3, 64, 128, 512], P(None, 'gx', 'gy', 'gz')
- accel_out: float32 [3, 64, 128, 512], P(None, 'gx', 'gy', 'gz')
The draws below stay inside these ranges and needn't reach their ends.
All inputs are finite; a program needn't handle non-finite values. No bound on the sum of `broken` or of `flags` on one device may be relied on, other than what follows from the above.
Results may differ from the reference program's by a relative error of at most 0.00002.
Values sent between devices are 32-bit elements; how exact they have to be, the bound alone decides.
No kernel may reach another device: no remote copies, remote signals or barrier semaphores. Data moves between devices by JAX's collectives and lax.ppermute only.
A program may use at most 192 MiB of HBM per device.

```python
import math
import jax
import jax.numpy as jnp
from jax import lax

HALF = 61
NB = 8
STEPS = 2
NX = 64
NY = 128
NZ = 512


def place_ends(values, stream_key, low, high):
    longest = values.shape.index(max(values.shape))
    spots = []
    for shift in (0, 1):
        where = [jax.random.randint(jax.random.fold_in(stream_key, axis), (), 0, length) for axis, length in enumerate(values.shape)]
        where[longest] = (where[longest] + shift) % values.shape[longest]
        spots.append(tuple(where))
    return values.at[spots[0]].set(low).at[spots[1]].set(high)


def block_levels(own_key, dims, pieces, low, top_value):
    def one(dim, parts):
        draws = jax.random.uniform(jax.random.fold_in(jax.random.fold_in(own_key, 6), dim), (parts,), jnp.float32, low / len(pieces), top_value / len(pieces))
        return jnp.repeat(jnp.exp(draws), dims[dim] // parts).reshape((-1,) + (1,) * (len(dims) - dim - 1))

    gain = one(*pieces[0])
    for cut in pieces[1:]:
        gain = gain * one(*cut)
    return gain


def normal_values(stream_key, shape, spread, most, split=(), held_as=jnp.bfloat16):
    entries = jax.random.normal(stream_key, shape, jnp.float32) * spread
    if len(split) > 0:
        entries = block_levels(stream_key, shape, split, -0.22, 0.18) * entries
    return jnp.clip(entries, min=-most, max=most).astype(held_as)


def setup_inputs(seed: int = 0) -> dict:
    key_of = jax.random.split(jax.random.key(seed), 8)
    displacement = normal_values(key_of[0], (3, NX, NY, NZ), 0.04, 0.16, ((1, 8), (2, 8), (3, 4)), jnp.float32)
    velocity = normal_values(key_of[1], (3, NX, NY, NZ), 0.3, 1.2, ((1, 8), (2, 8), (3, 4)), jnp.float32)
    stiffness = jnp.clip(jnp.exp(math.log(2.0) - 1.3862944 * jax.random.uniform(key_of[2], (NX, NY, NZ), jnp.float32) ** block_levels(key_of[2], (NX, NY, NZ), ((0, 8), (1, 8), (2, 4)), -0.2, 0.2)), 0.5, 2.0)
    broken = place_ends((jax.random.randint(key_of[3], (HALF, NX, NY, NZ), 0, 5) < 1).astype(jnp.int32), jax.random.fold_in(key_of[3], 1), 0, 1)
    borehole_id = place_ends(jax.random.randint(key_of[4], (NX, NY, NZ), 0, NB), jax.random.fold_in(key_of[4], 1), 0, NB - 1).astype(jnp.int32)
    flags = place_ends((jax.random.randint(key_of[5], (NX, NY, NZ), 0, 2) < 1).astype(jnp.int32), jax.random.fold_in(key_of[5], 1), 0, 1)
    pressure = jnp.clip(jnp.exp(jax.random.uniform(key_of[6], (NB,), jnp.float32, math.log(0.5), math.log(4.0))), 0.5, 4.0)
    return {"displacement": displacement, "velocity": velocity, "stiffness": stiffness, "broken": broken, "borehole_id": borehole_id, "flags": flags, "pressure": pressure}


C_BOND = 3.0
DT_STEP = 0.04

def half_offsets():
    result = []
    for step_x in range(0, 4):
        for step_y in range(-3, 4):
            for step_z in range(-3, 4):
                square = step_x * step_x + step_y * step_y + step_z * step_z
                if square == 0 or square > 9:
                    continue
                if step_x > 0 or (step_x == 0 and (step_y > 0 or (step_y == 0 and step_z > 0))):
                    result.append((step_x, step_y, step_z))
    return result

def bond_force(motion_own, motion_far, stiff_own, stiff_far, weight_keep, offset):
    radial = [float(offset[dimension]) + (motion_far[dimension] - motion_own[dimension]) for dimension in range(3)]
    length = jnp.sqrt(radial[0] * radial[0] + radial[1] * radial[1] + radial[2] * radial[2])
    rest_length = math.sqrt(offset[0] ** 2 + offset[1] ** 2 + offset[2] ** 2)
    factor = weight_keep * (0.5 * C_BOND) * (stiff_own + stiff_far) * ((length - rest_length) / rest_length) / length
    return jnp.stack([factor * radial[0], factor * radial[1], factor * radial[2]])

def pore_pressure(borehole_id, flags, pressure):
    labels = jnp.arange(pressure.shape[0], dtype=jnp.int32)
    matches = borehole_id[None] == labels[:, None, None, None]
    return flags.astype(pressure.dtype) * lax.optimization_barrier(jnp.sum(jnp.where(matches, pressure[:, None, None, None], 0.0), axis=0))

def pressure_force(pore_field):
    components = []
    for dimension in range(3):
        half_diff = -0.5 * jnp.diff(pore_field, axis=dimension)
        widths_up = [(0, 0), (0, 0), (0, 0)]
        widths_down = [(0, 0), (0, 0), (0, 0)]
        widths_up[dimension] = (0, 1)
        widths_down[dimension] = (1, 0)
        components.append(jnp.pad(half_diff, widths_up) + jnp.pad(half_diff, widths_down))
    return jnp.stack(components)

def forces(motion, stiffness, broken, pressing):
    padding = ((3, 3), (3, 3), (3, 3))
    motion_pad = jnp.pad(motion, ((0, 0),) + padding)
    stiff_pad = jnp.pad(stiffness, padding)
    inside_pad = jnp.pad(jnp.ones_like(stiffness), padding)
    extent = stiffness.shape
    reaction = jnp.zeros_like(motion_pad)
    summed = pressing
    for bond_index, offset in enumerate(half_offsets()):
        window = tuple((slice(3 + offset[dimension], 3 + offset[dimension] + extent[dimension]) for dimension in range(3)))
        weight_keep = (1 - broken[bond_index]).astype(stiffness.dtype) * inside_pad[window]
        bond_term = bond_force(motion, motion_pad[(slice(None),) + window], stiffness, stiff_pad[window], weight_keep, offset)
        summed = summed + bond_term
        reaction = reaction.at[(slice(None),) + window].add(-bond_term)
    return summed + reaction[:, 3:-3, 3:-3, 3:-3]

def reference(displacement, velocity, stiffness, broken, borehole_id, flags, pressure):
    pressing = pressure_force(pore_pressure(borehole_id, flags, pressure))
    accel = forces(displacement, stiffness, broken, pressing)
    motion = displacement
    speed = velocity
    for step_index in range(STEPS):
        halfway = speed + 0.5 * DT_STEP * accel
        motion = motion + DT_STEP * halfway
        accel = forces(motion, stiffness, broken, pressing)
        speed = halfway + 0.5 * DT_STEP * accel
    return (motion, speed, accel)
```

```python
import functools
import math

import jax
import jax.numpy as jnp
from jax import lax
from jax.experimental import pallas as pl
from jax.experimental.pallas import tpu as pltpu
from jax.sharding import PartitionSpec as P

STEPS = 2
C_BOND = 3.0
DT_STEP = 0.04
REACH = 3
LANES = 128
SLOT = 16
HALF_DT = 0.5 * DT_STEP


def half_offsets():
    result = []
    for step_x in range(0, 4):
        for step_y in range(-3, 4):
            for step_z in range(-3, 4):
                square = step_x * step_x + step_y * step_y + step_z * step_z
                if square == 0 or square > 9:
                    continue
                if step_x > 0 or (step_x == 0 and (step_y > 0 or (step_y == 0 and step_z > 0))):
                    result.append((step_x, step_y, step_z))
    return result


OFFSETS = half_offsets()
BONDS = {step: [] for step in range(-REACH, REACH + 1)}
for _plane, (_a, _b, _c) in enumerate(OFFSETS):
    BONDS[_a].append((_b, _c, _plane, True))
    BONDS[-_a].append((-_b, -_c, _plane, False))


def inner_layers(step, extent):
    return max(0, -step), min(extent, extent - step)


def outer_layers(step, extent):
    return (extent - step, extent) if step > 0 else (0, -step)


def slot_bases(extent, layers_of, steps):
    bases, total = {}, 0
    for step in steps:
        bases[step] = total
        low, high = layers_of(step, extent)
        total += (high - low) * len(BONDS[step])
    return bases, total


STEPS_ALL = list(range(-REACH, REACH + 1))
STEPS_OUT = [step for step in STEPS_ALL if step != 0]


def round_up(count):
    return (count + 7) // 8 * 8


def running(amounts):
    places, total = {}, 0
    for plane, amount in amounts:
        places[plane] = total
        total += amount
    return places, total


Z_UP, Z_UP_COUNT = running([(k, c) for k, (a, b, c) in enumerate(OFFSETS) if c > 0])
Z_DOWN, Z_DOWN_COUNT = running([(k, -c) for k, (a, b, c) in enumerate(OFFSETS) if c < 0])
Y_UP, Y_UP_COUNT = running([(k, b) for k, (a, b, c) in enumerate(OFFSETS) if b > 0])
Y_DOWN, Y_DOWN_COUNT = running([(k, -b) for k, (a, b, c) in enumerate(OFFSETS) if b < 0])
X_UP, X_UP_COUNT = running([(k, a) for k, (a, b, c) in enumerate(OFFSETS) if a > 0])
XY_UP, XY_UP_COUNT = running([(k, a * abs(b)) for k, (a, b, c) in enumerate(OFFSETS) if a * abs(b) > 0])


def lanes_like(value):
    return lax.broadcasted_iota(jnp.int32, value.shape, value.ndim - 1)


def rolled(value, shift):
    shift = shift % LANES
    return value if shift == 0 else pltpu.roll(value, shift, value.ndim - 1)


def beside_columns(low_pack, high_pack, lane_of):
    lanes = lanes_like(low_pack)
    return jnp.where(
        lanes < REACH, rolled(high_pack, -lane_of), rolled(low_pack, LANES - REACH - lane_of)
    )


def moved(main, beside, step):
    if step == 0:
        return main
    lanes = lanes_like(main)
    if step > 0:
        return rolled(jnp.where(lanes < step, beside, main), -step)
    return rolled(jnp.where(lanes >= LANES + step, beside, main), -step)


def pack_columns(field_of, count, extent, height):
    lanes = lax.broadcasted_iota(jnp.int32, (height, LANES), 1)
    up = jnp.zeros((height, LANES), jnp.float32)
    down = up
    for layer in range(extent):
        for field in range(count):
            lane_of = layer * SLOT + field * REACH
            value = field_of(field, layer)
            here = (lanes >= lane_of) & (lanes < lane_of + REACH)
            up = jnp.where(here, rolled(value, lane_of - (LANES - REACH)), up)
            down = jnp.where(here, rolled(value, lane_of), down)
    return up, down


def kept(flag, value):
    return jnp.where(flag > 0, value, 0.0)


def start_kernel(extent, pressure, motion, stiffness, borehole, flags, broken, pore, z_up, z_down, x_up):
    size_x, size_y, _ = extent
    ids = borehole[...]
    level = jnp.zeros(ids.shape, jnp.float32)
    for label in range(pressure.shape[0]):
        level = jnp.where(ids == label, pressure[label], level)
    pore[...] = flags[...].astype(jnp.float32) * level

    def field_of(field, layer):
        if field < 3:
            return motion[field, layer]
        return stiffness[layer] if field == 3 else pore[layer]

    up, down = pack_columns(field_of, 5, size_x, size_y)
    z_up[0:size_y] = up
    z_down[0:size_y] = down

    def one_layer(layer, carry):
        lanes = lax.broadcasted_iota(jnp.int32, (size_y, LANES), 1)
        rows = pl.ds(size_y + layer * size_y, size_y)
        up = jnp.zeros((size_y, LANES), jnp.float32)
        down = up
        for plane, (_, _, c) in enumerate(OFFSETS):
            if c > 0:
                at = Z_UP[plane]
                value = broken[plane, layer].astype(jnp.float32)
                up = jnp.where((lanes >= at) & (lanes < at + c), rolled(value, at + c), up)
            if c < 0:
                at = Z_DOWN[plane]
                value = broken[plane, layer].astype(jnp.float32)
                down = jnp.where((lanes >= at) & (lanes < at - c), rolled(value, at), down)
        z_up[rows] = up
        z_down[rows] = down
        return carry

    lax.fori_loop(0, size_x, one_layer, 0)
    for plane, (a, _, _) in enumerate(OFFSETS):
        for layer in range(a):
            at = (X_UP[plane] + layer) * size_y
            x_up[at : at + size_y] = broken[plane, size_x - a + layer].astype(jnp.float32)


def copy_y_rows(field_of, count, extent, low_pack, high_pack, y_up, y_down):
    size_x, size_y, _ = extent
    for field in range(count):
        for layer in range(size_x):
            at = (field * size_x + layer) * REACH
            y_up[at : at + REACH] = field_of(field, layer, slice(size_y - REACH, size_y))
            y_down[at : at + REACH] = field_of(field, layer, slice(0, REACH))
    at = count * size_x * REACH
    for pack in (low_pack, high_pack):
        y_up[at : at + REACH] = pack[size_y - REACH : size_y]
        y_down[at : at + REACH] = pack[0:REACH]
        at += REACH
    return at


def y_rows_kernel(extent, edges, motion, z_low, z_high, y_up, y_down):
    size_y = extent[1]
    low_pack = kept(edges[0], z_low[0:size_y])
    high_pack = kept(edges[1], z_high[0:size_y])
    copy_y_rows(
        lambda field, layer, rows: motion[field, layer, rows],
        3, extent, low_pack, high_pack, y_up, y_down,
    )


def y_rows_first_kernel(extent, edges, motion, stiffness, pore, broken, z_low, z_high, y_up, y_down):
    size_x, size_y, _ = extent
    low_pack = kept(edges[0], z_low[0:size_y])
    high_pack = kept(edges[1], z_high[0:size_y])

    def field_of(field, layer, rows):
        if field < 3:
            return motion[field, layer, rows]
        return stiffness[layer, rows] if field == 3 else pore[layer, rows]

    base = copy_y_rows(field_of, 5, extent, low_pack, high_pack, y_up, y_down)
    for plane, (_, b, _) in enumerate(OFFSETS):
        for layer in range(size_x):
            if b > 0:
                at = base + Y_UP[plane] * size_x + layer * b
                y_up[at : at + b] = broken[plane, layer, size_y - b : size_y].astype(jnp.float32)
            if b < 0:
                at = base + Y_DOWN[plane] * size_x - layer * b
                y_down[at : at - b] = broken[plane, layer, 0:-b].astype(jnp.float32)
    for order, pack in enumerate((z_low, z_high)):
        for layer in range(size_x):
            first = size_y + layer * size_y
            at = (order * size_x + layer) * REACH
            to_up = base + Y_UP_COUNT * size_x + at
            to_down = base + Y_DOWN_COUNT * size_x + at
            y_up[to_up : to_up + REACH] = pack[first + size_y - REACH : first + size_y]
            y_down[to_down : to_down + REACH] = pack[first : first + REACH]


def widen(target, low_rows, middle, high_rows):
    size_y = middle.shape[0]
    target[0:REACH] = low_rows
    target[REACH : REACH + size_y] = middle
    target[REACH + size_y : 2 * REACH + size_y] = high_rows
    height = target.shape[0]
    target[2 * REACH + size_y : height] = jnp.zeros((height - 2 * REACH - size_y, LANES), jnp.float32)


def widen_fields(edges, field_of, count, extent, z_low, z_high, y_low, y_high, wide, wide_pack):
    size_x, size_y, _ = extent
    for field in range(count):
        for layer in range(size_x):
            at = (field * size_x + layer) * REACH
            widen(
                wide.at[field, layer],
                kept(edges[2], y_low[at : at + REACH]),
                field_of(field, layer),
                kept(edges[3], y_high[at : at + REACH]),
            )
    at = count * size_x * REACH
    for order, pack in enumerate((z_low, z_high)):
        widen(
            wide_pack.at[order],
            kept(edges[2], y_low[at : at + REACH]),
            kept(edges[order], pack[0:size_y]),
            kept(edges[3], y_high[at : at + REACH]),
        )
        at += REACH
    return at


def copy_x_layers(count, size_x, wide, wide_pack, x_up, x_down):
    height = wide.shape[2]
    for field in range(count):
        for layer in range(REACH):
            at = (field * REACH + layer) * height
            x_up[at : at + height] = wide[field, size_x - REACH + layer]
            x_down[at : at + height] = wide[field, layer]
    at = count * REACH * height
    for order in range(2):
        x_up[at : at + height] = wide_pack[order]
        x_down[at : at + height] = wide_pack[order]
        at += height
    return at


def x_layers_kernel(
    extent, edges, motion, z_low, z_high, y_low, y_high, wide, wide_pack, x_up, x_down
):
    widen_fields(
        edges, lambda field, layer: motion[field, layer],
        3, extent, z_low, z_high, y_low, y_high, wide, wide_pack,
    )
    copy_x_layers(3, extent[0], wide, wide_pack, x_up, x_down)


def x_layers_first_kernel(
    extent, edges, motion, stiffness, pore, z_low, z_high, y_low, y_high,
    wide, wide_pack, wide_broken, x_up, x_down,
):
    size_x, size_y, _ = extent

    def field_of(field, layer):
        if field < 3:
            return motion[field, layer]
        return stiffness[layer] if field == 3 else pore[layer]

    base = widen_fields(
        edges, field_of, 5, extent, z_low, z_high, y_low, y_high, wide, wide_pack
    )
    for order, pack in enumerate((z_low, z_high)):
        for layer in range(size_x):
            first = size_y + layer * size_y
            at = (order * size_x + layer) * REACH
            from_low = base + Y_UP_COUNT * size_x + at
            from_high = base + Y_DOWN_COUNT * size_x + at
            widen(
                wide_broken.at[order, layer],
                y_low[from_low : from_low + REACH],
                pack[first : first + size_y],
                y_high[from_high : from_high + REACH],
            )
    at = copy_x_layers(5, size_x, wide, wide_pack, x_up, x_down)
    height = wide.shape[2]
    for order in range(2):
        for layer in range(REACH):
            x_up[at : at + height] = wide_broken[order, size_x - REACH + layer]
            at += height
    for plane, (a, b, _) in enumerate(OFFSETS):
        if a * b == 0:
            continue
        rows, many = abs(b), a * abs(b)
        source = y_low if b > 0 else y_high
        first = base + (Y_UP if b > 0 else Y_DOWN)[plane] * size_x + (size_x - a) * rows
        x_up[at + XY_UP[plane] : at + XY_UP[plane] + many] = source[first : first + many]


def fill_shifts(shifts, place, main, low_pack, high_pack, lane_of, field, add_step):
    beside = beside_columns(low_pack, high_pack, lane_of)
    for step in range(-REACH, REACH + 1):
        value = moved(main, beside, step)
        if add_step and step:
            value = value + float(step)
        shifts[(step + REACH, field) + place] = value


def wanted_keep(low_broken, high_broken, rows_of, plane, step_z):
    value, low, high = rows_of
    if step_z == 0:
        return 1.0 - value
    lanes = lanes_like(value)
    if step_z < 0:
        beside = rolled(low, -Z_UP[plane])
        value = jnp.where(lanes < -step_z, beside, rolled(value, -step_z))
    else:
        beside = rolled(high, LANES - step_z - Z_DOWN[plane])
        value = jnp.where(lanes >= LANES - step_z, beside, rolled(value, -step_z))
    return 1.0 - value


def weights_inner_kernel(
    extent, stiffness, wide, wide_pack, wide_broken, broken, y_low, y_high, weights,
    shifts, planes,
):
    size_x, size_y, _ = extent
    for layer in range(size_x):
        fill_shifts(
            shifts, (layer,), wide[0, layer], wide_pack[0], wide_pack[1],
            layer * SLOT + 3 * REACH, 0, False,
        )
    base = 5 * size_x * REACH + 2 * REACH
    for plane, (_, b, _) in enumerate(OFFSETS):

        def fill(layer, carry, plane=plane):
            planes[plane, layer, REACH : REACH + size_y] = broken[plane, layer].astype(jnp.float32)
            return carry

        lax.fori_loop(0, size_x, fill, 0)
        for layer in range(size_x):
            if b > 0:
                at = base + Y_UP[plane] * size_x + layer * b
                planes[plane, layer, REACH - b : REACH] = y_low[at : at + b]
            if b < 0:
                at = base + Y_DOWN[plane] * size_x - layer * b
                planes[plane, layer, REACH + size_y : REACH + size_y - b] = y_high[at : at - b]
    bases, _ = slot_bases(size_x, inner_layers, STEPS_ALL)
    for step in STEPS_ALL:
        first, last = inner_layers(step, size_x)
        bonds = BONDS[step]

        def one_layer(layer, carry, step=step, first=first, bonds=bonds):
            slot = bases[step] + (layer - first) * len(bonds)
            far_layer = layer + step
            for tile in range(size_y // 8):
                rows = slice(8 * tile, 8 * tile + 8)
                own = stiffness[layer, rows]
                for order, (step_y, step_z, plane, owner) in enumerate(bonds):
                    far_rows = slice(REACH + step_y + 8 * tile, REACH + step_y + 8 * tile + 8)
                    far = shifts[step_z + REACH, 0, far_layer, far_rows]
                    if owner:
                        keep = 1.0 - broken[plane, layer, rows].astype(jnp.float32)
                    else:
                        keep = wanted_keep(
                            None, None,
                            (
                                planes[plane, far_layer, far_rows],
                                wide_broken[0, far_layer, far_rows],
                                wide_broken[1, far_layer, far_rows],
                            ),
                            plane, step_z,
                        )
                    value = keep * (0.5 * C_BOND) * (own + far)
                    weights[slot + order, rows] = jnp.where(far > 0.0, value, 0.0)
            return carry

        lax.fori_loop(first, last, one_layer, 0)


def weights_outer_kernel(
    extent, edges, stiffness, pore, wide, wide_pack, broken, x_broken, x_low, x_high,
    weights, pressing, shifts, planes,
):
    size_x, size_y, _ = extent
    height = wide.shape[2]
    pack_at = 5 * REACH * height
    broken_at = pack_at + 2 * height
    rows_at = broken_at + 2 * REACH * height

    def pack_of(source, order):
        return source[pack_at + order * height : pack_at + (order + 1) * height]

    for side, source in enumerate((x_low, x_high)):
        for layer in range(REACH):
            at = (3 * REACH + layer) * height
            from_layer = size_x - REACH + layer if side == 0 else layer
            fill_shifts(
                shifts, (side * REACH + layer,),
                kept(edges[4 + side], source[at : at + height]),
                kept(edges[4 + side], pack_of(source, 0)),
                kept(edges[4 + side], pack_of(source, 1)),
                from_layer * SLOT + 3 * REACH, 0, False,
            )
    for plane, (a, b, _) in enumerate(OFFSETS):
        for layer in range(a):
            at = (X_UP[plane] + layer) * size_y
            place = X_UP[plane] + layer
            planes[place, REACH : REACH + size_y] = x_broken[at : at + size_y]
            at = rows_at + XY_UP.get(plane, 0) + layer * abs(b)
            if b > 0:
                planes[place, REACH - b : REACH] = x_low[at : at + b]
            if b < 0:
                planes[place, REACH + size_y : REACH + size_y - b] = x_low[at : at - b]
    bases, _ = slot_bases(size_x, outer_layers, STEPS_OUT)
    for step in STEPS_OUT:
        first, last = outer_layers(step, size_x)
        bonds = BONDS[step]
        for layer in range(first, last):
            slot = bases[step] + (layer - first) * len(bonds)
            far_layer = layer + step
            far_layer = far_layer + REACH if far_layer < 0 else far_layer - size_x + REACH
            for tile in range(size_y // 8):
                rows = slice(8 * tile, 8 * tile + 8)
                own = stiffness[layer, rows]
                for order, (step_y, step_z, plane, owner) in enumerate(bonds):
                    far_rows = slice(REACH + step_y + 8 * tile, REACH + step_y + 8 * tile + 8)
                    far = shifts[step_z + REACH, 0, far_layer, far_rows]
                    if owner:
                        keep = 1.0 - broken[plane, layer, rows].astype(jnp.float32)
                    else:
                        low_at = broken_at + far_layer * height
                        high_at = low_at + REACH * height
                        moved_rows = slice(far_rows.start + low_at, far_rows.stop + low_at)
                        moved_high = slice(far_rows.start + high_at, far_rows.stop + high_at)
                        keep = wanted_keep(
                            None, None,
                            (
                                planes[X_UP[plane] + layer, far_rows],
                                x_low[moved_rows],
                                x_low[moved_high],
                            ),
                            plane, step_z,
                        )
                    value = keep * (0.5 * C_BOND) * (own + far)
                    weights[slot + order, rows] = jnp.where(far > 0.0, value, 0.0)

    middle = slice(REACH, REACH + size_y)

    def wide_field(field, layer):
        if layer < 0 or layer >= size_x:
            source = x_low if layer < 0 else x_high
            at = (field * REACH + (layer + REACH if layer < 0 else layer - size_x)) * height
            return kept(edges[4 if layer < 0 else 5], source[at : at + height])
        return wide[field - 3, layer]

    for layer in range(size_x):
        own = pore[layer]
        for axis in range(3):
            total = jnp.zeros((size_y, LANES), jnp.float32)
            for sign in (1, -1):
                if axis == 0:
                    inside = wide_field(3, layer + sign)[middle]
                    level = wide_field(4, layer + sign)[middle]
                elif axis == 1:
                    rows = slice(REACH + sign, REACH + sign + size_y)
                    inside = wide[0, layer, rows]
                    level = wide[1, layer, rows]
                else:
                    inside, level = (
                        moved(
                            wide[field - 3, layer],
                            beside_columns(
                                wide_pack[0], wide_pack[1], layer * SLOT + field * REACH
                            ),
                            sign,
                        )[middle]
                        for field in (3, 4)
                    )
                total = total + jnp.where(inside > 0.0, (-0.5 * sign) * (level - own), 0.0)
            pressing[axis, layer] = total


def add_bonds(extent, step, layer, far_layer, motion, shifts, weights, slot, total):
    size_y = extent[1]
    for tile in range(size_y // 8):
        rows = slice(8 * tile, 8 * tile + 8)
        own = [motion[axis, layer, rows] for axis in range(3)]
        near_x = own[0] - float(step)
        near_y = {step_y: own[1] - float(step_y) for step_y in range(-REACH, REACH + 1)}
        force = [total[axis, layer, rows] for axis in range(3)]
        for order, (step_y, step_z, plane, _) in enumerate(BONDS[step]):
            far_rows = slice(REACH + step_y + 8 * tile, REACH + step_y + 8 * tile + 8)
            far = [shifts[step_z + REACH, axis, far_layer, far_rows] for axis in range(3)]
            radial = [far[0] - near_x, far[1] - near_y[step_y], far[2] - own[2]]
            square = radial[0] * radial[0] + radial[1] * radial[1] + radial[2] * radial[2]
            rest = math.sqrt(sum(part * part for part in OFFSETS[plane]))
            factor = weights[slot + order, rows] * (1.0 / rest - lax.rsqrt(square))
            force = [force[axis] + factor * radial[axis] for axis in range(3)]
        for axis in range(3):
            total[axis, layer, rows] = force[axis]


def force_inner_kernel(extent, motion, wide, wide_pack, weights, total, shifts):
    size_x = extent[0]
    total[...] = jnp.zeros(total.shape, jnp.float32)
    for layer in range(size_x):
        for axis in range(3):
            fill_shifts(
                shifts, (layer,), wide[axis, layer], wide_pack[0], wide_pack[1],
                layer * SLOT + axis * REACH, axis, axis == 2,
            )
    bases, _ = slot_bases(size_x, inner_layers, STEPS_ALL)
    for step in STEPS_ALL:
        first, last = inner_layers(step, size_x)

        def one_layer(layer, carry, step=step, first=first):
            slot = bases[step] + (layer - first) * len(BONDS[step])
            add_bonds(extent, step, layer, layer + step, motion, shifts, weights, slot, total)
            return carry

        lax.fori_loop(first, last, one_layer, 0)


def finish_kernel(extent, count, stage, edges, motion, speed, pressing, inner, weights, x_low, x_high, *refs):
    size_x, size_y, _ = extent
    if stage == "last":
        accel_out, speed_out, total, shifts = refs
    else:
        motion_out, speed_out, z_up, z_down, total, shifts = refs
    height = (x_low.shape[0] if stage != "first" else x_high.shape[0]) // (count * REACH + 2)
    total[...] = inner[...] + pressing[...]
    pack_at = count * REACH * height
    for side, source in enumerate((x_low, x_high)):
        packs = [
            kept(edges[4 + side], source[pack_at + order * height : pack_at + (order + 1) * height])
            for order in range(2)
        ]
        for layer in range(REACH):
            from_layer = size_x - REACH + layer if side == 0 else layer
            for axis in range(3):
                at = (axis * REACH + layer) * height
                fill_shifts(
                    shifts, (side * REACH + layer,),
                    kept(edges[4 + side], source[at : at + height]),
                    packs[0], packs[1], from_layer * SLOT + axis * REACH, axis, axis == 2,
                )
    bases, _ = slot_bases(size_x, outer_layers, STEPS_OUT)
    for step in STEPS_OUT:
        first, last = outer_layers(step, size_x)

        def one_layer(layer, carry, step=step, first=first):
            slot = bases[step] + (layer - first) * len(BONDS[step])
            far_layer = layer + step + (REACH if step < 0 else REACH - size_x)
            add_bonds(extent, step, layer, far_layer, motion, shifts, weights, slot, total)
            return carry

        lax.fori_loop(first, last, one_layer, 0)
    accel = total[...]
    new_speed = speed[...] + HALF_DT * accel
    if stage == "last":
        accel_out[...] = accel
        speed_out[...] = new_speed
        return
    if stage == "middle":
        new_speed = new_speed + HALF_DT * accel
    speed_out[...] = new_speed
    motion_out[...] = motion[...] + DT_STEP * new_speed
    up, down = pack_columns(lambda axis, layer: motion_out[axis, layer], 3, size_x, size_y)
    z_up[...] = up
    z_down[...] = down


VMEM = pl.BlockSpec(memory_space=pltpu.VMEM)
SMEM = pl.BlockSpec(memory_space=pltpu.SMEM)


def call(kernel, scalars, operands, shapes, scratch=(), name=None):
    return pl.pallas_call(
        kernel,
        out_shape=[jax.ShapeDtypeStruct(shape, jnp.float32) for shape in shapes],
        in_specs=[SMEM] * len(scalars) + [VMEM] * len(operands),
        out_specs=[VMEM] * len(shapes),
        scratch_shapes=[pltpu.VMEM(shape, jnp.float32) for shape in scratch],
        compiler_params=pltpu.CompilerParams(vmem_limit_bytes=56 * 1024 * 1024),
        name=name,
    )(*scalars, *operands)


def sent(value, axis, distance):
    count = lax.axis_size(axis)
    return lax.ppermute(value, axis, [(i, (i + distance) % count) for i in range(count)])


def on_device(displacement, velocity, stiffness, broken, borehole_id, flags, pressure):
    extent = stiffness.shape
    size_x, size_y, _ = extent
    height = size_y + 8
    edges = jnp.stack(
        [
            end
            for axis in ("gz", "gy", "gx")
            for end in (
                (lax.axis_index(axis) > 0).astype(jnp.int32),
                (lax.axis_index(axis) < lax.axis_size(axis) - 1).astype(jnp.int32),
            )
        ]
    )
    field = (size_x, size_y, LANES)
    vector = (3,) + field
    part = functools.partial

    pack = (size_y + size_x * size_y, LANES)
    pore, z_up, z_down, x_up = call(
        part(start_kernel, extent), [pressure],
        [displacement, stiffness, borehole_id, flags, broken],
        [field, pack, pack, (X_UP_COUNT * size_y, LANES)], name="start",
    )
    z_low = sent(z_up, "gz", 1)
    z_high = sent(z_down, "gz", -1)
    x_broken = sent(x_up, "gx", 1)
    base = 5 * size_x * REACH + 2 * REACH + 2 * size_x * REACH
    y_up, y_down = call(
        part(y_rows_first_kernel, extent), [edges],
        [displacement, stiffness, pore, broken, z_low, z_high],
        [
            (round_up(base + Y_UP_COUNT * size_x), LANES),
            (round_up(base + Y_DOWN_COUNT * size_x), LANES),
        ], name="y_rows_first",
    )
    y_low = sent(y_up, "gy", 1)
    y_high = sent(y_down, "gy", -1)
    layers = (5 * REACH + 2) * height
    wide, wide_pack, wide_broken, x_up, x_down = call(
        part(x_layers_first_kernel, extent), [edges],
        [displacement, stiffness, pore, z_low, z_high, y_low, y_high],
        [
            (5, size_x, height, LANES),
            (2, height, LANES),
            (2, size_x, height, LANES),
            (round_up(layers + 2 * REACH * height + XY_UP_COUNT), LANES),
            (layers, LANES),
        ], name="x_layers_first",
    )
    x_low = sent(x_up, "gx", 1)
    x_high = sent(x_down, "gx", -1)
    moves = 2 * REACH + 1
    inner_slots = slot_bases(size_x, inner_layers, STEPS_ALL)[1]
    outer_slots = slot_bases(size_x, outer_layers, STEPS_OUT)[1]
    (inner_weights,) = call(
        part(weights_inner_kernel, extent), [],
        [stiffness, wide[3:], wide_pack, wide_broken, broken, y_low, y_high],
        [(inner_slots, size_y, LANES)],
        [(moves, 1, size_x, height, LANES), (len(OFFSETS), size_x, height, LANES)],
        name="weights_inner",
    )

    def inner_force(motion, wide, wide_pack):
        return call(
            part(force_inner_kernel, extent), [], [motion, wide, wide_pack, inner_weights],
            [vector], [(moves, 3, size_x, height, LANES)], name="force_inner",
        )[0]

    inner = inner_force(displacement, wide[:3], wide_pack)
    outer_weights, pressing = call(
        part(weights_outer_kernel, extent), [edges],
        [stiffness, pore, wide[3:], wide_pack, broken, x_broken, x_low, x_high],
        [(outer_slots, size_y, LANES), vector],
        [(moves, 1, 2 * REACH, height, LANES), (X_UP_COUNT, height, LANES)],
        name="weights_outer",
    )

    def finish(stage, count, motion, speed, inner, x_low, x_high):
        columns = (size_y, LANES)
        shapes = [vector, vector] if stage == "last" else [vector, vector, columns, columns]
        return call(
            part(finish_kernel, extent, count, stage), [edges],
            [motion, speed, pressing, inner, outer_weights, x_low, x_high],
            shapes, [vector, (moves, 3, 2 * REACH, height, LANES)], name="finish_" + stage,
        )

    motion, speed, z_up, z_down = finish(
        "first", 5, displacement, velocity, inner, x_low, x_high
    )
    for step_index in range(STEPS):
        z_low = sent(z_up, "gz", 1)
        z_high = sent(z_down, "gz", -1)
        rows = (round_up(3 * size_x * REACH + 2 * REACH), LANES)
        y_up, y_down = call(
            part(y_rows_kernel, extent), [edges], [motion, z_low, z_high], [rows, rows],
            name="y_rows",
        )
        y_low = sent(y_up, "gy", 1)
        y_high = sent(y_down, "gy", -1)
        layers = (3 * REACH + 2) * height
        wide, wide_pack, x_up, x_down = call(
            part(x_layers_kernel, extent), [edges],
            [motion, z_low, z_high, y_low, y_high],
            [
                (3, size_x, height, LANES),
                (2, height, LANES),
                (layers, LANES),
                (layers, LANES),
            ], name="x_layers",
        )
        x_low = sent(x_up, "gx", 1)
        x_high = sent(x_down, "gx", -1)
        inner = inner_force(motion, wide, wide_pack)
        if step_index < STEPS - 1:
            motion, speed, z_up, z_down = finish("middle", 3, motion, speed, inner, x_low, x_high)
        else:
            accel, speed = finish("last", 3, motion, speed, inner, x_low, x_high)
    return (motion, speed, accel)


def solution(mesh):
    in_specs = (
        P(None, "gx", "gy", "gz"),
        P(None, "gx", "gy", "gz"),
        P("gx", "gy", "gz"),
        P(None, "gx", "gy", "gz"),
        P("gx", "gy", "gz"),
        P("gx", "gy", "gz"),
        P(),
    )
    out_specs = (P(None, "gx", "gy", "gz"), P(None, "gx", "gy", "gz"), P(None, "gx", "gy", "gz"))
    return jax.shard_map(
        on_device, mesh=mesh, in_specs=in_specs, out_specs=out_specs, check_vma=False
    )
```

```python
import functools
import math

import jax
import jax.numpy as jnp
from jax import lax
from jax.experimental import pallas as pl
from jax.experimental.pallas import tpu as pltpu
from jax.sharding import PartitionSpec as P

STEPS = 2
C_BOND = 3.0
DT_STEP = 0.04
REACH = 3
NEAR = 2
LANES = 128
SLOT = 16
PAD = 8
HALF_DT = 0.5 * DT_STEP


def half_offsets():
    result = []
    for step_x in range(0, 4):
        for step_y in range(-3, 4):
            for step_z in range(-3, 4):
                square = step_x * step_x + step_y * step_y + step_z * step_z
                if square == 0 or square > 9:
                    continue
                if step_x > 0 or (step_x == 0 and (step_y > 0 or (step_y == 0 and step_z > 0))):
                    result.append((step_x, step_y, step_z))
    return result


OFFSETS = half_offsets()
BONDS = {step: [] for step in range(-REACH, REACH + 1)}
for _plane, (_a, _b, _c) in enumerate(OFFSETS):
    BONDS[_a].append((_b, _c, _plane, True))
    BONDS[-_a].append((-_b, -_c, _plane, False))


def inner_layers(step, extent):
    return max(0, -step), min(extent, extent - step)


def outer_layers(step, extent):
    return (extent - step, extent) if step > 0 else (0, -step)


STEPS_ALL = list(range(-REACH, REACH + 1))
STEPS_OUT = [step for step in STEPS_ALL if step != 0]


def tiled_bonds(step, tiles):
    early, late = [], []
    for tile in range(tiles):
        for bond in BONDS[step]:
            low, high = 8 * tile + bond[0], 8 * tile + 8 + bond[0]
            (early if low >= 0 and high <= 8 * tiles else late).append((tile, *bond))
    return early, late


def inner_plan(extent, late):
    plan, total = [], 0
    for step in STEPS_ALL:
        bonds = tiled_bonds(step, extent[1] // 8)[int(late)]
        first, last = inner_layers(step, extent[0])
        plan.append((step, first, last, bonds, total))
        total += (last - first) * len(bonds)
    return plan, total


def outer_plan(extent):
    plan, total = [], 0
    for step in STEPS_OUT:
        bonds = [(tile, *bond) for tile in range(extent[1] // 8) for bond in BONDS[step]]
        first, last = outer_layers(step, extent[0])
        plan.append((step, first, last, bonds, total))
        total += (last - first) * len(bonds)
    return plan, total


def reach_z(distance):
    return max(abs(c) for a, b, c in OFFSETS if a >= distance)


def round_up(count):
    return (count + 7) // 8 * 8


def running(amounts):
    places, total = {}, 0
    for plane, amount in amounts:
        places[plane] = total
        total += amount
    return places, total


Z_UP, Z_UP_COUNT = running([(k, c) for k, (a, b, c) in enumerate(OFFSETS) if c > 0])
Z_DOWN, Z_DOWN_COUNT = running([(k, -c) for k, (a, b, c) in enumerate(OFFSETS) if c < 0])
Y_UP, Y_UP_COUNT = running([(k, b) for k, (a, b, c) in enumerate(OFFSETS) if b > 0])
Y_DOWN, Y_DOWN_COUNT = running([(k, -b) for k, (a, b, c) in enumerate(OFFSETS) if b < 0])
X_UP, X_UP_COUNT = running([(k, a) for k, (a, b, c) in enumerate(OFFSETS) if a > 0])
XY_UP, XY_UP_COUNT = running([(k, a * abs(b)) for k, (a, b, c) in enumerate(OFFSETS) if a * abs(b) > 0])


def lanes_like(value):
    return lax.broadcasted_iota(jnp.int32, value.shape, value.ndim - 1)


def rolled(value, shift):
    shift = shift % LANES
    return value if shift == 0 else pltpu.roll(value, shift, value.ndim - 1)


def beside_columns(low_pack, high_pack, lane_of):
    lanes = lanes_like(low_pack)
    return jnp.where(
        lanes < REACH, rolled(high_pack, -lane_of), rolled(low_pack, LANES - REACH - lane_of)
    )


def moved(main, beside, step):
    if step == 0:
        return main
    lanes = lanes_like(main)
    if step > 0:
        return rolled(jnp.where(lanes < step, beside, main), -step)
    return rolled(jnp.where(lanes >= LANES + step, beside, main), -step)


def pack_columns(field_of, count, extent, height):
    lanes = lax.broadcasted_iota(jnp.int32, (height, LANES), 1)
    up = jnp.zeros((height, LANES), jnp.float32)
    down = up
    for layer in range(extent):
        for field in range(count):
            lane_of = layer * SLOT + field * REACH
            value = field_of(field, layer)
            here = (lanes >= lane_of) & (lanes < lane_of + REACH)
            up = jnp.where(here, rolled(value, lane_of - (LANES - REACH)), up)
            down = jnp.where(here, rolled(value, lane_of), down)
    return up, down


def kept(flag, value):
    return jnp.where(flag > 0, value, 0.0)


def start_kernel(
    extent, pressure_in, motion_in, stiffness_in, borehole_in, flags_in, broken_in,
    motion, stiffness, pore, z_up, z_down, rows_up, rows_down, x_up,
    broken, pressure, borehole, flags, field_sems, layer_sems,
):
    size_x, size_y, _ = extent
    pairs = (
        (pressure_in, pressure), (borehole_in, borehole), (flags_in, flags),
        (motion_in, motion), (stiffness_in, stiffness),
    )
    copies = [
        pltpu.make_async_copy(source, target, field_sems.at[place])
        for place, (source, target) in enumerate(pairs)
    ]

    def layer_copy(layer):
        return pltpu.make_async_copy(
            broken_in.at[:, layer], broken.at[:, layer], layer_sems.at[layer]
        )

    for copy in copies:
        copy.start()
    for layer in range(size_x):
        layer_copy(layer).start()
    for copy in copies:
        copy.wait()
    ids = borehole[...]
    level = jnp.zeros(ids.shape, jnp.float32)
    for label in range(pressure.shape[0]):
        level = jnp.where(ids == label, pressure[label], level)
    pore[...] = flags[...].astype(jnp.float32) * level

    def field_of(field, layer):
        if field < 3:
            return motion[field, layer]
        return stiffness[layer] if field == 3 else pore[layer]

    up, down = pack_columns(field_of, 5, size_x, size_y)
    z_up[0:size_y] = up
    z_down[0:size_y] = down

    def one_layer(layer, carry):
        layer_copy(layer).wait()
        lanes = lax.broadcasted_iota(jnp.int32, (size_y, LANES), 1)
        rows = pl.ds(size_y + layer * size_y, size_y)
        up = jnp.zeros((size_y, LANES), jnp.float32)
        down = up
        for plane, (_, _, c) in enumerate(OFFSETS):
            if c > 0:
                at = Z_UP[plane]
                value = broken[plane, layer].astype(jnp.float32)
                up = jnp.where((lanes >= at) & (lanes < at + c), rolled(value, at + c), up)
            if c < 0:
                at = Z_DOWN[plane]
                value = broken[plane, layer].astype(jnp.float32)
                down = jnp.where((lanes >= at) & (lanes < at - c), rolled(value, at), down)
        z_up[rows] = up
        z_down[rows] = down
        return carry

    lax.fori_loop(0, size_x, one_layer, 0)
    for plane, (a, _, _) in enumerate(OFFSETS):
        for layer in range(a):
            at = (X_UP[plane] + layer) * size_y
            x_up[at : at + size_y] = broken[plane, size_x - a + layer].astype(jnp.float32)
    for plane, (_, b, _) in enumerate(OFFSETS):
        for layer in range(size_x):
            if b > 0:
                at = PAD + Y_UP[plane] * size_x + layer * b
                rows_up[at : at + b] = broken[plane, layer, size_y - b : size_y].astype(jnp.float32)
            if b < 0:
                at = PAD + Y_DOWN[plane] * size_x - layer * b
                rows_down[at : at - b] = broken[plane, layer, 0:-b].astype(jnp.float32)


def copy_y_rows(field_of, count, extent, low_pack, high_pack, y_up, y_down):
    size_x, size_y, _ = extent
    for field in range(count):
        for layer in range(size_x):
            at = (field * size_x + layer) * REACH
            y_up[at : at + REACH] = field_of(field, layer, slice(size_y - REACH, size_y))
            y_down[at : at + REACH] = field_of(field, layer, slice(0, REACH))
    at = count * size_x * REACH
    for pack in (low_pack, high_pack):
        y_up[at : at + REACH] = pack[size_y - REACH : size_y]
        y_down[at : at + REACH] = pack[0:REACH]
        at += REACH
    return at


def y_rows_kernel(extent, edges, motion, z_low, z_high, y_up, y_down):
    size_y = extent[1]
    low_pack = kept(edges[0], z_low[0:size_y])
    high_pack = kept(edges[1], z_high[0:size_y])
    copy_y_rows(
        lambda field, layer, rows: motion[field, layer, rows],
        3, extent, low_pack, high_pack, y_up, y_down,
    )


def y_rows_first_kernel(extent, edges, motion, stiffness, pore, z_low, z_high, y_up, y_down):
    size_x, size_y, _ = extent
    low_pack = kept(edges[0], z_low[0:size_y])
    high_pack = kept(edges[1], z_high[0:size_y])

    def field_of(field, layer, rows):
        if field < 3:
            return motion[field, layer, rows]
        return stiffness[layer, rows] if field == 3 else pore[layer, rows]

    base = copy_y_rows(field_of, 5, extent, low_pack, high_pack, y_up, y_down)
    for order, pack in enumerate((z_low, z_high)):
        for layer in range(size_x):
            first = size_y + layer * size_y
            at = base + (order * size_x + layer) * REACH
            y_up[at : at + REACH] = pack[first + size_y - REACH : first + size_y]
            y_down[at : at + REACH] = pack[first : first + REACH]


def widen(target, low_rows, middle, high_rows):
    size_y = middle.shape[0]
    target[0:REACH] = low_rows
    target[REACH : REACH + size_y] = middle
    target[REACH + size_y : 2 * REACH + size_y] = high_rows
    height = target.shape[0]
    target[2 * REACH + size_y : height] = jnp.zeros((height - 2 * REACH - size_y, LANES), jnp.float32)


def widen_fields(edges, field_of, count, extent, z_low, z_high, y_low, y_high, target, wide_pack):
    size_x, size_y, _ = extent
    for field in range(count):
        for layer in range(size_x):
            at = (field * size_x + layer) * REACH
            widen(
                target(field).at[layer],
                kept(edges[2], y_low[at : at + REACH]),
                field_of(field, layer),
                kept(edges[3], y_high[at : at + REACH]),
            )
    at = count * size_x * REACH
    for order, pack in enumerate((z_low, z_high)):
        widen(
            wide_pack.at[order],
            kept(edges[2], y_low[at : at + REACH]),
            kept(edges[order], pack[0:size_y]),
            kept(edges[3], y_high[at : at + REACH]),
        )
        at += REACH
    return at


def copy_x_layers(count, size_x, target, wide_pack, x_up, x_down):
    height = wide_pack.shape[1]
    for field in range(count):
        for layer in range(REACH):
            at = (field * REACH + layer) * height
            x_up[at : at + height] = target(field)[size_x - REACH + layer]
            x_down[at : at + height] = target(field)[layer]
    at = count * REACH * height
    for order in range(2):
        x_up[at : at + height] = wide_pack[order]
        x_down[at : at + height] = wide_pack[order]
        at += height
    return at


def x_layers_kernel(
    extent, edges, motion, z_low, z_high, y_low, y_high, x_up, x_down, wide, wide_pack
):
    widen_fields(
        edges, lambda field, layer: motion[field, layer],
        3, extent, z_low, z_high, y_low, y_high, lambda field: wide.at[field], wide_pack,
    )
    copy_x_layers(3, extent[0], lambda field: wide.at[field], wide_pack, x_up, x_down)


def x_layers_first_kernel(
    extent, edges, motion, stiffness, pore, z_low, z_high, y_low, y_high, rows_low, rows_high,
    wide_static, wide_pack, wide_broken, x_up, x_down, wide,
):
    size_x, size_y, _ = extent

    def field_of(field, layer):
        if field < 3:
            return motion[field, layer]
        return stiffness[layer] if field == 3 else pore[layer]

    def target(field):
        return wide.at[field] if field < 3 else wide_static.at[field - 3]

    base = widen_fields(
        edges, field_of, 5, extent, z_low, z_high, y_low, y_high, target, wide_pack
    )
    for order, pack in enumerate((z_low, z_high)):
        for layer in range(size_x):
            first = size_y + layer * size_y
            at = base + (order * size_x + layer) * REACH
            widen(
                wide_broken.at[order, layer],
                y_low[at : at + REACH],
                pack[first : first + size_y],
                y_high[at : at + REACH],
            )
    at = copy_x_layers(4, size_x, target, wide_pack, x_up, x_down)
    height = wide.shape[2]
    x_up[at : at + height] = wide_static[1, size_x - 1]
    x_down[at : at + height] = wide_static[1, 0]
    at += height
    for order in range(2):
        for layer in range(NEAR):
            x_up[at : at + height] = wide_broken[order, size_x - NEAR + layer]
            at += height
    for plane, (a, b, _) in enumerate(OFFSETS):
        if a * b == 0:
            continue
        rows, many = abs(b), a * abs(b)
        source = rows_low if b > 0 else rows_high
        first = PAD + (Y_UP if b > 0 else Y_DOWN)[plane] * size_x + (size_x - a) * rows
        x_up[at + XY_UP[plane] : at + XY_UP[plane] + many] = source[first : first + many]


def each_shift(main, low_pack, high_pack, lane_of, add_step, reach=REACH):
    beside = beside_columns(low_pack, high_pack, lane_of) if reach else None
    for step in range(-reach, reach + 1):
        value = moved(main, beside, step)
        yield step + REACH, value + float(step) if add_step and step else value


def wanted_keep(value, low, high, plane, step_z):
    if step_z == 0:
        return 1.0 - value
    lanes = lanes_like(value)
    if step_z < 0:
        beside = rolled(low(), -Z_UP[plane])
        value = jnp.where(lanes < -step_z, beside, rolled(value, -step_z))
    else:
        beside = rolled(high(), LANES - step_z - Z_DOWN[plane])
        value = jnp.where(lanes >= LANES - step_z, beside, rolled(value, -step_z))
    return 1.0 - value


def weights_early_kernel(
    extent, edges, broken_in, stiffness, z_low, z_high, weights, keeps, shifts, planes, broken, sems
):
    size_x, size_y, _ = extent

    def layer_copy(layer):
        return pltpu.make_async_copy(broken_in.at[:, layer], broken.at[:, layer], sems.at[layer])

    for layer in range(size_x):
        layer_copy(layer).start()
    low_pack = kept(edges[0], z_low[0:size_y])
    high_pack = kept(edges[1], z_high[0:size_y])
    for layer in range(size_x):
        for order, value in each_shift(
            stiffness[layer], low_pack, high_pack, layer * SLOT + 3 * REACH, False
        ):
            shifts[order, layer, REACH : REACH + size_y] = value

    def fill(layer, carry):
        layer_copy(layer).wait()
        for plane in range(len(OFFSETS)):
            planes[plane, layer, REACH : REACH + size_y] = broken[plane, layer].astype(jnp.float32)
        return carry

    lax.fori_loop(0, size_x, fill, 0)
    for late, target in ((False, weights), (True, keeps)):
        for step, first, last, bonds, base in inner_plan(extent, late)[0]:

            def one_layer(layer, carry, step=step, first=first, bonds=bonds, base=base):
                slot = base + (layer - first) * len(bonds)
                far_layer = layer + step
                for order, (tile, step_y, step_z, plane, owner) in enumerate(bonds):
                    rows = slice(8 * tile, 8 * tile + 8)
                    far_rows = slice(REACH + step_y + 8 * tile, REACH + step_y + 8 * tile + 8)
                    if owner:
                        keep = 1.0 - broken[plane, layer, rows].astype(jnp.float32)
                    else:
                        at = size_y + far_layer * size_y + step_y + 8 * tile
                        keep = wanted_keep(
                            planes[plane, far_layer, far_rows],
                            lambda: z_low[pl.ds(at, 8)],
                            lambda: z_high[pl.ds(at, 8)],
                            plane, step_z,
                        )
                    keep = (0.5 * C_BOND) * keep
                    if not late:
                        far = shifts[step_z + REACH, far_layer, far_rows]
                        keep = jnp.where(far > 0.0, keep * (stiffness[layer, rows] + far), 0.0)
                    target[slot + order] = keep
                return carry

            lax.fori_loop(first, last, one_layer, 0)


def weights_late_kernel(
    extent, stiffness, wide, wide_pack, wide_broken, rows_low, rows_high, keeps, weights, shifts
):
    size_x, size_y, _ = extent
    for layer in range(size_x):
        for order, value in each_shift(
            wide[0, layer], wide_pack[0], wide_pack[1], layer * SLOT + 3 * REACH, False
        ):
            shifts[order, layer] = value
    for step, first, last, bonds, base in inner_plan(extent, True)[0]:

        def one_layer(layer, carry, step=step, first=first, bonds=bonds, base=base):
            slot = base + (layer - first) * len(bonds)
            far_layer = layer + step
            sublanes = lax.broadcasted_iota(jnp.int32, (8, LANES), 0)
            for order, (tile, step_y, step_z, plane, owner) in enumerate(bonds):
                rows = slice(8 * tile, 8 * tile + 8)
                far_rows = slice(REACH + step_y + 8 * tile, REACH + step_y + 8 * tile + 8)
                keep = keeps[slot + order]
                if not owner:
                    if step_y < 0:
                        at = PAD + Y_UP[plane] * size_x - far_layer * step_y
                        value = rows_low[pl.ds(at, 8)]
                        across = sublanes < -step_y
                    else:
                        at = PAD + Y_DOWN[plane] * size_x + far_layer * step_y + step_y - 8
                        value = rows_high[pl.ds(at, 8)]
                        across = sublanes >= 8 - step_y
                    halo = wanted_keep(
                        value,
                        lambda: wide_broken[0, far_layer, far_rows],
                        lambda: wide_broken[1, far_layer, far_rows],
                        plane, step_z,
                    )
                    keep = jnp.where(across, (0.5 * C_BOND) * halo, keep)
                far = shifts[step_z + REACH, far_layer, far_rows]
                weights[slot + order] = jnp.where(
                    far > 0.0, keep * (stiffness[layer, rows] + far), 0.0
                )
            return carry

        lax.fori_loop(first, last, one_layer, 0)


def weights_outer_kernel(
    extent, edges, stiffness, pore, wide, wide_pack, x_up, x_broken, x_low, x_high,
    weights, pressing, shifts, planes,
):
    size_x, size_y, _ = extent
    height = wide.shape[2]
    pack_at = 4 * REACH * height
    pore_at = pack_at + 2 * height
    broken_at = pore_at + height
    rows_at = broken_at + 2 * NEAR * height

    def pack_of(source, order):
        return source[pack_at + order * height : pack_at + (order + 1) * height]

    for side, source in enumerate((x_low, x_high)):
        packs = [kept(edges[4 + side], pack_of(source, order)) for order in range(2)]
        for layer in range(REACH):
            at = (3 * REACH + layer) * height
            from_layer = size_x - REACH + layer if side == 0 else layer
            distance = REACH - layer if side == 0 else layer + 1
            for order, value in each_shift(
                kept(edges[4 + side], source[at : at + height]), *packs,
                from_layer * SLOT + 3 * REACH, False, reach_z(distance),
            ):
                shifts[order, side * REACH + layer] = value
    for plane, (a, b, _) in enumerate(OFFSETS):
        for layer in range(a):
            at = (X_UP[plane] + layer) * size_y
            place = X_UP[plane] + layer
            planes[place, REACH : REACH + size_y] = x_broken[at : at + size_y]
            at = rows_at + XY_UP.get(plane, 0) + layer * abs(b)
            if b > 0:
                planes[place, REACH - b : REACH] = x_low[at : at + b]
            if b < 0:
                planes[place, REACH + size_y : REACH + size_y - b] = x_low[at : at - b]
    for step, first, last, bonds, base in outer_plan(extent)[0]:
        for layer in range(first, last):
            slot = base + (layer - first) * len(bonds)
            far_layer = layer + step
            far_layer = far_layer + REACH if far_layer < 0 else far_layer - size_x + REACH
            for order, (tile, step_y, step_z, plane, owner) in enumerate(bonds):
                rows = slice(8 * tile, 8 * tile + 8)
                far_rows = slice(REACH + step_y + 8 * tile, REACH + step_y + 8 * tile + 8)
                far = shifts[step_z + REACH, far_layer, far_rows]
                if owner:
                    at = (X_UP[plane] + layer - first) * size_y + 8 * tile
                    keep = 1.0 - x_up[at : at + 8]
                else:
                    low_at = broken_at + (far_layer + NEAR - REACH) * height
                    high_at = low_at + NEAR * height
                    keep = wanted_keep(
                        planes[X_UP[plane] + layer, far_rows],
                        lambda: x_low[far_rows.start + low_at : far_rows.stop + low_at],
                        lambda: x_low[far_rows.start + high_at : far_rows.stop + high_at],
                        plane, step_z,
                    )
                value = keep * (0.5 * C_BOND) * (stiffness[layer, rows] + far)
                weights[slot + order] = jnp.where(far > 0.0, value, 0.0)

    middle = slice(REACH, REACH + size_y)

    def wide_field(field, layer):
        if layer < 0 or layer >= size_x:
            source = x_low if layer < 0 else x_high
            at = (field * REACH + (layer + REACH if layer < 0 else layer - size_x)) * height
            at = pore_at if field == 4 else at
            return kept(edges[4 if layer < 0 else 5], source[at : at + height])
        return wide[field - 3, layer]

    for layer in range(size_x):
        own = pore[layer]
        for axis in range(3):
            total = jnp.zeros((size_y, LANES), jnp.float32)
            for sign in (1, -1):
                if axis == 0:
                    inside = wide_field(3, layer + sign)[middle]
                    level = wide_field(4, layer + sign)[middle]
                elif axis == 1:
                    rows = slice(REACH + sign, REACH + sign + size_y)
                    inside = wide[0, layer, rows]
                    level = wide[1, layer, rows]
                else:
                    inside, level = (
                        moved(
                            wide[field - 3, layer],
                            beside_columns(
                                wide_pack[0], wide_pack[1], layer * SLOT + field * REACH
                            ),
                            sign,
                        )[middle]
                        for field in (3, 4)
                    )
                total = total + jnp.where(inside > 0.0, (-0.5 * sign) * (level - own), 0.0)
            pressing[axis, layer] = total


def add_bonds(bonds, step, layer, far_layer, motion, shifts, weights, slot, total):
    for tile in sorted({bond[0] for bond in bonds}):
        rows = slice(8 * tile, 8 * tile + 8)
        own = [motion[axis, layer, rows] for axis in range(3)]
        near_x = own[0] - float(step)
        near_y = {step_y: own[1] - float(step_y) for step_y in range(-REACH, REACH + 1)}
        force = [total[axis, layer, rows] for axis in range(3)]
        for order, (bond_tile, step_y, step_z, plane, _) in enumerate(bonds):
            if bond_tile != tile:
                continue
            far_rows = slice(REACH + step_y + 8 * tile, REACH + step_y + 8 * tile + 8)
            far = [shifts[step_z + REACH, axis, far_layer, far_rows] for axis in range(3)]
            radial = [far[0] - near_x, far[1] - near_y[step_y], far[2] - own[2]]
            square = radial[0] * radial[0] + radial[1] * radial[1] + radial[2] * radial[2]
            rest = math.sqrt(sum(part * part for part in OFFSETS[plane]))
            factor = weights[slot + order] * (1.0 / rest - lax.rsqrt(square))
            force = [force[axis] + factor * radial[axis] for axis in range(3)]
        for axis in range(3):
            total[axis, layer, rows] = force[axis]


def add_inner(extent, late, motion, shifts, weights, total):
    for step, first, last, bonds, base in inner_plan(extent, late)[0]:
        if not bonds:
            continue

        def one_layer(layer, carry, step=step, first=first, bonds=bonds, base=base):
            slot = base + (layer - first) * len(bonds)
            add_bonds(bonds, step, layer, layer + step, motion, shifts, weights, slot, total)
            return carry

        lax.fori_loop(first, last, one_layer, 0)


def force_early_kernel(extent, edges, motion, z_low, z_high, weights, total, shifts):
    size_x, size_y, _ = extent
    total[...] = jnp.zeros(total.shape, jnp.float32)
    low_pack = kept(edges[0], z_low[0:size_y])
    high_pack = kept(edges[1], z_high[0:size_y])
    for layer in range(size_x):
        for axis in range(3):
            for order, value in each_shift(
                motion[axis, layer], low_pack, high_pack, layer * SLOT + axis * REACH, axis == 2
            ):
                shifts[order, axis, layer, REACH : REACH + size_y] = value
    add_inner(extent, False, motion, shifts, weights, total)


def force_late_kernel(
    extent, count, edges, motion, early, early_shifts, y_low, y_high, weights, total, shifts, halo
):
    size_x, size_y, _ = extent
    total[...] = early[...]
    shifts[...] = early_shifts[...]
    pack_at = count * size_x * REACH
    for order in range(2):
        at = pack_at + order * REACH
        halo[order, 0:REACH] = kept(edges[2], y_low[at : at + REACH])
        halo[order, REACH : 2 * REACH] = kept(edges[3], y_high[at : at + REACH])
        halo[order, 2 * REACH : 8] = jnp.zeros((8 - 2 * REACH, LANES), jnp.float32)
    low_pack, high_pack = halo[0], halo[1]
    for axis in range(3):
        for layer in range(size_x):
            at = (axis * size_x + layer) * REACH
            place = 2 + axis * size_x + layer
            halo[place, 0:REACH] = kept(edges[2], y_low[at : at + REACH])
            halo[place, REACH : 2 * REACH] = kept(edges[3], y_high[at : at + REACH])
            halo[place, 2 * REACH : 8] = jnp.zeros((8 - 2 * REACH, LANES), jnp.float32)
            for order, value in each_shift(
                halo[place], low_pack, high_pack, layer * SLOT + axis * REACH, axis == 2
            ):
                shifts[order, axis, layer, 0:REACH] = value[0:REACH]
                shifts[order, axis, layer, REACH + size_y : 2 * REACH + size_y] = value[
                    REACH : 2 * REACH
                ]
    add_inner(extent, True, motion, shifts, weights, total)


def finish_kernel(
    extent, count, height, stage, edges, motion, speed, pressing, inner, weights, x_low, x_high, *refs
):
    size_x, size_y, _ = extent
    if stage == "last":
        motion_out, speed_out, accel_out, total, shifts = refs
    else:
        motion_out, speed_out, z_up, z_down, total, shifts = refs
    total[...] = inner[...] + pressing[...]
    pack_at = count * REACH * height
    for side, source in enumerate((x_low, x_high)):
        packs = [
            kept(edges[4 + side], source[pack_at + order * height : pack_at + (order + 1) * height])
            for order in range(2)
        ]
        for layer in range(REACH):
            from_layer = size_x - REACH + layer if side == 0 else layer
            distance = REACH - layer if side == 0 else layer + 1
            for axis in range(3):
                at = (axis * REACH + layer) * height
                for order, value in each_shift(
                    kept(edges[4 + side], source[at : at + height]), *packs,
                    from_layer * SLOT + axis * REACH, axis == 2, reach_z(distance),
                ):
                    shifts[order, axis, side * REACH + layer] = value
    for step, first, last, bonds, base in outer_plan(extent)[0]:

        def one_layer(layer, carry, step=step, first=first, bonds=bonds, base=base):
            slot = base + (layer - first) * len(bonds)
            far_layer = layer + step + (REACH if step < 0 else REACH - size_x)
            add_bonds(bonds, step, layer, far_layer, motion, shifts, weights, slot, total)
            return carry

        lax.fori_loop(first, last, one_layer, 0)
    accel = total[...]
    new_speed = speed[...] + HALF_DT * accel
    if stage == "last":
        motion_out[...] = motion[...]
        speed_out[...] = new_speed
        accel_out[...] = accel
        return
    if stage == "middle":
        new_speed = new_speed + HALF_DT * accel
    speed_out[...] = new_speed
    motion_out[...] = motion[...] + DT_STEP * new_speed
    up, down = pack_columns(lambda axis, layer: motion_out[axis, layer], 3, size_x, size_y)
    z_up[...] = up
    z_down[...] = down


VMEM = pl.BlockSpec(memory_space=pltpu.VMEM)
SMEM = pl.BlockSpec(memory_space=pltpu.SMEM)


def call(kernel, scalars, operands, shapes, scratch=(), name=None, results=(), far=()):
    operands = [pltpu.with_memory_space_constraint(operand, pltpu.HBM) for operand in far] + [
        pltpu.with_memory_space_constraint(operand, pltpu.VMEM) for operand in operands
    ]
    return pl.pallas_call(
        kernel,
        out_shape=[
            jax.ShapeDtypeStruct(shape, jnp.float32)
            if place in results
            else pltpu.VMEM(shape, jnp.float32)
            for place, shape in enumerate(shapes)
        ],
        in_specs=[SMEM] * len(scalars)
        + [pl.BlockSpec(memory_space=pltpu.HBM)] * len(far)
        + [VMEM] * (len(operands) - len(far)),
        out_specs=[VMEM] * len(shapes),
        scratch_shapes=[
            pltpu.VMEM(item, jnp.float32) if isinstance(item, tuple) else item for item in scratch
        ],
        compiler_params=pltpu.CompilerParams(vmem_limit_bytes=24 * 1024 * 1024),
        name=name,
    )(*scalars, *operands)


def sent(value, axis, distance):
    count = lax.axis_size(axis)
    return lax.ppermute(value, axis, [(i, (i + distance) % count) for i in range(count)])


def on_device(displacement, velocity, stiffness, broken, borehole_id, flags, pressure):
    extent = stiffness.shape
    size_x, size_y, _ = extent
    height = size_y + 8
    edges = jnp.stack(
        [
            end
            for axis in ("gz", "gy", "gx")
            for end in (
                (lax.axis_index(axis) > 0).astype(jnp.int32),
                (lax.axis_index(axis) < lax.axis_size(axis) - 1).astype(jnp.int32),
            )
        ]
    )
    field = (size_x, size_y, LANES)
    vector = (3,) + field
    part = functools.partial

    pack = (size_y + size_x * size_y + PAD, LANES)
    rows_shapes = [(count * size_x + 2 * PAD, LANES) for count in (Y_UP_COUNT, Y_DOWN_COUNT)]
    layers_shape = (X_UP_COUNT * size_y, LANES)
    motion, stiffness, pore, z_up, z_down, rows_up, rows_down, x_up = pl.pallas_call(
        part(start_kernel, extent),
        out_shape=[
            pltpu.VMEM(shape, kind)
            for shape, kind in (
                (vector, jnp.float32), (field, jnp.float32),
                (field, jnp.float32), (pack, jnp.float32), (pack, jnp.float32),
                (rows_shapes[0], jnp.float32), (rows_shapes[1], jnp.float32),
                (layers_shape, jnp.float32),
            )
        ],
        in_specs=[pl.BlockSpec(memory_space=pltpu.HBM)] * 6,
        out_specs=[VMEM] * 8,
        scratch_shapes=[
            pltpu.VMEM(broken.shape, jnp.int32),
            pltpu.SMEM(pressure.shape, jnp.float32),
            pltpu.VMEM(field, jnp.int32),
            pltpu.VMEM(field, jnp.int32),
            pltpu.SemaphoreType.DMA((5,)),
            pltpu.SemaphoreType.DMA((size_x,)),
        ],
        compiler_params=pltpu.CompilerParams(vmem_limit_bytes=24 * 1024 * 1024),
        name="start",
    )(
        *(
            pltpu.with_memory_space_constraint(operand, pltpu.HBM)
            for operand in (pressure, displacement, stiffness, borehole_id, flags, broken)
        )
    )
    z_low = sent(z_up, "gz", 1)
    z_high = sent(z_down, "gz", -1)
    rows_low = sent(rows_up, "gy", 1)
    rows_high = sent(rows_down, "gy", -1)
    x_broken = sent(x_up, "gx", 1)
    rows = (round_up(5 * size_x * REACH + 2 * REACH + 2 * size_x * REACH), LANES)
    y_up, y_down = call(
        part(y_rows_first_kernel, extent), [edges],
        [motion, stiffness, pore, z_low, z_high], [rows, rows], name="y_rows_first",
    )
    y_low = sent(y_up, "gy", 1)
    y_high = sent(y_down, "gy", -1)
    moves = 2 * REACH + 1
    early_slots = inner_plan(extent, False)[1]
    late_slots = inner_plan(extent, True)[1]
    outer_slots = outer_plan(extent)[1]
    weights_early, keeps = call(
        part(weights_early_kernel, extent), [edges], [stiffness, z_low, z_high],
        [(early_slots, 8, LANES), (late_slots, 8, LANES)],
        [
            (moves, size_x, height, LANES),
            (len(OFFSETS), size_x, height, LANES),
            pltpu.VMEM(broken.shape, jnp.int32),
            pltpu.SemaphoreType.DMA((size_x,)),
        ], name="weights_early", far=[broken],
    )

    def force_early(motion, z_low, z_high):
        return call(
            part(force_early_kernel, extent), [edges], [motion, z_low, z_high, weights_early],
            [vector, (moves, 3, size_x, height, LANES)], name="force_early",
        )

    def force_late(count, motion, early, early_shifts, y_low, y_high):
        return call(
            part(force_late_kernel, extent, count), [edges],
            [motion, early, early_shifts, y_low, y_high, weights_late], [vector],
            [(moves, 3, size_x, height, LANES), (2 + 3 * size_x, 8, LANES)], name="force_late",
        )[0]

    early, early_shifts = force_early(motion, z_low, z_high)
    y_low, y_high, x_broken, early = lax.optimization_barrier((y_low, y_high, x_broken, early))
    layers = (4 * REACH + 3) * height
    wide_static, wide_pack, wide_broken, x_fields_up, x_fields_down = call(
        part(x_layers_first_kernel, extent), [edges],
        [motion, stiffness, pore, z_low, z_high, y_low, y_high, rows_low, rows_high],
        [
            (2, size_x, height, LANES),
            (2, height, LANES),
            (2, size_x, height, LANES),
            (round_up(layers + 2 * NEAR * height + XY_UP_COUNT), LANES),
            (layers, LANES),
        ], [(3, size_x, height, LANES)], name="x_layers_first",
    )
    x_low = sent(x_fields_up, "gx", 1)
    x_high = sent(x_fields_down, "gx", -1)
    (weights_late,) = call(
        part(weights_late_kernel, extent), [],
        [stiffness, wide_static, wide_pack, wide_broken, rows_low, rows_high, keeps],
        [(late_slots, 8, LANES)], [(moves, size_x, height, LANES)], name="weights_late",
    )
    inner = force_late(5, motion, early, early_shifts, y_low, y_high)
    outer_weights, pressing = call(
        part(weights_outer_kernel, extent), [edges],
        [stiffness, pore, wide_static, wide_pack, x_up, x_broken, x_low, x_high],
        [(outer_slots, 8, LANES), vector],
        [(moves, 2 * REACH, height, LANES), (X_UP_COUNT, height, LANES)],
        name="weights_outer",
    )

    def finish(stage, count, motion, speed, inner, x_low, x_high):
        columns = (size_y, LANES)
        shapes = [vector] * 3 if stage == "last" else [vector, vector, columns, columns]
        return call(
            part(finish_kernel, extent, count, height, stage), [edges],
            [motion, speed, pressing, inner, outer_weights, x_low, x_high],
            shapes, [vector, (moves, 3, 2 * REACH, height, LANES)], name="finish_" + stage,
            results=(0, 1, 2) if stage == "last" else (),
        )

    motion, speed, z_up, z_down = finish(
        "first", 4, motion, velocity, inner, x_low, x_high
    )
    for step_index in range(STEPS):
        z_low = sent(z_up, "gz", 1)
        z_high = sent(z_down, "gz", -1)
        rows = (round_up(3 * size_x * REACH + 2 * REACH), LANES)
        y_up, y_down = call(
            part(y_rows_kernel, extent), [edges], [motion, z_low, z_high], [rows, rows],
            name="y_rows",
        )
        y_low = sent(y_up, "gy", 1)
        y_high = sent(y_down, "gy", -1)
        early, early_shifts = force_early(motion, z_low, z_high)
        y_low, y_high, early = lax.optimization_barrier((y_low, y_high, early))
        layers = (3 * REACH + 2) * height
        x_up, x_down = call(
            part(x_layers_kernel, extent), [edges],
            [motion, z_low, z_high, y_low, y_high],
            [(layers, LANES), (layers, LANES)],
            [(3, size_x, height, LANES), (2, height, LANES)], name="x_layers",
        )
        x_low = sent(x_up, "gx", 1)
        x_high = sent(x_down, "gx", -1)
        inner = force_late(3, motion, early, early_shifts, y_low, y_high)
        if step_index < STEPS - 1:
            motion, speed, z_up, z_down = finish("middle", 3, motion, speed, inner, x_low, x_high)
        else:
            motion, speed, accel = finish("last", 3, motion, speed, inner, x_low, x_high)
    return (motion, speed, accel)


def solution(mesh):
    in_specs = (
        P(None, "gx", "gy", "gz"),
        P(None, "gx", "gy", "gz"),
        P("gx", "gy", "gz"),
        P(None, "gx", "gy", "gz"),
        P("gx", "gy", "gz"),
        P("gx", "gy", "gz"),
        P(),
    )
    out_specs = (P(None, "gx", "gy", "gz"), P(None, "gx", "gy", "gz"), P(None, "gx", "gy", "gz"))
    return jax.shard_map(
        on_device, mesh=mesh, in_specs=in_specs, out_specs=out_specs, check_vma=False
    )
```

```python
import functools
import math

import jax
import jax.numpy as jnp
from jax import lax
from jax.experimental import pallas as pl
from jax.experimental.pallas import tpu as pltpu
from jax.sharding import PartitionSpec as P

STEPS = 2
C_BOND = 3.0
DT_STEP = 0.04
REACH = 3
NEAR = 2
LANES = 128
SLOT = 16
PAD = 8
FIRST = 8
HALF_DT = 0.5 * DT_STEP


def half_offsets():
    result = []
    for step_x in range(0, 4):
        for step_y in range(-3, 4):
            for step_z in range(-3, 4):
                square = step_x * step_x + step_y * step_y + step_z * step_z
                if square == 0 or square > 9:
                    continue
                if step_x > 0 or (step_x == 0 and (step_y > 0 or (step_y == 0 and step_z > 0))):
                    result.append((step_x, step_y, step_z))
    return result


OFFSETS = half_offsets()
BONDS = {step: [] for step in range(-REACH, REACH + 1)}
for _plane, (_a, _b, _c) in enumerate(OFFSETS):
    BONDS[_a].append((_b, _c, _plane, True))
    BONDS[-_a].append((-_b, -_c, _plane, False))


def inner_layers(step, extent):
    return max(0, -step), min(extent, extent - step)


def outer_layers(step, extent):
    return (extent - step, extent) if step > 0 else (0, -step)


STEPS_ALL = list(range(-REACH, REACH + 1))
STEPS_OUT = [step for step in STEPS_ALL if step != 0]


def tiled_bonds(step, tiles):
    early, late = [], []
    for tile in range(tiles):
        for bond in BONDS[step]:
            low, high = 8 * tile + bond[0], 8 * tile + 8 + bond[0]
            (early if low >= 0 and high <= 8 * tiles else late).append((tile, *bond))
    return early, late


def inner_plan(extent, late):
    plan, total = [], 0
    for step in STEPS_ALL:
        bonds = tiled_bonds(step, extent[1] // 8)[int(late)]
        first, last = inner_layers(step, extent[0])
        plan.append((step, first, last, bonds, total))
        total += (last - first) * len(bonds)
    return plan, total


def outer_plan(extent):
    plan, total = [], 0
    for step in STEPS_OUT:
        bonds = [(tile, *bond) for tile in range(extent[1] // 8) for bond in BONDS[step]]
        first, last = outer_layers(step, extent[0])
        plan.append((step, first, last, bonds, total))
        total += (last - first) * len(bonds)
    return plan, total


def reach_beside(distance):
    return max(max(abs(b), abs(c)) for a, b, c in OFFSETS if a >= distance)


def x_span(distance, size_y):
    return REACH - reach_beside(distance), REACH + size_y + reach_beside(distance)


def x_place(field, distance, size_y):
    lengths = [high - low for low, high in (x_span(far, size_y) for far in (3, 2, 1))]
    return field * sum(lengths) + sum(lengths[: REACH - distance])


def round_up(count):
    return (count + 7) // 8 * 8


def running(amounts):
    places, total = {}, 0
    for plane, amount in amounts:
        places[plane] = total
        total += amount
    return places, total


Z_UP, Z_UP_COUNT = running([(k, c) for k, (a, b, c) in enumerate(OFFSETS) if c > 0])
Z_DOWN, Z_DOWN_COUNT = running([(k, -c) for k, (a, b, c) in enumerate(OFFSETS) if c < 0])
Y_UP, Y_UP_COUNT = running([(k, b) for k, (a, b, c) in enumerate(OFFSETS) if b > 0])
Y_DOWN, Y_DOWN_COUNT = running([(k, -b) for k, (a, b, c) in enumerate(OFFSETS) if b < 0])
X_UP, X_UP_COUNT = running([(k, a) for k, (a, b, c) in enumerate(OFFSETS) if a > 0])
XY_UP, XY_UP_COUNT = running([(k, a * abs(b)) for k, (a, b, c) in enumerate(OFFSETS) if a * abs(b) > 0])


def lanes_like(value):
    return lax.broadcasted_iota(jnp.int32, value.shape, value.ndim - 1)


def rolled(value, shift):
    shift = shift % LANES
    return value if shift == 0 else pltpu.roll(value, shift, value.ndim - 1)


def beside_columns(low_pack, high_pack, lane_of, high_lanes=0):
    lanes = lanes_like(low_pack)
    return jnp.where(
        lanes < REACH,
        rolled(high_pack, -lane_of - high_lanes),
        rolled(low_pack, LANES - REACH - lane_of),
    )


def moved(main, beside, step):
    if step == 0:
        return main
    lanes = lanes_like(main)
    if step > 0:
        return rolled(jnp.where(lanes < step, beside, main), -step)
    return rolled(jnp.where(lanes >= LANES + step, beside, main), -step)


def pack_columns(field_of, count, extent, height):
    lanes = lax.broadcasted_iota(jnp.int32, (height, LANES), 1)
    up = jnp.zeros((height, LANES), jnp.float32)
    down = up
    for layer in range(extent):
        for field in range(count):
            lane_of = layer * SLOT + field * REACH
            value = field_of(field, layer)
            here = (lanes >= lane_of) & (lanes < lane_of + REACH)
            up = jnp.where(here, rolled(value, lane_of - (LANES - REACH)), up)
            down = jnp.where(here, rolled(value, lane_of), down)
    return up, down


def kept(flag, value):
    return jnp.where(flag > 0, value, 0.0)


def start_kernel(
    extent, pressure_in, motion_in, stiffness_in, borehole_in, flags_in, broken_in,
    motion, stiffness, pore, z_up, z_down, rows_up, rows_down, x_up,
    broken, pressure, borehole, flags, field_sems, layer_sems,
):
    size_x, size_y, _ = extent
    pairs = (
        (pressure_in, pressure), (borehole_in, borehole), (flags_in, flags),
        (motion_in, motion), (stiffness_in, stiffness),
    )
    copies = [
        pltpu.make_async_copy(source, target, field_sems.at[place])
        for place, (source, target) in enumerate(pairs)
    ]

    def layer_copy(layer):
        return pltpu.make_async_copy(
            broken_in.at[:, layer], broken.at[:, layer], layer_sems.at[layer]
        )

    for copy in copies:
        copy.start()
    for layer in range(size_x):
        layer_copy(layer).start()
    for copy in copies:
        copy.wait()
    ids = borehole[...]
    level = jnp.zeros(ids.shape, jnp.float32)
    for label in range(pressure.shape[0]):
        level = jnp.where(ids == label, pressure[label], level)
    pore[...] = flags[...].astype(jnp.float32) * level

    def field_of(field, layer):
        if field < 3:
            return motion[field, layer]
        return stiffness[layer] if field == 3 else pore[layer]

    up, down = pack_columns(field_of, 5, size_x, size_y)
    z_up[0:size_y] = up
    z_down[0:size_y] = down

    def one_layer(layer, carry):
        layer_copy(layer).wait()
        lanes = lax.broadcasted_iota(jnp.int32, (size_y, LANES), 1)
        rows = pl.ds(size_y + layer * size_y, size_y)
        up = jnp.zeros((size_y, LANES), jnp.float32)
        down = up
        for plane, (_, _, c) in enumerate(OFFSETS):
            if c > 0:
                at = Z_UP[plane]
                value = broken[plane, layer].astype(jnp.float32)
                up = jnp.where((lanes >= at) & (lanes < at + c), rolled(value, at + c), up)
            if c < 0:
                at = Z_DOWN[plane]
                value = broken[plane, layer].astype(jnp.float32)
                down = jnp.where((lanes >= at) & (lanes < at - c), rolled(value, at), down)
        z_up[rows] = up
        z_down[rows] = down
        return carry

    lax.fori_loop(0, size_x, one_layer, 0)
    for plane, (a, _, _) in enumerate(OFFSETS):
        for layer in range(a):
            at = (X_UP[plane] + layer) * size_y
            x_up[at : at + size_y] = broken[plane, size_x - a + layer].astype(jnp.float32)
    for plane, (_, b, _) in enumerate(OFFSETS):
        for layer in range(size_x):
            if b > 0:
                at = PAD + Y_UP[plane] * size_x + layer * b
                rows_up[at : at + b] = broken[plane, layer, size_y - b : size_y].astype(jnp.float32)
            if b < 0:
                at = PAD + Y_DOWN[plane] * size_x - layer * b
                rows_down[at : at - b] = broken[plane, layer, 0:-b].astype(jnp.float32)


def copy_y_rows(field_of, count, extent, low_pack, high_pack, y_up, y_down):
    size_x, size_y, _ = extent
    for field in range(count):
        for layer in range(size_x):
            at = (field * size_x + layer) * REACH
            y_up[at : at + REACH] = field_of(field, layer, slice(size_y - REACH, size_y))
            y_down[at : at + REACH] = field_of(field, layer, slice(0, REACH))
    at = count * size_x * REACH
    for pack in (low_pack, high_pack):
        y_up[at : at + REACH] = pack[size_y - REACH : size_y]
        y_down[at : at + REACH] = pack[0:REACH]
        at += REACH
    return at


def y_rows_kernel(extent, edges, motion, z_low, z_high, y_up, y_down):
    size_y = extent[1]
    low_pack = kept(edges[0], z_low[0:size_y])
    high_pack = kept(edges[1], z_high[0:size_y])
    copy_y_rows(
        lambda field, layer, rows: motion[field, layer, rows],
        3, extent, low_pack, high_pack, y_up, y_down,
    )


def y_rows_first_kernel(extent, edges, motion, stiffness, pore, z_low, z_high, y_up, y_down):
    size_x, size_y, _ = extent
    low_pack = kept(edges[0], z_low[0:size_y])
    high_pack = kept(edges[1], z_high[0:size_y])

    def field_of(field, layer, rows):
        if field < 3:
            return motion[field, layer, rows]
        return stiffness[layer, rows] if field == 3 else pore[layer, rows]

    base = copy_y_rows(field_of, 5, extent, low_pack, high_pack, y_up, y_down)
    for order, pack in enumerate((z_low, z_high)):
        for layer in range(size_x):
            first = size_y + layer * size_y
            at = base + (order * size_x + layer) * REACH
            y_up[at : at + REACH] = pack[first + size_y - REACH : first + size_y]
            y_down[at : at + REACH] = pack[first : first + REACH]


def widen(target, low_rows, middle, high_rows):
    size_y = middle.shape[0]
    target[0:REACH] = low_rows
    target[REACH : REACH + size_y] = middle
    target[REACH + size_y : 2 * REACH + size_y] = high_rows
    height = target.shape[0]
    target[2 * REACH + size_y : height] = jnp.zeros((height - 2 * REACH - size_y, LANES), jnp.float32)


def widen_fields(edges, field_of, count, extent, z_low, z_high, y_low, y_high, target, wide_pack):
    size_x, size_y, _ = extent
    for field in range(count):
        for layer in range(size_x):
            at = (field * size_x + layer) * REACH
            widen(
                target(field).at[layer],
                kept(edges[2], y_low[at : at + REACH]),
                field_of(field, layer),
                kept(edges[3], y_high[at : at + REACH]),
            )
    at = count * size_x * REACH
    for order, pack in enumerate((z_low, z_high)):
        widen(
            wide_pack.at[order],
            kept(edges[2], y_low[at : at + REACH]),
            kept(edges[order], pack[0:size_y]),
            kept(edges[3], y_high[at : at + REACH]),
        )
        at += REACH
    return at


def copy_x_layers(count, extent, target, wide_pack, x_up, x_down):
    size_x, size_y, _ = extent
    height = wide_pack.shape[1]
    for field in range(count):
        for distance in (3, 2, 1):
            low, high = x_span(distance, size_y)
            at = x_place(field, distance, size_y)
            x_up[at : at + high - low] = target(field)[size_x - distance, low:high]
            x_down[at : at + high - low] = target(field)[distance - 1, low:high]
    at = x_place(count, REACH, size_y)
    low_pack, high_pack = wide_pack[0], wide_pack[1]
    half = lanes_like(low_pack) < LANES // 2
    other = rolled(high_pack, LANES // 2)
    x_up[at : at + height] = jnp.where(half, other, low_pack)
    x_down[at : at + height] = jnp.where(half, low_pack, other)
    return at + height


def x_layers_kernel(
    extent, edges, motion, z_low, z_high, y_low, y_high, x_up, x_down, wide, wide_pack
):
    widen_fields(
        edges, lambda field, layer: motion[field, layer],
        3, extent, z_low, z_high, y_low, y_high, lambda field: wide.at[field], wide_pack,
    )
    copy_x_layers(3, extent, lambda field: wide.at[field], wide_pack, x_up, x_down)


def x_layers_first_kernel(
    extent, edges, motion, stiffness, pore, z_low, z_high, y_low, y_high, rows_low, rows_high,
    wide_static, wide_pack, wide_broken, x_up, x_down, wide,
):
    size_x, size_y, _ = extent

    def field_of(field, layer):
        if field < 3:
            return motion[field, layer]
        return stiffness[layer] if field == 3 else pore[layer]

    def target(field):
        return wide.at[field] if field < 3 else wide_static.at[field - 3]

    base = widen_fields(
        edges, field_of, 5, extent, z_low, z_high, y_low, y_high, target, wide_pack
    )
    for order, pack in enumerate((z_low, z_high)):
        for layer in range(size_x):
            first = size_y + layer * size_y
            at = base + (order * size_x + layer) * REACH
            widen(
                wide_broken.at[order, layer],
                y_low[at : at + REACH],
                pack[first : first + size_y],
                y_high[at : at + REACH],
            )
    at = copy_x_layers(4, extent, target, wide_pack, x_up, x_down)
    height = wide.shape[2]
    x_up[at : at + size_y] = pore[size_x - 1]
    x_down[at : at + size_y] = pore[0]
    at += size_y
    for order in range(2):
        for layer in range(NEAR):
            x_up[at : at + height] = wide_broken[order, size_x - NEAR + layer]
            at += height
    for plane, (a, b, _) in enumerate(OFFSETS):
        if a * b == 0:
            continue
        rows, many = abs(b), a * abs(b)
        source = rows_low if b > 0 else rows_high
        first = PAD + (Y_UP if b > 0 else Y_DOWN)[plane] * size_x + (size_x - a) * rows
        x_up[at + XY_UP[plane] : at + XY_UP[plane] + many] = source[first : first + many]


def each_shift(main, beside, add_step, reach=REACH):
    for step in range(-reach, reach + 1):
        value = moved(main, beside, step)
        yield step + REACH, value + float(step) if add_step and step else value


def wanted_keep(value, low, high, plane, step_z):
    if step_z == 0:
        return 1.0 - value
    lanes = lanes_like(value)
    if step_z < 0:
        beside = rolled(low(), -Z_UP[plane])
        value = jnp.where(lanes < -step_z, beside, rolled(value, -step_z))
    else:
        beside = rolled(high(), LANES - step_z - Z_DOWN[plane])
        value = jnp.where(lanes >= LANES - step_z, beside, rolled(value, -step_z))
    return 1.0 - value


def fill_outer(extent, count, edges, fields, x_low, x_high, shifts, besides):
    size_x, size_y, _ = extent
    height = shifts.shape[3]
    at = x_place(count, REACH, size_y)
    sides = ((x_low, size_x - REACH, -LANES // 2), (x_high, 0, LANES // 2))
    for side, (source, first, high_lanes) in enumerate(sides):
        pack = kept(edges[4 + side], source[at : at + height])
        for layer in range(REACH):
            for order, field in enumerate(fields):
                lane_of = (first + layer) * SLOT + field * REACH
                besides[order, side * REACH + layer] = beside_columns(
                    pack, pack, lane_of, high_lanes
                )
    for side, (source, _, _) in enumerate(sides):
        for layer in range(REACH):
            distance = REACH - layer if side == 0 else layer + 1
            low, high = x_span(distance, size_y)
            for order, field in enumerate(fields):
                start = x_place(field, distance, size_y)
                for step, value in each_shift(
                    kept(edges[4 + side], source[start : start + high - low]),
                    besides[order, side * REACH + layer, low:high],
                    field == 2, reach_beside(distance),
                ):
                    shifts[step, order, side * REACH + layer, low:high] = value


def weights_early_kernel(
    extent, edges, broken_in, stiffness, z_low, z_high, weights, keeps,
    shifts, planes, besides, broken, sems,
):
    size_x, size_y, _ = extent

    def layer_copy(layer):
        return pltpu.make_async_copy(broken_in.at[:, layer], broken.at[:, layer], sems.at[layer])

    for layer in range(size_x):
        layer_copy(layer).start()
    low_pack = kept(edges[0], z_low[0:size_y])
    high_pack = kept(edges[1], z_high[0:size_y])
    for layer in range(size_x):
        besides[layer] = beside_columns(low_pack, high_pack, layer * SLOT + 3 * REACH)
    for layer in range(size_x):
        for order, value in each_shift(stiffness[layer], besides[layer], False):
            shifts[order, layer, FIRST : FIRST + size_y] = value

    def fill(layer, carry):
        layer_copy(layer).wait()
        for plane in range(len(OFFSETS)):
            planes[plane, layer, FIRST : FIRST + size_y] = broken[plane, layer].astype(jnp.float32)
        return carry

    lax.fori_loop(0, size_x, fill, 0)
    for late, target in ((False, weights), (True, keeps)):
        for step, first, last, bonds, base in inner_plan(extent, late)[0]:

            def one_layer(layer, carry, step=step, first=first, bonds=bonds, base=base):
                slot = base + (layer - first) * len(bonds)
                far_layer = layer + step
                for order, (tile, step_y, step_z, plane, owner) in enumerate(bonds):
                    rows = slice(8 * tile, 8 * tile + 8)
                    far_rows = slice(FIRST + step_y + 8 * tile, FIRST + step_y + 8 * tile + 8)
                    if owner:
                        keep = 1.0 - broken[plane, layer, rows].astype(jnp.float32)
                    else:
                        at = size_y + far_layer * size_y + step_y + 8 * tile
                        keep = wanted_keep(
                            planes[plane, far_layer, far_rows],
                            lambda: z_low[pl.ds(at, 8)],
                            lambda: z_high[pl.ds(at, 8)],
                            plane, step_z,
                        )
                    keep = (0.5 * C_BOND) * keep
                    if not late:
                        far = shifts[step_z + REACH, far_layer, far_rows]
                        keep = jnp.where(far > 0.0, keep * (stiffness[layer, rows] + far), 0.0)
                    target[slot + order] = keep
                return carry

            lax.fori_loop(first, last, one_layer, 0)


def weights_late_kernel(
    extent, stiffness, wide, wide_pack, wide_broken, rows_low, rows_high, keeps, weights,
    shifts, besides,
):
    size_x, size_y, _ = extent
    for layer in range(size_x):
        besides[layer] = beside_columns(wide_pack[0], wide_pack[1], layer * SLOT + 3 * REACH)
    for layer in range(size_x):
        for order, value in each_shift(wide[0, layer], besides[layer], False):
            shifts[order, layer] = value
    for step, first, last, bonds, base in inner_plan(extent, True)[0]:

        def one_layer(layer, carry, step=step, first=first, bonds=bonds, base=base):
            slot = base + (layer - first) * len(bonds)
            far_layer = layer + step
            sublanes = lax.broadcasted_iota(jnp.int32, (8, LANES), 0)
            for order, (tile, step_y, step_z, plane, owner) in enumerate(bonds):
                rows = slice(8 * tile, 8 * tile + 8)
                far_rows = slice(REACH + step_y + 8 * tile, REACH + step_y + 8 * tile + 8)
                keep = keeps[slot + order]
                if not owner:
                    if step_y < 0:
                        at = PAD + Y_UP[plane] * size_x - far_layer * step_y
                        value = rows_low[pl.ds(at, 8)]
                        across = sublanes < -step_y
                    else:
                        at = PAD + Y_DOWN[plane] * size_x + far_layer * step_y + step_y - 8
                        value = rows_high[pl.ds(at, 8)]
                        across = sublanes >= 8 - step_y
                    halo = wanted_keep(
                        value,
                        lambda: wide_broken[0, far_layer, far_rows],
                        lambda: wide_broken[1, far_layer, far_rows],
                        plane, step_z,
                    )
                    keep = jnp.where(across, (0.5 * C_BOND) * halo, keep)
                far = shifts[step_z + REACH, far_layer, far_rows]
                weights[slot + order] = jnp.where(
                    far > 0.0, keep * (stiffness[layer, rows] + far), 0.0
                )
            return carry

        lax.fori_loop(first, last, one_layer, 0)


def weights_outer_kernel(
    extent, edges, stiffness, pore, wide, wide_pack, x_up, x_broken, x_low, x_high,
    weights, pressing, shifts, planes, besides,
):
    size_x, size_y, _ = extent
    height = wide.shape[2]
    pore_at = x_place(4, REACH, size_y) + height
    broken_at = pore_at + size_y
    rows_at = broken_at + 2 * NEAR * height
    fill_outer(extent, 4, edges, (3,), x_low, x_high, shifts, besides)
    for plane, (a, b, _) in enumerate(OFFSETS):
        for layer in range(a):
            at = (X_UP[plane] + layer) * size_y
            place = X_UP[plane] + layer
            planes[place, REACH : REACH + size_y] = x_broken[at : at + size_y]
            at = rows_at + XY_UP.get(plane, 0) + layer * abs(b)
            if b > 0:
                planes[place, REACH - b : REACH] = x_low[at : at + b]
            if b < 0:
                planes[place, REACH + size_y : REACH + size_y - b] = x_low[at : at - b]
    for step, first, last, bonds, base in outer_plan(extent)[0]:
        for layer in range(first, last):
            slot = base + (layer - first) * len(bonds)
            far_layer = layer + step
            far_layer = far_layer + REACH if far_layer < 0 else far_layer - size_x + REACH
            for order, (tile, step_y, step_z, plane, owner) in enumerate(bonds):
                rows = slice(8 * tile, 8 * tile + 8)
                far_rows = slice(REACH + step_y + 8 * tile, REACH + step_y + 8 * tile + 8)
                far = shifts[step_z + REACH, 0, far_layer, far_rows]
                if owner:
                    at = (X_UP[plane] + layer - first) * size_y + 8 * tile
                    keep = 1.0 - x_up[at : at + 8]
                else:
                    low_at = broken_at + (far_layer + NEAR - REACH) * height
                    high_at = low_at + NEAR * height
                    keep = wanted_keep(
                        planes[X_UP[plane] + layer, far_rows],
                        lambda: x_low[far_rows.start + low_at : far_rows.stop + low_at],
                        lambda: x_low[far_rows.start + high_at : far_rows.stop + high_at],
                        plane, step_z,
                    )
                value = keep * (0.5 * C_BOND) * (stiffness[layer, rows] + far)
                weights[slot + order] = jnp.where(far > 0.0, value, 0.0)

    middle = slice(REACH, REACH + size_y)

    def wide_field(field, layer):
        if layer < 0 or layer >= size_x:
            source = x_low if layer < 0 else x_high
            at = x_place(field, 1, size_y) + reach_beside(1) if field == 3 else pore_at
            return kept(edges[4 if layer < 0 else 5], source[at : at + size_y])
        return wide[field - 3, layer, middle]

    for layer in range(size_x):
        own = pore[layer]
        for axis in range(3):
            total = jnp.zeros((size_y, LANES), jnp.float32)
            for sign in (1, -1):
                if axis == 0:
                    inside = wide_field(3, layer + sign)
                    level = wide_field(4, layer + sign)
                elif axis == 1:
                    rows = slice(REACH + sign, REACH + sign + size_y)
                    inside = wide[0, layer, rows]
                    level = wide[1, layer, rows]
                else:
                    inside, level = (
                        moved(
                            wide[field - 3, layer],
                            beside_columns(
                                wide_pack[0], wide_pack[1], layer * SLOT + field * REACH
                            ),
                            sign,
                        )[middle]
                        for field in (3, 4)
                    )
                total = total + jnp.where(inside > 0.0, (-0.5 * sign) * (level - own), 0.0)
            pressing[axis, layer] = total


def add_bonds(bonds, step, layer, far_layer, first_row, motion, shifts, weights, slot, total):
    for tile in sorted({bond[0] for bond in bonds}):
        rows = slice(8 * tile, 8 * tile + 8)
        own = [motion[axis, layer, rows] for axis in range(3)]
        near_x = own[0] - float(step)
        near_y = {step_y: own[1] - float(step_y) for step_y in range(-REACH, REACH + 1)}
        force = [total[axis, layer, rows] for axis in range(3)]
        for order, (bond_tile, step_y, step_z, plane, _) in enumerate(bonds):
            if bond_tile != tile:
                continue
            far_rows = slice(first_row + step_y + 8 * tile, first_row + step_y + 8 * tile + 8)
            far = [shifts[step_z + REACH, axis, far_layer, far_rows] for axis in range(3)]
            radial = [far[0] - near_x, far[1] - near_y[step_y], far[2] - own[2]]
            square = radial[0] * radial[0] + radial[1] * radial[1] + radial[2] * radial[2]
            rest = math.sqrt(sum(part * part for part in OFFSETS[plane]))
            factor = weights[slot + order] * (1.0 / rest - lax.rsqrt(square))
            force = [force[axis] + factor * radial[axis] for axis in range(3)]
        for axis in range(3):
            total[axis, layer, rows] = force[axis]


def add_inner(extent, late, fill, motion, shifts, weights, total):
    plan = [entry for entry in inner_plan(extent, late)[0] if entry[3]]
    for layer in range(extent[0]):
        fill(layer)
        for step, first, last, bonds, base in plan:
            own = layer if step <= 0 else layer - step
            if own < first or own >= last:
                continue
            slot = base + (own - first) * len(bonds)
            add_bonds(bonds, step, own, own + step, FIRST, motion, shifts, weights, slot, total)


def force_early_kernel(extent, edges, motion, z_low, z_high, weights, total, shifts, besides):
    size_x, size_y, _ = extent
    total[...] = jnp.zeros(total.shape, jnp.float32)
    low_pack = kept(edges[0], z_low[0:size_y])
    high_pack = kept(edges[1], z_high[0:size_y])
    for layer in range(size_x):
        for axis in range(3):
            besides[axis, layer] = beside_columns(
                low_pack, high_pack, layer * SLOT + axis * REACH
            )

    def fill(layer):
        for axis in range(3):
            for order, value in each_shift(motion[axis, layer], besides[axis, layer], axis == 2):
                shifts[order, axis, layer, FIRST : FIRST + size_y] = value

    add_inner(extent, False, fill, motion, shifts, weights, total)


def force_late_kernel(
    extent, count, edges, motion, early, early_shifts, y_low, y_high, weights,
    total, shifts, halo, besides,
):
    size_x, size_y, _ = extent
    total[...] = early[...]
    middle = slice(FIRST, FIRST + size_y)
    above = FIRST + size_y

    def across(place, at):
        halo[place, 0:REACH] = kept(edges[3], y_high[at : at + REACH])
        halo[place, REACH : 8 - REACH] = jnp.zeros((8 - 2 * REACH, LANES), jnp.float32)
        halo[place, 8 - REACH : 8] = kept(edges[2], y_low[at : at + REACH])

    packs = 3 * size_x
    for order in range(2):
        across(packs + order, (count * size_x + order) * REACH)
    for place in range(3 * size_x):
        across(place, place * REACH)
    low_pack, high_pack = halo[packs], halo[packs + 1]
    for layer in range(size_x):
        for axis in range(3):
            besides[axis * size_x + layer] = beside_columns(
                low_pack, high_pack, layer * SLOT + axis * REACH
            )

    def fill(layer):
        for axis in range(3):
            place = axis * size_x + layer
            for order, value in each_shift(halo[place], besides[place], axis == 2):
                shifts[order, axis, layer, middle] = early_shifts[order, axis, layer, middle]
                shifts[order, axis, layer, FIRST - REACH : FIRST] = value[8 - REACH : 8]
                shifts[order, axis, layer, above : above + REACH] = value[0:REACH]

    add_inner(extent, True, fill, motion, shifts, weights, total)


def finish_kernel(
    extent, count, stage, edges, motion, speed, pressing, inner, weights, x_low, x_high, *refs
):
    size_x, size_y, _ = extent
    if stage == "last":
        motion_out, speed_out, accel_out, total, shifts, besides = refs
    else:
        motion_out, speed_out, z_up, z_down, total, shifts, besides = refs
    total[...] = inner[...] + pressing[...]
    fill_outer(extent, count, edges, range(3), x_low, x_high, shifts, besides)
    for step, first, last, bonds, base in outer_plan(extent)[0]:
        for layer in range(first, last):
            slot = base + (layer - first) * len(bonds)
            far_layer = layer + step + (REACH if step < 0 else REACH - size_x)
            add_bonds(bonds, step, layer, far_layer, REACH, motion, shifts, weights, slot, total)
    accel = total[...]
    new_speed = speed[...] + HALF_DT * accel
    if stage == "last":
        motion_out[...] = motion[...]
        speed_out[...] = new_speed
        accel_out[...] = accel
        return
    if stage == "middle":
        new_speed = new_speed + HALF_DT * accel
    speed_out[...] = new_speed
    motion_out[...] = motion[...] + DT_STEP * new_speed
    up, down = pack_columns(lambda axis, layer: motion_out[axis, layer], 3, size_x, size_y)
    z_up[...] = up
    z_down[...] = down


VMEM = pl.BlockSpec(memory_space=pltpu.VMEM)
SMEM = pl.BlockSpec(memory_space=pltpu.SMEM)


def call(kernel, scalars, operands, shapes, scratch=(), name=None, results=(), far=()):
    operands = [pltpu.with_memory_space_constraint(operand, pltpu.HBM) for operand in far] + [
        pltpu.with_memory_space_constraint(operand, pltpu.VMEM) for operand in operands
    ]
    return pl.pallas_call(
        kernel,
        out_shape=[
            jax.ShapeDtypeStruct(shape, jnp.float32)
            if place in results
            else pltpu.VMEM(shape, jnp.float32)
            for place, shape in enumerate(shapes)
        ],
        in_specs=[SMEM] * len(scalars)
        + [pl.BlockSpec(memory_space=pltpu.HBM)] * len(far)
        + [VMEM] * (len(operands) - len(far)),
        out_specs=[VMEM] * len(shapes),
        scratch_shapes=[
            pltpu.VMEM(item, jnp.float32) if isinstance(item, tuple) else item for item in scratch
        ],
        compiler_params=pltpu.CompilerParams(vmem_limit_bytes=24 * 1024 * 1024),
        name=name,
    )(*scalars, *operands)


def sent(value, axis, distance):
    count = lax.axis_size(axis)
    return lax.ppermute(value, axis, [(i, (i + distance) % count) for i in range(count)])


def on_device(displacement, velocity, stiffness, broken, borehole_id, flags, pressure):
    extent = stiffness.shape
    size_x, size_y, _ = extent
    height = size_y + 8
    tall = size_y + 2 * FIRST
    edges = jnp.stack(
        [
            end
            for axis in ("gz", "gy", "gx")
            for end in (
                (lax.axis_index(axis) > 0).astype(jnp.int32),
                (lax.axis_index(axis) < lax.axis_size(axis) - 1).astype(jnp.int32),
            )
        ]
    )
    field = (size_x, size_y, LANES)
    vector = (3,) + field
    part = functools.partial

    pack = (size_y + size_x * size_y + PAD, LANES)
    rows_shapes = [(count * size_x + 2 * PAD, LANES) for count in (Y_UP_COUNT, Y_DOWN_COUNT)]
    layers_shape = (X_UP_COUNT * size_y, LANES)
    motion, stiffness, pore, z_up, z_down, rows_up, rows_down, x_up = pl.pallas_call(
        part(start_kernel, extent),
        out_shape=[
            pltpu.VMEM(shape, kind)
            for shape, kind in (
                (vector, jnp.float32), (field, jnp.float32),
                (field, jnp.float32), (pack, jnp.float32), (pack, jnp.float32),
                (rows_shapes[0], jnp.float32), (rows_shapes[1], jnp.float32),
                (layers_shape, jnp.float32),
            )
        ],
        in_specs=[pl.BlockSpec(memory_space=pltpu.HBM)] * 6,
        out_specs=[VMEM] * 8,
        scratch_shapes=[
            pltpu.VMEM(broken.shape, jnp.int32),
            pltpu.SMEM(pressure.shape, jnp.float32),
            pltpu.VMEM(field, jnp.int32),
            pltpu.VMEM(field, jnp.int32),
            pltpu.SemaphoreType.DMA((5,)),
            pltpu.SemaphoreType.DMA((size_x,)),
        ],
        compiler_params=pltpu.CompilerParams(vmem_limit_bytes=24 * 1024 * 1024),
        name="start",
    )(
        *(
            pltpu.with_memory_space_constraint(operand, pltpu.HBM)
            for operand in (pressure, displacement, stiffness, borehole_id, flags, broken)
        )
    )
    z_low = sent(z_up, "gz", 1)
    z_high = sent(z_down, "gz", -1)
    rows_low = sent(rows_up, "gy", 1)
    rows_high = sent(rows_down, "gy", -1)
    x_broken = sent(x_up, "gx", 1)
    rows = (round_up(5 * size_x * REACH + 2 * REACH + 2 * size_x * REACH), LANES)
    y_up, y_down = call(
        part(y_rows_first_kernel, extent), [edges],
        [motion, stiffness, pore, z_low, z_high], [rows, rows], name="y_rows_first",
    )
    y_low = sent(y_up, "gy", 1)
    y_high = sent(y_down, "gy", -1)
    moves = 2 * REACH + 1
    early_slots = inner_plan(extent, False)[1]
    late_slots = inner_plan(extent, True)[1]
    outer_slots = outer_plan(extent)[1]
    weights_early, keeps = call(
        part(weights_early_kernel, extent), [edges], [stiffness, z_low, z_high],
        [(early_slots, 8, LANES), (late_slots, 8, LANES)],
        [
            (moves, size_x, tall, LANES),
            (len(OFFSETS), size_x, tall, LANES),
            field,
            pltpu.VMEM(broken.shape, jnp.int32),
            pltpu.SemaphoreType.DMA((size_x,)),
        ], name="weights_early", far=[broken],
    )

    def force_early(motion, z_low, z_high):
        return call(
            part(force_early_kernel, extent), [edges], [motion, z_low, z_high, weights_early],
            [vector, (moves, 3, size_x, tall, LANES)], [vector], name="force_early",
        )

    def force_late(count, motion, early, early_shifts, y_low, y_high):
        return call(
            part(force_late_kernel, extent, count), [edges],
            [motion, early, early_shifts, y_low, y_high, weights_late], [vector],
            [(moves, 3, size_x, tall, LANES), (2 + 3 * size_x, 8, LANES), (3 * size_x, 8, LANES)], name="force_late",
        )[0]

    early, early_shifts = force_early(motion, z_low, z_high)
    y_low, y_high, x_broken, early = lax.optimization_barrier((y_low, y_high, x_broken, early))
    layers = x_place(4, REACH, size_y) + height + size_y
    wide_static, wide_pack, wide_broken, x_fields_up, x_fields_down = call(
        part(x_layers_first_kernel, extent), [edges],
        [motion, stiffness, pore, z_low, z_high, y_low, y_high, rows_low, rows_high],
        [
            (2, size_x, height, LANES),
            (2, height, LANES),
            (2, size_x, height, LANES),
            (round_up(layers + 2 * NEAR * height + XY_UP_COUNT), LANES),
            (round_up(layers), LANES),
        ], [(3, size_x, height, LANES)], name="x_layers_first",
    )
    x_low = sent(x_fields_up, "gx", 1)
    x_high = sent(x_fields_down, "gx", -1)
    (weights_late,) = call(
        part(weights_late_kernel, extent), [],
        [stiffness, wide_static, wide_pack, wide_broken, rows_low, rows_high, keeps],
        [(late_slots, 8, LANES)],
        [(moves, size_x, height, LANES), (size_x, height, LANES)], name="weights_late",
    )
    inner = force_late(5, motion, early, early_shifts, y_low, y_high)
    outer_weights, pressing = call(
        part(weights_outer_kernel, extent), [edges],
        [stiffness, pore, wide_static, wide_pack, x_up, x_broken, x_low, x_high],
        [(outer_slots, 8, LANES), vector],
        [
            (moves, 1, 2 * REACH, height, LANES),
            (X_UP_COUNT, height, LANES),
            (1, 2 * REACH, height, LANES),
        ], name="weights_outer",
    )

    def finish(stage, count, motion, speed, inner, x_low, x_high):
        columns = (size_y, LANES)
        shapes = [vector] * 3 if stage == "last" else [vector, vector, columns, columns]
        return call(
            part(finish_kernel, extent, count, stage), [edges],
            [motion, speed, pressing, inner, outer_weights, x_low, x_high],
            shapes,
            [
                vector,
                (moves, 3, 2 * REACH, height, LANES),
                (3, 2 * REACH, height, LANES),
            ], name="finish_" + stage,
            results=(0, 1, 2) if stage == "last" else (),
        )

    motion, speed, z_up, z_down = finish(
        "first", 4, motion, velocity, inner, x_low, x_high
    )
    for step_index in range(STEPS):
        z_low = sent(z_up, "gz", 1)
        z_high = sent(z_down, "gz", -1)
        rows = (round_up(3 * size_x * REACH + 2 * REACH), LANES)
        y_up, y_down = call(
            part(y_rows_kernel, extent), [edges], [motion, z_low, z_high], [rows, rows],
            name="y_rows",
        )
        y_low = sent(y_up, "gy", 1)
        y_high = sent(y_down, "gy", -1)
        early, early_shifts = force_early(motion, z_low, z_high)
        y_low, y_high, early = lax.optimization_barrier((y_low, y_high, early))
        layers = round_up(x_place(3, REACH, size_y) + height)
        x_up, x_down = call(
            part(x_layers_kernel, extent), [edges],
            [motion, z_low, z_high, y_low, y_high],
            [(layers, LANES), (layers, LANES)],
            [(3, size_x, height, LANES), (2, height, LANES)], name="x_layers",
        )
        x_low = sent(x_up, "gx", 1)
        x_high = sent(x_down, "gx", -1)
        inner = force_late(3, motion, early, early_shifts, y_low, y_high)
        if step_index < STEPS - 1:
            motion, speed, z_up, z_down = finish("middle", 3, motion, speed, inner, x_low, x_high)
        else:
            motion, speed, accel = finish("last", 3, motion, speed, inner, x_low, x_high)
    return (motion, speed, accel)


def solution(mesh):
    in_specs = (
        P(None, "gx", "gy", "gz"),
        P(None, "gx", "gy", "gz"),
        P("gx", "gy", "gz"),
        P(None, "gx", "gy", "gz"),
        P("gx", "gy", "gz"),
        P("gx", "gy", "gz"),
        P(),
    )
    out_specs = (P(None, "gx", "gy", "gz"), P(None, "gx", "gy", "gz"), P(None, "gx", "gy", "gz"))
    return jax.shard_map(
        on_device, mesh=mesh, in_specs=in_specs, out_specs=out_specs, check_vma=False
    )
```

```python
import functools
import math

import jax
import jax.numpy as jnp
from jax import lax
from jax.experimental import pallas as pl
from jax.experimental.pallas import tpu as pltpu
from jax.sharding import PartitionSpec as P

STEPS = 2
C_BOND = 3.0
DT_STEP = 0.04
REACH = 3
NEAR = 2
LANES = 128
SLOT = 16
PAD = 8
UNROLL = 2
UNROLL_FILL = 2
FIRST = 8
HALF_DT = 0.5 * DT_STEP


def half_offsets():
    result = []
    for step_x in range(0, 4):
        for step_y in range(-3, 4):
            for step_z in range(-3, 4):
                square = step_x * step_x + step_y * step_y + step_z * step_z
                if square == 0 or square > 9:
                    continue
                if step_x > 0 or (step_x == 0 and (step_y > 0 or (step_y == 0 and step_z > 0))):
                    result.append((step_x, step_y, step_z))
    return result


OFFSETS = half_offsets()
BONDS = {step: [] for step in range(-REACH, REACH + 1)}
for _plane, (_a, _b, _c) in enumerate(OFFSETS):
    BONDS[_a].append((_b, _c, _plane, True))
    BONDS[-_a].append((-_b, -_c, _plane, False))


def inner_layers(step, extent):
    return max(0, -step), min(extent, extent - step)


def outer_layers(step, extent):
    return (extent - step, extent) if step > 0 else (0, -step)


STEPS_ALL = list(range(-REACH, REACH + 1))
STEPS_OUT = [step for step in STEPS_ALL if step != 0]


def tiled_bonds(step, tiles):
    early, late = [], []
    for tile in range(tiles):
        for bond in BONDS[step]:
            low, high = 8 * tile + bond[0], 8 * tile + 8 + bond[0]
            (early if low >= 0 and high <= 8 * tiles else late).append((tile, *bond))
    return early, late


def inner_plan(extent, late):
    plan, total = [], 0
    for step in STEPS_ALL:
        bonds = tiled_bonds(step, extent[1] // 8)[int(late)]
        first, last = inner_layers(step, extent[0])
        plan.append((step, first, last, bonds, total))
        total += (last - first) * len(bonds)
    return plan, total


def outer_plan(extent):
    plan, total = [], 0
    for step in STEPS_OUT:
        bonds = [(tile, *bond) for tile in range(extent[1] // 8) for bond in BONDS[step]]
        first, last = outer_layers(step, extent[0])
        plan.append((step, first, last, bonds, total))
        total += (last - first) * len(bonds)
    return plan, total


def reach_beside(distance):
    return max(max(abs(b), abs(c)) for a, b, c in OFFSETS if a >= distance)


def x_span(distance, size_y):
    return REACH - reach_beside(distance), REACH + size_y + reach_beside(distance)


def x_place(field, distance, size_y):
    lengths = [high - low for low, high in (x_span(far, size_y) for far in (3, 2, 1))]
    return field * sum(lengths) + sum(lengths[: REACH - distance])


def round_up(count):
    return (count + 7) // 8 * 8


def running(amounts):
    places, total = {}, 0
    for plane, amount in amounts:
        places[plane] = total
        total += amount
    return places, total


Z_UP, Z_UP_COUNT = running([(k, c) for k, (a, b, c) in enumerate(OFFSETS) if c > 0])
Z_DOWN, Z_DOWN_COUNT = running([(k, -c) for k, (a, b, c) in enumerate(OFFSETS) if c < 0])
Y_UP, Y_UP_COUNT = running([(k, b) for k, (a, b, c) in enumerate(OFFSETS) if b > 0])
Y_DOWN, Y_DOWN_COUNT = running([(k, -b) for k, (a, b, c) in enumerate(OFFSETS) if b < 0])
X_UP, X_UP_COUNT = running([(k, a) for k, (a, b, c) in enumerate(OFFSETS) if a > 0])
XY_UP, XY_UP_COUNT = running([(k, a * abs(b)) for k, (a, b, c) in enumerate(OFFSETS) if a * abs(b) > 0])


def lanes_like(value):
    return lax.broadcasted_iota(jnp.int32, value.shape, value.ndim - 1)


def rolled(value, shift):
    shift = shift % LANES
    return value if shift == 0 else pltpu.roll(value, shift, value.ndim - 1)


def beside_columns(low_pack, high_pack, lane_of, high_lanes=0):
    lanes = lanes_like(low_pack)
    return jnp.where(
        lanes < REACH,
        rolled(high_pack, -lane_of - high_lanes),
        rolled(low_pack, LANES - REACH - lane_of),
    )


def moved(main, beside, step):
    if step == 0:
        return main
    lanes = lanes_like(main)
    if step > 0:
        return rolled(jnp.where(lanes < step, beside, main), -step)
    return rolled(jnp.where(lanes >= LANES + step, beside, main), -step)


def pack_columns(field_of, count, extent, height):
    lanes = lax.broadcasted_iota(jnp.int32, (height, LANES), 1)
    up = jnp.zeros((height, LANES), jnp.float32)
    down = up
    for layer in range(extent):
        for field in range(count):
            lane_of = layer * SLOT + field * REACH
            value = field_of(field, layer)
            here = (lanes >= lane_of) & (lanes < lane_of + REACH)
            up = jnp.where(here, rolled(value, lane_of - (LANES - REACH)), up)
            down = jnp.where(here, rolled(value, lane_of), down)
    return up, down


def kept(flag, value):
    return jnp.where(flag > 0, value, 0.0)


def start_kernel(
    extent, pressure_in, motion_in, stiffness_in, borehole_in, flags_in, broken_in,
    motion, stiffness, pore, z_up, z_down, rows_up, rows_down, x_up,
    broken, pressure, borehole, flags, field_sems, layer_sems,
):
    size_x, size_y, _ = extent
    pairs = (
        (pressure_in, pressure), (borehole_in, borehole), (flags_in, flags),
        (motion_in, motion), (stiffness_in, stiffness),
    )
    copies = [
        pltpu.make_async_copy(source, target, field_sems.at[place])
        for place, (source, target) in enumerate(pairs)
    ]

    def layer_copy(layer):
        return pltpu.make_async_copy(
            broken_in.at[:, layer], broken.at[:, layer], layer_sems.at[layer]
        )

    for copy in copies:
        copy.start()
    for layer in range(size_x):
        layer_copy(layer).start()
    for copy in copies:
        copy.wait()
    ids = borehole[...]
    level = jnp.zeros(ids.shape, jnp.float32)
    for label in range(pressure.shape[0]):
        level = jnp.where(ids == label, pressure[label], level)
    pore[...] = flags[...].astype(jnp.float32) * level

    def field_of(field, layer):
        if field < 3:
            return motion[field, layer]
        return stiffness[layer] if field == 3 else pore[layer]

    up, down = pack_columns(field_of, 5, size_x, size_y)
    z_up[0:size_y] = up
    z_down[0:size_y] = down

    def one_layer(layer, carry):
        layer_copy(layer).wait()
        lanes = lax.broadcasted_iota(jnp.int32, (size_y, LANES), 1)
        rows = pl.ds(size_y + layer * size_y, size_y)
        up = jnp.zeros((size_y, LANES), jnp.float32)
        down = up
        for plane, (_, _, c) in enumerate(OFFSETS):
            if c > 0:
                at = Z_UP[plane]
                value = broken[plane, layer].astype(jnp.float32)
                up = jnp.where((lanes >= at) & (lanes < at + c), rolled(value, at + c), up)
            if c < 0:
                at = Z_DOWN[plane]
                value = broken[plane, layer].astype(jnp.float32)
                down = jnp.where((lanes >= at) & (lanes < at - c), rolled(value, at), down)
        z_up[rows] = up
        z_down[rows] = down
        return carry

    lax.fori_loop(0, size_x, one_layer, 0)
    for plane, (a, _, _) in enumerate(OFFSETS):
        for layer in range(a):
            at = (X_UP[plane] + layer) * size_y
            x_up[at : at + size_y] = broken[plane, size_x - a + layer].astype(jnp.float32)
    for plane, (_, b, _) in enumerate(OFFSETS):
        for layer in range(size_x):
            if b > 0:
                at = PAD + Y_UP[plane] * size_x + layer * b
                rows_up[at : at + b] = broken[plane, layer, size_y - b : size_y].astype(jnp.float32)
            if b < 0:
                at = PAD + Y_DOWN[plane] * size_x - layer * b
                rows_down[at : at - b] = broken[plane, layer, 0:-b].astype(jnp.float32)


def copy_y_rows(field_of, count, extent, low_pack, high_pack, y_up, y_down):
    size_x, size_y, _ = extent
    for field in range(count):
        for layer in range(size_x):
            at = (field * size_x + layer) * REACH
            y_up[at : at + REACH] = field_of(field, layer, slice(size_y - REACH, size_y))
            y_down[at : at + REACH] = field_of(field, layer, slice(0, REACH))
    at = count * size_x * REACH
    for pack in (low_pack, high_pack):
        y_up[at : at + REACH] = pack[size_y - REACH : size_y]
        y_down[at : at + REACH] = pack[0:REACH]
        at += REACH
    return at


def y_rows_kernel(extent, edges, motion, z_low, z_high, y_up, y_down):
    size_y = extent[1]
    low_pack = kept(edges[0], z_low[0:size_y])
    high_pack = kept(edges[1], z_high[0:size_y])
    copy_y_rows(
        lambda field, layer, rows: motion[field, layer, rows],
        3, extent, low_pack, high_pack, y_up, y_down,
    )


def y_rows_first_kernel(extent, edges, motion, stiffness, pore, z_low, z_high, y_up, y_down):
    size_x, size_y, _ = extent
    low_pack = kept(edges[0], z_low[0:size_y])
    high_pack = kept(edges[1], z_high[0:size_y])

    def field_of(field, layer, rows):
        if field < 3:
            return motion[field, layer, rows]
        return stiffness[layer, rows] if field == 3 else pore[layer, rows]

    base = copy_y_rows(field_of, 5, extent, low_pack, high_pack, y_up, y_down)
    for order, pack in enumerate((z_low, z_high)):
        for layer in range(size_x):
            first = size_y + layer * size_y
            at = base + (order * size_x + layer) * REACH
            y_up[at : at + REACH] = pack[first + size_y - REACH : first + size_y]
            y_down[at : at + REACH] = pack[first : first + REACH]


def widen(target, low_rows, middle, high_rows):
    size_y = middle.shape[0]
    target[0:REACH] = low_rows
    target[REACH : REACH + size_y] = middle
    target[REACH + size_y : 2 * REACH + size_y] = high_rows
    height = target.shape[0]
    target[2 * REACH + size_y : height] = jnp.zeros((height - 2 * REACH - size_y, LANES), jnp.float32)


def widen_fields(edges, field_of, count, extent, z_low, z_high, y_low, y_high, target, wide_pack):
    size_x, size_y, _ = extent
    for field in range(count):
        for layer in range(size_x):
            at = (field * size_x + layer) * REACH
            widen(
                target(field).at[layer],
                kept(edges[2], y_low[at : at + REACH]),
                field_of(field, layer),
                kept(edges[3], y_high[at : at + REACH]),
            )
    at = count * size_x * REACH
    for order, pack in enumerate((z_low, z_high)):
        widen(
            wide_pack.at[order],
            kept(edges[2], y_low[at : at + REACH]),
            kept(edges[order], pack[0:size_y]),
            kept(edges[3], y_high[at : at + REACH]),
        )
        at += REACH
    return at


def copy_x_layers(count, extent, target, wide_pack, x_up, x_down):
    size_x, size_y, _ = extent
    height = wide_pack.shape[1]
    for field in range(count):
        for distance in (3, 2, 1):
            low, high = x_span(distance, size_y)
            at = x_place(field, distance, size_y)
            x_up[at : at + high - low] = target(field)[size_x - distance, low:high]
            x_down[at : at + high - low] = target(field)[distance - 1, low:high]
    at = x_place(count, REACH, size_y)
    low_pack, high_pack = wide_pack[0], wide_pack[1]
    half = lanes_like(low_pack) < LANES // 2
    other = rolled(high_pack, LANES // 2)
    x_up[at : at + height] = jnp.where(half, other, low_pack)
    x_down[at : at + height] = jnp.where(half, low_pack, other)
    return at + height


def x_layers_kernel(
    extent, edges, motion, z_low, z_high, y_low, y_high, x_up, x_down, wide, wide_pack
):
    widen_fields(
        edges, lambda field, layer: motion[field, layer],
        3, extent, z_low, z_high, y_low, y_high, lambda field: wide.at[field], wide_pack,
    )
    copy_x_layers(3, extent, lambda field: wide.at[field], wide_pack, x_up, x_down)


def x_layers_first_kernel(
    extent, edges, motion, stiffness, pore, z_low, z_high, y_low, y_high, rows_low, rows_high,
    wide_static, wide_pack, wide_broken, x_up, x_down, wide,
):
    size_x, size_y, _ = extent

    def field_of(field, layer):
        if field < 3:
            return motion[field, layer]
        return stiffness[layer] if field == 3 else pore[layer]

    def target(field):
        return wide.at[field] if field < 3 else wide_static.at[field - 3]

    base = widen_fields(
        edges, field_of, 5, extent, z_low, z_high, y_low, y_high, target, wide_pack
    )
    for order, pack in enumerate((z_low, z_high)):
        for layer in range(size_x):
            first = size_y + layer * size_y
            at = base + (order * size_x + layer) * REACH
            widen(
                wide_broken.at[order, layer],
                y_low[at : at + REACH],
                pack[first : first + size_y],
                y_high[at : at + REACH],
            )
    at = copy_x_layers(4, extent, target, wide_pack, x_up, x_down)
    height = wide.shape[2]
    x_up[at : at + size_y] = pore[size_x - 1]
    x_down[at : at + size_y] = pore[0]
    at += size_y
    for order in range(2):
        for layer in range(NEAR):
            x_up[at : at + height] = wide_broken[order, size_x - NEAR + layer]
            at += height
    for plane, (a, b, _) in enumerate(OFFSETS):
        if a * b == 0:
            continue
        rows, many = abs(b), a * abs(b)
        source = rows_low if b > 0 else rows_high
        first = PAD + (Y_UP if b > 0 else Y_DOWN)[plane] * size_x + (size_x - a) * rows
        x_up[at + XY_UP[plane] : at + XY_UP[plane] + many] = source[first : first + many]


def each_shift(main, beside, add_step, reach=REACH):
    for step in range(-reach, reach + 1):
        value = moved(main, beside, step)
        yield step + REACH, value + float(step) if add_step and step else value


def wanted_keep(value, low, high, plane, step_z):
    if step_z == 0:
        return 1.0 - value
    lanes = lanes_like(value)
    if step_z < 0:
        beside = rolled(low(), -Z_UP[plane])
        value = jnp.where(lanes < -step_z, beside, rolled(value, -step_z))
    else:
        beside = rolled(high(), LANES - step_z - Z_DOWN[plane])
        value = jnp.where(lanes >= LANES - step_z, beside, rolled(value, -step_z))
    return 1.0 - value


def fill_outer(extent, count, edges, fields, x_low, x_high, shifts, besides):
    size_x, size_y, _ = extent
    height = shifts.shape[3]
    at = x_place(count, REACH, size_y)
    sides = ((x_low, size_x - REACH, -LANES // 2), (x_high, 0, LANES // 2))
    for side, (source, first, high_lanes) in enumerate(sides):
        pack = kept(edges[4 + side], source[at : at + height])
        for layer in range(REACH):
            for order, field in enumerate(fields):
                lane_of = (first + layer) * SLOT + field * REACH
                besides[order, side * REACH + layer] = beside_columns(
                    pack, pack, lane_of, high_lanes
                )
    for side, (source, _, _) in enumerate(sides):
        for layer in range(REACH):
            distance = REACH - layer if side == 0 else layer + 1
            low, high = x_span(distance, size_y)
            for order, field in enumerate(fields):
                start = x_place(field, distance, size_y)
                for step, value in each_shift(
                    kept(edges[4 + side], source[start : start + high - low]),
                    besides[order, side * REACH + layer, low:high],
                    field == 2, reach_beside(distance),
                ):
                    shifts[step, order, side * REACH + layer, low:high] = value


def weights_early_kernel(
    extent, edges, broken_in, stiffness, z_low, z_high, weights, keeps,
    shifts, planes, besides, broken, sems,
):
    size_x, size_y, _ = extent

    def layer_copy(layer):
        return pltpu.make_async_copy(broken_in.at[:, layer], broken.at[:, layer], sems.at[layer])

    for layer in range(size_x):
        layer_copy(layer).start()
    low_pack = kept(edges[0], z_low[0:size_y])
    high_pack = kept(edges[1], z_high[0:size_y])
    for layer in range(size_x):
        besides[layer] = beside_columns(low_pack, high_pack, layer * SLOT + 3 * REACH)
    for layer in range(size_x):
        for order, value in each_shift(stiffness[layer], besides[layer], False):
            shifts[order, layer, FIRST : FIRST + size_y] = value

    def fill(layer, carry):
        layer_copy(layer).wait()
        for plane in range(len(OFFSETS)):
            planes[plane, layer, FIRST : FIRST + size_y] = broken[plane, layer].astype(jnp.float32)
        return carry

    lax.fori_loop(0, size_x, fill, 0)
    for late, target in ((False, weights), (True, keeps)):
        for step, first, last, bonds, base in inner_plan(extent, late)[0]:

            def one_layer(layer, carry, step=step, first=first, bonds=bonds, base=base):
                slot = base + (layer - first) * len(bonds)
                far_layer = layer + step
                for order, (tile, step_y, step_z, plane, owner) in enumerate(bonds):
                    rows = slice(8 * tile, 8 * tile + 8)
                    far_rows = slice(FIRST + step_y + 8 * tile, FIRST + step_y + 8 * tile + 8)
                    if owner:
                        keep = 1.0 - broken[plane, layer, rows].astype(jnp.float32)
                    else:
                        at = size_y + far_layer * size_y + step_y + 8 * tile
                        keep = wanted_keep(
                            planes[plane, far_layer, far_rows],
                            lambda: z_low[pl.ds(at, 8)],
                            lambda: z_high[pl.ds(at, 8)],
                            plane, step_z,
                        )
                    keep = (0.5 * C_BOND) * keep
                    if not late:
                        far = shifts[step_z + REACH, far_layer, far_rows]
                        keep = jnp.where(far > 0.0, keep * (stiffness[layer, rows] + far), 0.0)
                    target[slot + order] = keep
                return carry

            lax.fori_loop(first, last, one_layer, 0)


def weights_late_kernel(
    extent, stiffness, wide, wide_pack, wide_broken, rows_low, rows_high, keeps, weights,
    shifts, besides,
):
    size_x, size_y, _ = extent
    for layer in range(size_x):
        besides[layer] = beside_columns(wide_pack[0], wide_pack[1], layer * SLOT + 3 * REACH)
    for layer in range(size_x):
        for order, value in each_shift(wide[0, layer], besides[layer], False):
            shifts[order, layer] = value
    for step, first, last, bonds, base in inner_plan(extent, True)[0]:

        def one_layer(layer, carry, step=step, first=first, bonds=bonds, base=base):
            slot = base + (layer - first) * len(bonds)
            far_layer = layer + step
            sublanes = lax.broadcasted_iota(jnp.int32, (8, LANES), 0)
            for order, (tile, step_y, step_z, plane, owner) in enumerate(bonds):
                rows = slice(8 * tile, 8 * tile + 8)
                far_rows = slice(REACH + step_y + 8 * tile, REACH + step_y + 8 * tile + 8)
                keep = keeps[slot + order]
                if not owner:
                    if step_y < 0:
                        at = PAD + Y_UP[plane] * size_x - far_layer * step_y
                        value = rows_low[pl.ds(at, 8)]
                        across = sublanes < -step_y
                    else:
                        at = PAD + Y_DOWN[plane] * size_x + far_layer * step_y + step_y - 8
                        value = rows_high[pl.ds(at, 8)]
                        across = sublanes >= 8 - step_y
                    halo = wanted_keep(
                        value,
                        lambda: wide_broken[0, far_layer, far_rows],
                        lambda: wide_broken[1, far_layer, far_rows],
                        plane, step_z,
                    )
                    keep = jnp.where(across, (0.5 * C_BOND) * halo, keep)
                far = shifts[step_z + REACH, far_layer, far_rows]
                weights[slot + order] = jnp.where(
                    far > 0.0, keep * (stiffness[layer, rows] + far), 0.0
                )
            return carry

        lax.fori_loop(first, last, one_layer, 0)


def weights_outer_kernel(
    extent, edges, stiffness, pore, wide, wide_pack, x_up, x_broken, x_low, x_high,
    weights, pressing, shifts, planes, besides,
):
    size_x, size_y, _ = extent
    height = wide.shape[2]
    pore_at = x_place(4, REACH, size_y) + height
    broken_at = pore_at + size_y
    rows_at = broken_at + 2 * NEAR * height
    fill_outer(extent, 4, edges, (3,), x_low, x_high, shifts, besides)
    for plane, (a, b, _) in enumerate(OFFSETS):
        for layer in range(a):
            at = (X_UP[plane] + layer) * size_y
            place = X_UP[plane] + layer
            planes[place, REACH : REACH + size_y] = x_broken[at : at + size_y]
            at = rows_at + XY_UP.get(plane, 0) + layer * abs(b)
            if b > 0:
                planes[place, REACH - b : REACH] = x_low[at : at + b]
            if b < 0:
                planes[place, REACH + size_y : REACH + size_y - b] = x_low[at : at - b]
    for step, first, last, bonds, base in outer_plan(extent)[0]:
        for layer in range(first, last):
            slot = base + (layer - first) * len(bonds)
            far_layer = layer + step
            far_layer = far_layer + REACH if far_layer < 0 else far_layer - size_x + REACH
            for order, (tile, step_y, step_z, plane, owner) in enumerate(bonds):
                rows = slice(8 * tile, 8 * tile + 8)
                far_rows = slice(REACH + step_y + 8 * tile, REACH + step_y + 8 * tile + 8)
                far = shifts[step_z + REACH, 0, far_layer, far_rows]
                if owner:
                    at = (X_UP[plane] + layer - first) * size_y + 8 * tile
                    keep = 1.0 - x_up[at : at + 8]
                else:
                    low_at = broken_at + (far_layer + NEAR - REACH) * height
                    high_at = low_at + NEAR * height
                    keep = wanted_keep(
                        planes[X_UP[plane] + layer, far_rows],
                        lambda: x_low[far_rows.start + low_at : far_rows.stop + low_at],
                        lambda: x_low[far_rows.start + high_at : far_rows.stop + high_at],
                        plane, step_z,
                    )
                value = keep * (0.5 * C_BOND) * (stiffness[layer, rows] + far)
                weights[slot + order] = jnp.where(far > 0.0, value, 0.0)

    middle = slice(REACH, REACH + size_y)

    def wide_field(field, layer):
        if layer < 0 or layer >= size_x:
            source = x_low if layer < 0 else x_high
            at = x_place(field, 1, size_y) + reach_beside(1) if field == 3 else pore_at
            return kept(edges[4 if layer < 0 else 5], source[at : at + size_y])
        return wide[field - 3, layer, middle]

    for layer in range(size_x):
        own = pore[layer]
        for axis in range(3):
            total = jnp.zeros((size_y, LANES), jnp.float32)
            for sign in (1, -1):
                if axis == 0:
                    inside = wide_field(3, layer + sign)
                    level = wide_field(4, layer + sign)
                elif axis == 1:
                    rows = slice(REACH + sign, REACH + sign + size_y)
                    inside = wide[0, layer, rows]
                    level = wide[1, layer, rows]
                else:
                    inside, level = (
                        moved(
                            wide[field - 3, layer],
                            beside_columns(
                                wide_pack[0], wide_pack[1], layer * SLOT + field * REACH
                            ),
                            sign,
                        )[middle]
                        for field in (3, 4)
                    )
                total = total + jnp.where(inside > 0.0, (-0.5 * sign) * (level - own), 0.0)
            pressing[axis, layer] = total


def add_bonds(bonds, step, layer, far_layer, first_row, motion, shifts, weights, slot, total):
    for tile in sorted({bond[0] for bond in bonds}):
        rows = slice(8 * tile, 8 * tile + 8)
        own = [motion[axis, layer, rows] for axis in range(3)]
        near_x = own[0] - float(step)
        near_y = {step_y: own[1] - float(step_y) for step_y in range(-REACH, REACH + 1)}
        force = [total[axis, layer, rows] for axis in range(3)]
        for order, (bond_tile, step_y, step_z, plane, _) in enumerate(bonds):
            if bond_tile != tile:
                continue
            far_rows = slice(first_row + step_y + 8 * tile, first_row + step_y + 8 * tile + 8)
            far = [shifts[step_z + REACH, axis, far_layer, far_rows] for axis in range(3)]
            radial = [far[0] - near_x, far[1] - near_y[step_y], far[2] - own[2]]
            square = radial[0] * radial[0] + radial[1] * radial[1] + radial[2] * radial[2]
            rest = math.sqrt(sum(part * part for part in OFFSETS[plane]))
            factor = weights[slot + order] * (1.0 / rest - lax.rsqrt(square))
            force = [force[axis] + factor * radial[axis] for axis in range(3)]
        for axis in range(3):
            total[axis, layer, rows] = force[axis]


def add_inner(extent, late, fill, motion, shifts, weights, total):
    lax.fori_loop(0, extent[0], fill, 0, unroll=UNROLL_FILL)
    for step, first, last, bonds, base in inner_plan(extent, late)[0]:
        if not bonds:
            continue

        def one_layer(layer, carry, step=step, first=first, bonds=bonds, base=base):
            slot = base + (layer - first) * len(bonds)
            add_bonds(bonds, step, layer, layer + step, FIRST, motion, shifts, weights, slot, total)
            return carry

        lax.fori_loop(first, last, one_layer, 0, unroll=UNROLL if last - first > 1 else 1)


def force_early_kernel(extent, edges, motion, z_low, z_high, weights, total, shifts, besides):
    size_x, size_y, _ = extent
    total[...] = jnp.zeros(total.shape, jnp.float32)
    low_pack = kept(edges[0], z_low[0:size_y])
    high_pack = kept(edges[1], z_high[0:size_y])
    for layer in range(size_x):
        for axis in range(3):
            besides[axis, layer] = beside_columns(
                low_pack, high_pack, layer * SLOT + axis * REACH
            )

    def fill(layer, carry):
        for axis in range(3):
            for order, value in each_shift(motion[axis, layer], besides[axis, layer], axis == 2):
                shifts[order, axis, layer, FIRST : FIRST + size_y] = value
        return carry

    add_inner(extent, False, fill, motion, shifts, weights, total)


def force_late_kernel(
    extent, count, edges, motion, early, early_shifts, y_low, y_high, weights,
    total, shifts, halo, besides,
):
    size_x, size_y, _ = extent
    total[...] = early[...]
    middle = slice(FIRST, FIRST + size_y)
    above = FIRST + size_y

    def across(place, at):
        halo[place, 0:REACH] = kept(edges[3], y_high[at : at + REACH])
        halo[place, REACH : 8 - REACH] = jnp.zeros((8 - 2 * REACH, LANES), jnp.float32)
        halo[place, 8 - REACH : 8] = kept(edges[2], y_low[at : at + REACH])

    packs = 3 * size_x
    for order in range(2):
        across(packs + order, (count * size_x + order) * REACH)
    for place in range(3 * size_x):
        across(place, place * REACH)
    low_pack, high_pack = halo[packs], halo[packs + 1]
    for layer in range(size_x):
        for axis in range(3):
            besides[axis * size_x + layer] = beside_columns(
                low_pack, high_pack, layer * SLOT + axis * REACH
            )

    def fill(layer, carry):
        for axis in range(3):
            place = axis * size_x + layer
            for order, value in each_shift(halo[place], besides[place], axis == 2):
                shifts[order, axis, layer, middle] = early_shifts[order, axis, layer, middle]
                shifts[order, axis, layer, FIRST - REACH : FIRST] = value[8 - REACH : 8]
                shifts[order, axis, layer, above : above + REACH] = value[0:REACH]
        return carry

    add_inner(extent, True, fill, motion, shifts, weights, total)


def finish_kernel(
    extent, count, stage, edges, motion, speed, pressing, inner, weights, x_low, x_high, *refs
):
    size_x, size_y, _ = extent
    if stage == "last":
        motion_out, speed_out, accel_out, total, shifts, besides = refs
    else:
        motion_out, speed_out, z_up, z_down, total, shifts, besides = refs
    total[...] = inner[...] + pressing[...]
    fill_outer(extent, count, edges, range(3), x_low, x_high, shifts, besides)
    for step, first, last, bonds, base in outer_plan(extent)[0]:
        for layer in range(first, last):
            slot = base + (layer - first) * len(bonds)
            far_layer = layer + step + (REACH if step < 0 else REACH - size_x)
            add_bonds(bonds, step, layer, far_layer, REACH, motion, shifts, weights, slot, total)
    accel = total[...]
    new_speed = speed[...] + HALF_DT * accel
    if stage == "last":
        motion_out[...] = motion[...]
        speed_out[...] = new_speed
        accel_out[...] = accel
        return
    if stage == "middle":
        new_speed = new_speed + HALF_DT * accel
    speed_out[...] = new_speed
    motion_out[...] = motion[...] + DT_STEP * new_speed
    up, down = pack_columns(lambda axis, layer: motion_out[axis, layer], 3, size_x, size_y)
    z_up[...] = up
    z_down[...] = down


VMEM = pl.BlockSpec(memory_space=pltpu.VMEM)
SMEM = pl.BlockSpec(memory_space=pltpu.SMEM)


def call(kernel, scalars, operands, shapes, scratch=(), name=None, results=(), far=()):
    operands = [pltpu.with_memory_space_constraint(operand, pltpu.HBM) for operand in far] + [
        pltpu.with_memory_space_constraint(operand, pltpu.VMEM) for operand in operands
    ]
    return pl.pallas_call(
        kernel,
        out_shape=[
            jax.ShapeDtypeStruct(shape, jnp.float32)
            if place in results
            else pltpu.VMEM(shape, jnp.float32)
            for place, shape in enumerate(shapes)
        ],
        in_specs=[SMEM] * len(scalars)
        + [pl.BlockSpec(memory_space=pltpu.HBM)] * len(far)
        + [VMEM] * (len(operands) - len(far)),
        out_specs=[VMEM] * len(shapes),
        scratch_shapes=[
            pltpu.VMEM(item, jnp.float32) if isinstance(item, tuple) else item for item in scratch
        ],
        compiler_params=pltpu.CompilerParams(vmem_limit_bytes=24 * 1024 * 1024),
        name=name,
    )(*scalars, *operands)


def sent(value, axis, distance):
    count = lax.axis_size(axis)
    return lax.ppermute(value, axis, [(i, (i + distance) % count) for i in range(count)])


def on_device(displacement, velocity, stiffness, broken, borehole_id, flags, pressure):
    extent = stiffness.shape
    size_x, size_y, _ = extent
    height = size_y + 8
    tall = size_y + 2 * FIRST
    edges = jnp.stack(
        [
            end
            for axis in ("gz", "gy", "gx")
            for end in (
                (lax.axis_index(axis) > 0).astype(jnp.int32),
                (lax.axis_index(axis) < lax.axis_size(axis) - 1).astype(jnp.int32),
            )
        ]
    )
    field = (size_x, size_y, LANES)
    vector = (3,) + field
    part = functools.partial

    pack = (size_y + size_x * size_y + PAD, LANES)
    rows_shapes = [(count * size_x + 2 * PAD, LANES) for count in (Y_UP_COUNT, Y_DOWN_COUNT)]
    layers_shape = (X_UP_COUNT * size_y, LANES)
    motion, stiffness, pore, z_up, z_down, rows_up, rows_down, x_up = pl.pallas_call(
        part(start_kernel, extent),
        out_shape=[
            pltpu.VMEM(shape, kind)
            for shape, kind in (
                (vector, jnp.float32), (field, jnp.float32),
                (field, jnp.float32), (pack, jnp.float32), (pack, jnp.float32),
                (rows_shapes[0], jnp.float32), (rows_shapes[1], jnp.float32),
                (layers_shape, jnp.float32),
            )
        ],
        in_specs=[pl.BlockSpec(memory_space=pltpu.HBM)] * 6,
        out_specs=[VMEM] * 8,
        scratch_shapes=[
            pltpu.VMEM(broken.shape, jnp.int32),
            pltpu.SMEM(pressure.shape, jnp.float32),
            pltpu.VMEM(field, jnp.int32),
            pltpu.VMEM(field, jnp.int32),
            pltpu.SemaphoreType.DMA((5,)),
            pltpu.SemaphoreType.DMA((size_x,)),
        ],
        compiler_params=pltpu.CompilerParams(vmem_limit_bytes=24 * 1024 * 1024),
        name="start",
    )(
        *(
            pltpu.with_memory_space_constraint(operand, pltpu.HBM)
            for operand in (pressure, displacement, stiffness, borehole_id, flags, broken)
        )
    )
    z_low = sent(z_up, "gz", 1)
    z_high = sent(z_down, "gz", -1)
    rows_low = sent(rows_up, "gy", 1)
    rows_high = sent(rows_down, "gy", -1)
    x_broken = sent(x_up, "gx", 1)
    rows = (round_up(5 * size_x * REACH + 2 * REACH + 2 * size_x * REACH), LANES)
    y_up, y_down = call(
        part(y_rows_first_kernel, extent), [edges],
        [motion, stiffness, pore, z_low, z_high], [rows, rows], name="y_rows_first",
    )
    y_low = sent(y_up, "gy", 1)
    y_high = sent(y_down, "gy", -1)
    moves = 2 * REACH + 1
    early_slots = inner_plan(extent, False)[1]
    late_slots = inner_plan(extent, True)[1]
    outer_slots = outer_plan(extent)[1]
    weights_early, keeps = call(
        part(weights_early_kernel, extent), [edges], [stiffness, z_low, z_high],
        [(early_slots, 8, LANES), (late_slots, 8, LANES)],
        [
            (moves, size_x, tall, LANES),
            (len(OFFSETS), size_x, tall, LANES),
            field,
            pltpu.VMEM(broken.shape, jnp.int32),
            pltpu.SemaphoreType.DMA((size_x,)),
        ], name="weights_early", far=[broken],
    )

    def force_early(motion, z_low, z_high):
        return call(
            part(force_early_kernel, extent), [edges], [motion, z_low, z_high, weights_early],
            [vector, (moves, 3, size_x, tall, LANES)], [vector], name="force_early",
        )

    def force_late(count, motion, early, early_shifts, y_low, y_high):
        return call(
            part(force_late_kernel, extent, count), [edges],
            [motion, early, early_shifts, y_low, y_high, weights_late], [vector],
            [(moves, 3, size_x, tall, LANES), (2 + 3 * size_x, 8, LANES), (3 * size_x, 8, LANES)], name="force_late",
        )[0]

    early, early_shifts = force_early(motion, z_low, z_high)
    y_low, y_high, x_broken, early = lax.optimization_barrier((y_low, y_high, x_broken, early))
    layers = x_place(4, REACH, size_y) + height + size_y
    wide_static, wide_pack, wide_broken, x_fields_up, x_fields_down = call(
        part(x_layers_first_kernel, extent), [edges],
        [motion, stiffness, pore, z_low, z_high, y_low, y_high, rows_low, rows_high],
        [
            (2, size_x, height, LANES),
            (2, height, LANES),
            (2, size_x, height, LANES),
            (round_up(layers + 2 * NEAR * height + XY_UP_COUNT), LANES),
            (round_up(layers), LANES),
        ], [(3, size_x, height, LANES)], name="x_layers_first",
    )
    x_low = sent(x_fields_up, "gx", 1)
    x_high = sent(x_fields_down, "gx", -1)
    (weights_late,) = call(
        part(weights_late_kernel, extent), [],
        [stiffness, wide_static, wide_pack, wide_broken, rows_low, rows_high, keeps],
        [(late_slots, 8, LANES)],
        [(moves, size_x, height, LANES), (size_x, height, LANES)], name="weights_late",
    )
    inner = force_late(5, motion, early, early_shifts, y_low, y_high)
    outer_weights, pressing = call(
        part(weights_outer_kernel, extent), [edges],
        [stiffness, pore, wide_static, wide_pack, x_up, x_broken, x_low, x_high],
        [(outer_slots, 8, LANES), vector],
        [
            (moves, 1, 2 * REACH, height, LANES),
            (X_UP_COUNT, height, LANES),
            (1, 2 * REACH, height, LANES),
        ], name="weights_outer",
    )

    def finish(stage, count, motion, speed, inner, x_low, x_high):
        columns = (size_y, LANES)
        shapes = [vector] * 3 if stage == "last" else [vector, vector, columns, columns]
        return call(
            part(finish_kernel, extent, count, stage), [edges],
            [motion, speed, pressing, inner, outer_weights, x_low, x_high],
            shapes,
            [
                vector,
                (moves, 3, 2 * REACH, height, LANES),
                (3, 2 * REACH, height, LANES),
            ], name="finish_" + stage,
            results=(0, 1, 2) if stage == "last" else (),
        )

    motion, speed, z_up, z_down = finish(
        "first", 4, motion, velocity, inner, x_low, x_high
    )
    for step_index in range(STEPS):
        z_low = sent(z_up, "gz", 1)
        z_high = sent(z_down, "gz", -1)
        rows = (round_up(3 * size_x * REACH + 2 * REACH), LANES)
        y_up, y_down = call(
            part(y_rows_kernel, extent), [edges], [motion, z_low, z_high], [rows, rows],
            name="y_rows",
        )
        y_low = sent(y_up, "gy", 1)
        y_high = sent(y_down, "gy", -1)
        early, early_shifts = force_early(motion, z_low, z_high)
        y_low, y_high, early = lax.optimization_barrier((y_low, y_high, early))
        layers = round_up(x_place(3, REACH, size_y) + height)
        x_up, x_down = call(
            part(x_layers_kernel, extent), [edges],
            [motion, z_low, z_high, y_low, y_high],
            [(layers, LANES), (layers, LANES)],
            [(3, size_x, height, LANES), (2, height, LANES)], name="x_layers",
        )
        x_low = sent(x_up, "gx", 1)
        x_high = sent(x_down, "gx", -1)
        inner = force_late(3, motion, early, early_shifts, y_low, y_high)
        if step_index < STEPS - 1:
            motion, speed, z_up, z_down = finish("middle", 3, motion, speed, inner, x_low, x_high)
        else:
            motion, speed, accel = finish("last", 3, motion, speed, inner, x_low, x_high)
    return (motion, speed, accel)


def solution(mesh):
    in_specs = (
        P(None, "gx", "gy", "gz"),
        P(None, "gx", "gy", "gz"),
        P("gx", "gy", "gz"),
        P(None, "gx", "gy", "gz"),
        P("gx", "gy", "gz"),
        P("gx", "gy", "gz"),
        P(),
    )
    out_specs = (P(None, "gx", "gy", "gz"), P(None, "gx", "gy", "gz"), P(None, "gx", "gy", "gz"))
    return jax.shard_map(
        on_device, mesh=mesh, in_specs=in_specs, out_specs=out_specs, check_vma=False
    )
```

```python
import functools
import math

import jax
import jax.numpy as jnp
from jax import lax
from jax.experimental import pallas as pl
from jax.experimental.pallas import tpu as pltpu
from jax.sharding import PartitionSpec as P

STEPS = 2
C_BOND = 3.0
DT_STEP = 0.04
REACH = 3
NEAR = 2
LANES = 128
SLOT = 16
PAD = 8
UNROLL = 2
UNROLL_FILL = 2
FIRST = 8
HALF_DT = 0.5 * DT_STEP


def half_offsets():
    result = []
    for step_x in range(0, 4):
        for step_y in range(-3, 4):
            for step_z in range(-3, 4):
                square = step_x * step_x + step_y * step_y + step_z * step_z
                if square == 0 or square > 9:
                    continue
                if step_x > 0 or (step_x == 0 and (step_y > 0 or (step_y == 0 and step_z > 0))):
                    result.append((step_x, step_y, step_z))
    return result


OFFSETS = half_offsets()
BONDS = {step: [] for step in range(-REACH, REACH + 1)}
for _plane, (_a, _b, _c) in enumerate(OFFSETS):
    BONDS[_a].append((_b, _c, _plane, True))
    BONDS[-_a].append((-_b, -_c, _plane, False))


def inner_layers(step, extent):
    return max(0, -step), min(extent, extent - step)


def outer_layers(step, extent):
    return (extent - step, extent) if step > 0 else (0, -step)


STEPS_ALL = list(range(-REACH, REACH + 1))
STEPS_OUT = [step for step in STEPS_ALL if step != 0]


def tiled_bonds(step, tiles):
    early, late = [], []
    for tile in range(tiles):
        for bond in BONDS[step]:
            low, high = 8 * tile + bond[0], 8 * tile + 8 + bond[0]
            (early if low >= 0 and high <= 8 * tiles else late).append((tile, *bond))
    return early, late


def inner_plan(extent, late):
    plan, total = [], 0
    for step in STEPS_ALL:
        bonds = tiled_bonds(step, extent[1] // 8)[int(late)]
        first, last = inner_layers(step, extent[0])
        plan.append((step, first, last, bonds, total))
        total += (last - first) * len(bonds)
    return plan, total


def outer_plan(extent):
    plan, total = [], 0
    for step in STEPS_OUT:
        bonds = [(tile, *bond) for tile in range(extent[1] // 8) for bond in BONDS[step]]
        first, last = outer_layers(step, extent[0])
        plan.append((step, first, last, bonds, total))
        total += (last - first) * len(bonds)
    return plan, total


def reach_beside(distance):
    return max(max(abs(b), abs(c)) for a, b, c in OFFSETS if a >= distance)


def x_span(distance, size_y):
    return REACH - reach_beside(distance), REACH + size_y + reach_beside(distance)


def x_place(field, distance, size_y):
    lengths = [high - low for low, high in (x_span(far, size_y) for far in (3, 2, 1))]
    return field * sum(lengths) + sum(lengths[: REACH - distance])


def round_up(count):
    return (count + 7) // 8 * 8


def running(amounts):
    places, total = {}, 0
    for plane, amount in amounts:
        places[plane] = total
        total += amount
    return places, total


Z_UP, Z_UP_COUNT = running([(k, c) for k, (a, b, c) in enumerate(OFFSETS) if c > 0])
Z_DOWN, Z_DOWN_COUNT = running([(k, -c) for k, (a, b, c) in enumerate(OFFSETS) if c < 0])
Y_UP, Y_UP_COUNT = running([(k, b) for k, (a, b, c) in enumerate(OFFSETS) if b > 0])
Y_DOWN, Y_DOWN_COUNT = running([(k, -b) for k, (a, b, c) in enumerate(OFFSETS) if b < 0])
X_UP, X_UP_COUNT = running([(k, a) for k, (a, b, c) in enumerate(OFFSETS) if a > 0])
XY_UP, XY_UP_COUNT = running([(k, a * abs(b)) for k, (a, b, c) in enumerate(OFFSETS) if a * abs(b) > 0])


def lanes_like(value):
    return lax.broadcasted_iota(jnp.int32, value.shape, value.ndim - 1)


def rolled(value, shift):
    shift = shift % LANES
    return value if shift == 0 else pltpu.roll(value, shift, value.ndim - 1)


def beside_columns(low_pack, high_pack, lane_of, high_lanes=0):
    lanes = lanes_like(low_pack)
    return jnp.where(
        lanes < REACH,
        rolled(high_pack, -lane_of - high_lanes),
        rolled(low_pack, LANES - REACH - lane_of),
    )


def moved(main, beside, step):
    if step == 0:
        return main
    lanes = lanes_like(main)
    if step > 0:
        return rolled(jnp.where(lanes < step, beside, main), -step)
    return rolled(jnp.where(lanes >= LANES + step, beside, main), -step)


def pack_columns(field_of, count, extent, height):
    lanes = lax.broadcasted_iota(jnp.int32, (height, LANES), 1)
    up = jnp.zeros((height, LANES), jnp.float32)
    down = up
    for layer in range(extent):
        for field in range(count):
            lane_of = layer * SLOT + field * REACH
            value = field_of(field, layer)
            here = (lanes >= lane_of) & (lanes < lane_of + REACH)
            up = jnp.where(here, rolled(value, lane_of - (LANES - REACH)), up)
            down = jnp.where(here, rolled(value, lane_of), down)
    return up, down


class Either:
    def __init__(self, odd, if_odd, if_even):
        self.odd, self.if_odd, self.if_even = odd, if_odd, if_even

    def __getitem__(self, rows):
        return jnp.where(self.odd > 0, self.if_odd[rows], self.if_even[rows])


def by_parity(odd, near, far, write):
    @pl.when(odd > 0)
    def _():
        write(far, near)

    @pl.when(odd == 0)
    def _():
        write(near, far)


def kept(flag, value):
    return jnp.where(flag > 0, value, 0.0)


def start_kernel(
    extent, pressure_in, motion_in, stiffness_in, borehole_in, flags_in, broken_in,
    motion, stiffness, pore, z_up, z_down, rows_up, rows_down, x_up,
    broken, pressure, borehole, flags, field_sems, layer_sems,
):
    size_x, size_y, _ = extent
    pairs = (
        (pressure_in, pressure), (borehole_in, borehole), (flags_in, flags),
        (motion_in, motion), (stiffness_in, stiffness),
    )
    copies = [
        pltpu.make_async_copy(source, target, field_sems.at[place])
        for place, (source, target) in enumerate(pairs)
    ]

    def layer_copy(layer):
        return pltpu.make_async_copy(
            broken_in.at[:, layer], broken.at[:, layer], layer_sems.at[layer]
        )

    for copy in copies:
        copy.start()
    for layer in range(size_x):
        layer_copy(layer).start()
    for copy in copies:
        copy.wait()
    ids = borehole[...]
    level = jnp.zeros(ids.shape, jnp.float32)
    for label in range(pressure.shape[0]):
        level = jnp.where(ids == label, pressure[label], level)
    pore[...] = flags[...].astype(jnp.float32) * level

    def field_of(field, layer):
        if field < 3:
            return motion[field, layer]
        return stiffness[layer] if field == 3 else pore[layer]

    up, down = pack_columns(field_of, 5, size_x, size_y)
    z_up[0:size_y] = up
    z_down[0:size_y] = down

    def one_layer(layer, carry):
        layer_copy(layer).wait()
        lanes = lax.broadcasted_iota(jnp.int32, (size_y, LANES), 1)
        rows = pl.ds(size_y + layer * size_y, size_y)
        up = jnp.zeros((size_y, LANES), jnp.float32)
        down = up
        for plane, (_, _, c) in enumerate(OFFSETS):
            if c > 0:
                at = Z_UP[plane]
                value = broken[plane, layer].astype(jnp.float32)
                up = jnp.where((lanes >= at) & (lanes < at + c), rolled(value, at + c), up)
            if c < 0:
                at = Z_DOWN[plane]
                value = broken[plane, layer].astype(jnp.float32)
                down = jnp.where((lanes >= at) & (lanes < at - c), rolled(value, at), down)
        z_up[rows] = up
        z_down[rows] = down
        return carry

    lax.fori_loop(0, size_x, one_layer, 0)
    for plane, (a, _, _) in enumerate(OFFSETS):
        for layer in range(a):
            at = (X_UP[plane] + layer) * size_y
            x_up[at : at + size_y] = broken[plane, size_x - a + layer].astype(jnp.float32)
    for plane, (_, b, _) in enumerate(OFFSETS):
        for layer in range(size_x):
            if b > 0:
                at = PAD + Y_UP[plane] * size_x + layer * b
                rows_up[at : at + b] = broken[plane, layer, size_y - b : size_y].astype(jnp.float32)
            if b < 0:
                at = PAD + Y_DOWN[plane] * size_x - layer * b
                rows_down[at : at - b] = broken[plane, layer, 0:-b].astype(jnp.float32)


def copy_y_rows(field_of, count, extent, low_pack, high_pack, y_up, y_down):
    size_x, size_y, _ = extent
    for field in range(count):
        for layer in range(size_x):
            at = (field * size_x + layer) * REACH
            y_up[at : at + REACH] = field_of(field, layer, slice(size_y - REACH, size_y))
            y_down[at : at + REACH] = field_of(field, layer, slice(0, REACH))
    at = count * size_x * REACH
    for pack in (low_pack, high_pack):
        y_up[at : at + REACH] = pack[size_y - REACH : size_y]
        y_down[at : at + REACH] = pack[0:REACH]
        at += REACH
    return at


def y_rows_kernel(extent, edges, motion, z_low, z_high, y_up, y_down):
    size_y = extent[1]
    low_pack = kept(edges[0], z_low[0:size_y])
    high_pack = kept(edges[1], z_high[0:size_y])
    copy_y_rows(
        lambda field, layer, rows: motion[field, layer, rows],
        3, extent, low_pack, high_pack, y_up, y_down,
    )


def y_rows_first_kernel(extent, edges, motion, stiffness, pore, z_low, z_high, y_up, y_down):
    size_x, size_y, _ = extent
    low_pack = kept(edges[0], z_low[0:size_y])
    high_pack = kept(edges[1], z_high[0:size_y])

    def field_of(field, layer, rows):
        if field < 3:
            return motion[field, layer, rows]
        return stiffness[layer, rows] if field == 3 else pore[layer, rows]

    base = copy_y_rows(field_of, 5, extent, low_pack, high_pack, y_up, y_down)
    for order, pack in enumerate((z_low, z_high)):
        for layer in range(size_x):
            first = size_y + layer * size_y
            at = base + (order * size_x + layer) * REACH
            y_up[at : at + REACH] = pack[first + size_y - REACH : first + size_y]
            y_down[at : at + REACH] = pack[first : first + REACH]


def widen(target, low_rows, middle, high_rows):
    size_y = middle.shape[0]
    target[0:REACH] = low_rows
    target[REACH : REACH + size_y] = middle
    target[REACH + size_y : 2 * REACH + size_y] = high_rows
    height = target.shape[0]
    target[2 * REACH + size_y : height] = jnp.zeros((height - 2 * REACH - size_y, LANES), jnp.float32)


def widen_fields(edges, field_of, count, extent, z_low, z_high, y_low, y_high, target, wide_pack):
    size_x, size_y, _ = extent
    for field in range(count):
        for layer in range(size_x):
            at = (field * size_x + layer) * REACH
            widen(
                target(field).at[layer],
                kept(edges[2], y_low[at : at + REACH]),
                field_of(field, layer),
                kept(edges[3], y_high[at : at + REACH]),
            )
    at = count * size_x * REACH
    for order, pack in enumerate((z_low, z_high)):
        widen(
            wide_pack.at[order],
            kept(edges[2], y_low[at : at + REACH]),
            kept(edges[order], pack[0:size_y]),
            kept(edges[3], y_high[at : at + REACH]),
        )
        at += REACH
    return at


def copy_x_layers(count, extent, target, wide_pack, x_up, x_down):
    size_x, size_y, _ = extent
    height = wide_pack.shape[1]
    for field in range(count):
        for distance in (3, 2, 1):
            low, high = x_span(distance, size_y)
            at = x_place(field, distance, size_y)
            x_up[at : at + high - low] = target(field)[size_x - distance, low:high]
            x_down[at : at + high - low] = target(field)[distance - 1, low:high]
    at = x_place(count, REACH, size_y)
    low_pack, high_pack = wide_pack[0], wide_pack[1]
    half = lanes_like(low_pack) < LANES // 2
    other = rolled(high_pack, LANES // 2)
    x_up[at : at + height] = jnp.where(half, other, low_pack)
    x_down[at : at + height] = jnp.where(half, low_pack, other)
    return at + height


def x_layers_kernel(
    extent, edges, motion, z_low, z_high, y_low, y_high, x_near, x_far, wide, wide_pack
):
    widen_fields(
        edges, lambda field, layer: motion[field, layer],
        3, extent, z_low, z_high, y_low, y_high, lambda field: wide.at[field], wide_pack,
    )

    def write(x_up, x_down):
        copy_x_layers(3, extent, lambda field: wide.at[field], wide_pack, x_up, x_down)

    by_parity(edges[6], x_near, x_far, write)


def x_layers_first_kernel(
    extent, edges, motion, stiffness, pore, z_low, z_high, y_low, y_high, rows_low, rows_high,
    wide_static, wide_pack, wide_broken, x_near, x_far, wide,
):
    size_x, size_y, _ = extent

    def field_of(field, layer):
        if field < 3:
            return motion[field, layer]
        return stiffness[layer] if field == 3 else pore[layer]

    def target(field):
        return wide.at[field] if field < 3 else wide_static.at[field - 3]

    base = widen_fields(
        edges, field_of, 5, extent, z_low, z_high, y_low, y_high, target, wide_pack
    )
    for order, pack in enumerate((z_low, z_high)):
        for layer in range(size_x):
            first = size_y + layer * size_y
            at = base + (order * size_x + layer) * REACH
            widen(
                wide_broken.at[order, layer],
                y_low[at : at + REACH],
                pack[first : first + size_y],
                y_high[at : at + REACH],
            )

    def write(x_up, x_down):
        at = copy_x_layers(4, extent, target, wide_pack, x_up, x_down)
        height = wide.shape[2]
        x_up[at : at + size_y] = pore[size_x - 1]
        x_down[at : at + size_y] = pore[0]
        at += size_y
        for order in range(2):
            for layer in range(NEAR):
                x_up[at : at + height] = wide_broken[order, size_x - NEAR + layer]
                at += height
        for plane, (a, b, _) in enumerate(OFFSETS):
            if a * b == 0:
                continue
            rows, many = abs(b), a * abs(b)
            source = rows_low if b > 0 else rows_high
            first = PAD + (Y_UP if b > 0 else Y_DOWN)[plane] * size_x + (size_x - a) * rows
            x_up[at + XY_UP[plane] : at + XY_UP[plane] + many] = source[first : first + many]

    by_parity(edges[6], x_near, x_far, write)


def each_shift(main, beside, add_step, reach=REACH):
    for step in range(-reach, reach + 1):
        value = moved(main, beside, step)
        yield step + REACH, value + float(step) if add_step and step else value


def wanted_keep(value, low, high, plane, step_z):
    if step_z == 0:
        return 1.0 - value
    lanes = lanes_like(value)
    if step_z < 0:
        beside = rolled(low(), -Z_UP[plane])
        value = jnp.where(lanes < -step_z, beside, rolled(value, -step_z))
    else:
        beside = rolled(high(), LANES - step_z - Z_DOWN[plane])
        value = jnp.where(lanes >= LANES - step_z, beside, rolled(value, -step_z))
    return 1.0 - value


def fill_outer(extent, count, edges, fields, x_low, x_high, shifts, besides):
    size_x, size_y, _ = extent
    height = shifts.shape[3]
    at = x_place(count, REACH, size_y)
    sides = ((x_low, size_x - REACH, -LANES // 2), (x_high, 0, LANES // 2))
    for side, (source, first, high_lanes) in enumerate(sides):
        pack = kept(edges[4 + side], source[at : at + height])
        for layer in range(REACH):
            for order, field in enumerate(fields):
                lane_of = (first + layer) * SLOT + field * REACH
                besides[order, side * REACH + layer] = beside_columns(
                    pack, pack, lane_of, high_lanes
                )
    for side, (source, _, _) in enumerate(sides):
        for layer in range(REACH):
            distance = REACH - layer if side == 0 else layer + 1
            low, high = x_span(distance, size_y)
            for order, field in enumerate(fields):
                start = x_place(field, distance, size_y)
                for step, value in each_shift(
                    kept(edges[4 + side], source[start : start + high - low]),
                    besides[order, side * REACH + layer, low:high],
                    field == 2, reach_beside(distance),
                ):
                    shifts[step, order, side * REACH + layer, low:high] = value


def weights_early_kernel(
    extent, edges, broken_in, stiffness, z_low, z_high, weights, keeps,
    shifts, planes, besides, broken, sems,
):
    size_x, size_y, _ = extent

    def layer_copy(layer):
        return pltpu.make_async_copy(broken_in.at[:, layer], broken.at[:, layer], sems.at[layer])

    for layer in range(size_x):
        layer_copy(layer).start()
    low_pack = kept(edges[0], z_low[0:size_y])
    high_pack = kept(edges[1], z_high[0:size_y])
    for layer in range(size_x):
        besides[layer] = beside_columns(low_pack, high_pack, layer * SLOT + 3 * REACH)
    for layer in range(size_x):
        for order, value in each_shift(stiffness[layer], besides[layer], False):
            shifts[order, layer, FIRST : FIRST + size_y] = value

    def fill(layer, carry):
        layer_copy(layer).wait()
        for plane in range(len(OFFSETS)):
            planes[plane, layer, FIRST : FIRST + size_y] = broken[plane, layer].astype(jnp.float32)
        return carry

    lax.fori_loop(0, size_x, fill, 0)
    for late, target in ((False, weights), (True, keeps)):
        for step, first, last, bonds, base in inner_plan(extent, late)[0]:

            def one_layer(layer, carry, step=step, first=first, bonds=bonds, base=base):
                slot = base + (layer - first) * len(bonds)
                far_layer = layer + step
                for order, (tile, step_y, step_z, plane, owner) in enumerate(bonds):
                    rows = slice(8 * tile, 8 * tile + 8)
                    far_rows = slice(FIRST + step_y + 8 * tile, FIRST + step_y + 8 * tile + 8)
                    if owner:
                        keep = 1.0 - broken[plane, layer, rows].astype(jnp.float32)
                    else:
                        at = size_y + far_layer * size_y + step_y + 8 * tile
                        keep = wanted_keep(
                            planes[plane, far_layer, far_rows],
                            lambda: z_low[pl.ds(at, 8)],
                            lambda: z_high[pl.ds(at, 8)],
                            plane, step_z,
                        )
                    keep = (0.5 * C_BOND) * keep
                    if not late:
                        far = shifts[step_z + REACH, far_layer, far_rows]
                        keep = jnp.where(far > 0.0, keep * (stiffness[layer, rows] + far), 0.0)
                    target[slot + order] = keep
                return carry

            lax.fori_loop(first, last, one_layer, 0)


def weights_late_kernel(
    extent, stiffness, wide, wide_pack, wide_broken, rows_low, rows_high, keeps, weights,
    shifts, besides,
):
    size_x, size_y, _ = extent
    for layer in range(size_x):
        besides[layer] = beside_columns(wide_pack[0], wide_pack[1], layer * SLOT + 3 * REACH)
    for layer in range(size_x):
        for order, value in each_shift(wide[0, layer], besides[layer], False):
            shifts[order, layer] = value
    for step, first, last, bonds, base in inner_plan(extent, True)[0]:

        def one_layer(layer, carry, step=step, first=first, bonds=bonds, base=base):
            slot = base + (layer - first) * len(bonds)
            far_layer = layer + step
            sublanes = lax.broadcasted_iota(jnp.int32, (8, LANES), 0)
            for order, (tile, step_y, step_z, plane, owner) in enumerate(bonds):
                rows = slice(8 * tile, 8 * tile + 8)
                far_rows = slice(REACH + step_y + 8 * tile, REACH + step_y + 8 * tile + 8)
                keep = keeps[slot + order]
                if not owner:
                    if step_y < 0:
                        at = PAD + Y_UP[plane] * size_x - far_layer * step_y
                        value = rows_low[pl.ds(at, 8)]
                        across = sublanes < -step_y
                    else:
                        at = PAD + Y_DOWN[plane] * size_x + far_layer * step_y + step_y - 8
                        value = rows_high[pl.ds(at, 8)]
                        across = sublanes >= 8 - step_y
                    halo = wanted_keep(
                        value,
                        lambda: wide_broken[0, far_layer, far_rows],
                        lambda: wide_broken[1, far_layer, far_rows],
                        plane, step_z,
                    )
                    keep = jnp.where(across, (0.5 * C_BOND) * halo, keep)
                far = shifts[step_z + REACH, far_layer, far_rows]
                weights[slot + order] = jnp.where(
                    far > 0.0, keep * (stiffness[layer, rows] + far), 0.0
                )
            return carry

        lax.fori_loop(first, last, one_layer, 0)


def weights_outer_kernel(
    extent, edges, stiffness, pore, wide, wide_pack, x_up, x_broken, x_far, x_near,
    weights, pressing, shifts, planes, besides,
):
    size_x, size_y, _ = extent
    height = wide.shape[2]
    pore_at = x_place(4, REACH, size_y) + height
    broken_at = pore_at + size_y
    rows_at = broken_at + 2 * NEAR * height
    x_low = Either(edges[6], x_near, x_far)
    x_high = Either(edges[6], x_far, x_near)
    fill_outer(extent, 4, edges, (3,), x_low, x_high, shifts, besides)
    for plane, (a, b, _) in enumerate(OFFSETS):
        for layer in range(a):
            at = (X_UP[plane] + layer) * size_y
            place = X_UP[plane] + layer
            planes[place, REACH : REACH + size_y] = x_broken[at : at + size_y]
            at = rows_at + XY_UP.get(plane, 0) + layer * abs(b)
            if b > 0:
                planes[place, REACH - b : REACH] = x_low[at : at + b]
            if b < 0:
                planes[place, REACH + size_y : REACH + size_y - b] = x_low[at : at - b]
    for step, first, last, bonds, base in outer_plan(extent)[0]:
        for layer in range(first, last):
            slot = base + (layer - first) * len(bonds)
            far_layer = layer + step
            far_layer = far_layer + REACH if far_layer < 0 else far_layer - size_x + REACH
            for order, (tile, step_y, step_z, plane, owner) in enumerate(bonds):
                rows = slice(8 * tile, 8 * tile + 8)
                far_rows = slice(REACH + step_y + 8 * tile, REACH + step_y + 8 * tile + 8)
                far = shifts[step_z + REACH, 0, far_layer, far_rows]
                if owner:
                    at = (X_UP[plane] + layer - first) * size_y + 8 * tile
                    keep = 1.0 - x_up[at : at + 8]
                else:
                    low_at = broken_at + (far_layer + NEAR - REACH) * height
                    high_at = low_at + NEAR * height
                    keep = wanted_keep(
                        planes[X_UP[plane] + layer, far_rows],
                        lambda: x_low[far_rows.start + low_at : far_rows.stop + low_at],
                        lambda: x_low[far_rows.start + high_at : far_rows.stop + high_at],
                        plane, step_z,
                    )
                value = keep * (0.5 * C_BOND) * (stiffness[layer, rows] + far)
                weights[slot + order] = jnp.where(far > 0.0, value, 0.0)

    middle = slice(REACH, REACH + size_y)

    def wide_field(field, layer):
        if layer < 0 or layer >= size_x:
            source = x_low if layer < 0 else x_high
            at = x_place(field, 1, size_y) + reach_beside(1) if field == 3 else pore_at
            return kept(edges[4 if layer < 0 else 5], source[at : at + size_y])
        return wide[field - 3, layer, middle]

    for layer in range(size_x):
        own = pore[layer]
        for axis in range(3):
            total = jnp.zeros((size_y, LANES), jnp.float32)
            for sign in (1, -1):
                if axis == 0:
                    inside = wide_field(3, layer + sign)
                    level = wide_field(4, layer + sign)
                elif axis == 1:
                    rows = slice(REACH + sign, REACH + sign + size_y)
                    inside = wide[0, layer, rows]
                    level = wide[1, layer, rows]
                else:
                    inside, level = (
                        moved(
                            wide[field - 3, layer],
                            beside_columns(
                                wide_pack[0], wide_pack[1], layer * SLOT + field * REACH
                            ),
                            sign,
                        )[middle]
                        for field in (3, 4)
                    )
                total = total + jnp.where(inside > 0.0, (-0.5 * sign) * (level - own), 0.0)
            pressing[axis, layer] = total


def add_bonds(bonds, step, layer, far_layer, first_row, motion, shifts, weights, slot, total):
    for tile in sorted({bond[0] for bond in bonds}):
        rows = slice(8 * tile, 8 * tile + 8)
        own = [motion[axis, layer, rows] for axis in range(3)]
        near_x = own[0] - float(step)
        near_y = {step_y: own[1] - float(step_y) for step_y in range(-REACH, REACH + 1)}
        force = [total[axis, layer, rows] for axis in range(3)]
        for order, (bond_tile, step_y, step_z, plane, _) in enumerate(bonds):
            if bond_tile != tile:
                continue
            far_rows = slice(first_row + step_y + 8 * tile, first_row + step_y + 8 * tile + 8)
            far = [shifts[step_z + REACH, axis, far_layer, far_rows] for axis in range(3)]
            radial = [far[0] - near_x, far[1] - near_y[step_y], far[2] - own[2]]
            square = radial[0] * radial[0] + radial[1] * radial[1] + radial[2] * radial[2]
            rest = math.sqrt(sum(part * part for part in OFFSETS[plane]))
            factor = weights[slot + order] * (1.0 / rest - lax.rsqrt(square))
            force = [force[axis] + factor * radial[axis] for axis in range(3)]
        for axis in range(3):
            total[axis, layer, rows] = force[axis]


def add_inner(extent, late, fill, motion, shifts, weights, total):
    lax.fori_loop(0, extent[0], fill, 0, unroll=UNROLL_FILL)
    for step, first, last, bonds, base in inner_plan(extent, late)[0]:
        if not bonds:
            continue

        def one_layer(layer, carry, step=step, first=first, bonds=bonds, base=base):
            slot = base + (layer - first) * len(bonds)
            add_bonds(bonds, step, layer, layer + step, FIRST, motion, shifts, weights, slot, total)
            return carry

        lax.fori_loop(first, last, one_layer, 0, unroll=UNROLL if last - first > 1 else 1)


def force_early_kernel(extent, edges, motion, z_low, z_high, weights, total, shifts, besides):
    size_x, size_y, _ = extent
    total[...] = jnp.zeros(total.shape, jnp.float32)
    low_pack = kept(edges[0], z_low[0:size_y])
    high_pack = kept(edges[1], z_high[0:size_y])
    for layer in range(size_x):
        for axis in range(3):
            besides[axis, layer] = beside_columns(
                low_pack, high_pack, layer * SLOT + axis * REACH
            )

    def fill(layer, carry):
        for axis in range(3):
            for order, value in each_shift(motion[axis, layer], besides[axis, layer], axis == 2):
                shifts[order, axis, layer, FIRST : FIRST + size_y] = value
        return carry

    add_inner(extent, False, fill, motion, shifts, weights, total)


def force_late_kernel(
    extent, count, edges, motion, early, early_shifts, y_low, y_high, weights,
    total, shifts, halo, besides,
):
    size_x, size_y, _ = extent
    total[...] = early[...]
    middle = slice(FIRST, FIRST + size_y)
    above = FIRST + size_y

    def across(place, at):
        halo[place, 0:REACH] = kept(edges[3], y_high[at : at + REACH])
        halo[place, REACH : 8 - REACH] = jnp.zeros((8 - 2 * REACH, LANES), jnp.float32)
        halo[place, 8 - REACH : 8] = kept(edges[2], y_low[at : at + REACH])

    packs = 3 * size_x
    for order in range(2):
        across(packs + order, (count * size_x + order) * REACH)
    for place in range(3 * size_x):
        across(place, place * REACH)
    low_pack, high_pack = halo[packs], halo[packs + 1]
    for layer in range(size_x):
        for axis in range(3):
            besides[axis * size_x + layer] = beside_columns(
                low_pack, high_pack, layer * SLOT + axis * REACH
            )

    def fill(layer, carry):
        for axis in range(3):
            place = axis * size_x + layer
            for order, value in each_shift(halo[place], besides[place], axis == 2):
                shifts[order, axis, layer, middle] = early_shifts[order, axis, layer, middle]
                shifts[order, axis, layer, FIRST - REACH : FIRST] = value[8 - REACH : 8]
                shifts[order, axis, layer, above : above + REACH] = value[0:REACH]
        return carry

    add_inner(extent, True, fill, motion, shifts, weights, total)


def finish_kernel(
    extent, count, stage, edges, motion, speed, pressing, inner, weights, x_far, x_near, *refs
):
    size_x, size_y, _ = extent
    if stage == "last":
        motion_out, speed_out, accel_out, total, shifts, besides = refs
    else:
        motion_out, speed_out, z_up, z_down, total, shifts, besides = refs
    total[...] = inner[...] + pressing[...]
    x_low = Either(edges[6], x_near, x_far)
    x_high = Either(edges[6], x_far, x_near)
    fill_outer(extent, count, edges, range(3), x_low, x_high, shifts, besides)
    for step, first, last, bonds, base in outer_plan(extent)[0]:
        for layer in range(first, last):
            slot = base + (layer - first) * len(bonds)
            far_layer = layer + step + (REACH if step < 0 else REACH - size_x)
            add_bonds(bonds, step, layer, far_layer, REACH, motion, shifts, weights, slot, total)
    accel = total[...]
    new_speed = speed[...] + HALF_DT * accel
    if stage == "last":
        motion_out[...] = motion[...]
        speed_out[...] = new_speed
        accel_out[...] = accel
        return
    if stage == "middle":
        new_speed = new_speed + HALF_DT * accel
    speed_out[...] = new_speed
    motion_out[...] = motion[...] + DT_STEP * new_speed
    up, down = pack_columns(lambda axis, layer: motion_out[axis, layer], 3, size_x, size_y)
    z_up[...] = up
    z_down[...] = down


VMEM = pl.BlockSpec(memory_space=pltpu.VMEM)
SMEM = pl.BlockSpec(memory_space=pltpu.SMEM)


def call(kernel, scalars, operands, shapes, scratch=(), name=None, results=(), far=()):
    operands = [pltpu.with_memory_space_constraint(operand, pltpu.HBM) for operand in far] + [
        pltpu.with_memory_space_constraint(operand, pltpu.VMEM) for operand in operands
    ]
    return pl.pallas_call(
        kernel,
        out_shape=[
            jax.ShapeDtypeStruct(shape, jnp.float32)
            if place in results
            else pltpu.VMEM(shape, jnp.float32)
            for place, shape in enumerate(shapes)
        ],
        in_specs=[SMEM] * len(scalars)
        + [pl.BlockSpec(memory_space=pltpu.HBM)] * len(far)
        + [VMEM] * (len(operands) - len(far)),
        out_specs=[VMEM] * len(shapes),
        scratch_shapes=[
            pltpu.VMEM(item, jnp.float32) if isinstance(item, tuple) else item for item in scratch
        ],
        compiler_params=pltpu.CompilerParams(vmem_limit_bytes=24 * 1024 * 1024),
        name=name,
    )(*scalars, *operands)


def sent(value, axis, distance):
    count = lax.axis_size(axis)
    return lax.ppermute(value, axis, [(i, (i + distance) % count) for i in range(count)])


def swapped(near, far):
    count = lax.axis_size("gx")
    side = [1 - 2 * (i % 2) for i in range(count)]
    far = lax.ppermute(far, "gx", [(i, (i - side[i]) % count) for i in range(count)])
    return lax.ppermute(near, "gx", [(i, i + side[i]) for i in range(count)]), far


def on_device(displacement, velocity, stiffness, broken, borehole_id, flags, pressure):
    extent = stiffness.shape
    size_x, size_y, _ = extent
    height = size_y + 8
    tall = size_y + 2 * FIRST
    edges = jnp.stack(
        [
            end
            for axis in ("gz", "gy", "gx")
            for end in (
                (lax.axis_index(axis) > 0).astype(jnp.int32),
                (lax.axis_index(axis) < lax.axis_size(axis) - 1).astype(jnp.int32),
            )
        ]
        + [lax.axis_index("gx") % 2]
    )
    field = (size_x, size_y, LANES)
    vector = (3,) + field
    part = functools.partial

    pack = (size_y + size_x * size_y + PAD, LANES)
    rows_shapes = [(count * size_x + 2 * PAD, LANES) for count in (Y_UP_COUNT, Y_DOWN_COUNT)]
    layers_shape = (X_UP_COUNT * size_y, LANES)
    motion, stiffness, pore, z_up, z_down, rows_up, rows_down, x_up = pl.pallas_call(
        part(start_kernel, extent),
        out_shape=[
            pltpu.VMEM(shape, kind)
            for shape, kind in (
                (vector, jnp.float32), (field, jnp.float32),
                (field, jnp.float32), (pack, jnp.float32), (pack, jnp.float32),
                (rows_shapes[0], jnp.float32), (rows_shapes[1], jnp.float32),
                (layers_shape, jnp.float32),
            )
        ],
        in_specs=[pl.BlockSpec(memory_space=pltpu.HBM)] * 6,
        out_specs=[VMEM] * 8,
        scratch_shapes=[
            pltpu.VMEM(broken.shape, jnp.int32),
            pltpu.SMEM(pressure.shape, jnp.float32),
            pltpu.VMEM(field, jnp.int32),
            pltpu.VMEM(field, jnp.int32),
            pltpu.SemaphoreType.DMA((5,)),
            pltpu.SemaphoreType.DMA((size_x,)),
        ],
        compiler_params=pltpu.CompilerParams(vmem_limit_bytes=24 * 1024 * 1024),
        name="start",
    )(
        *(
            pltpu.with_memory_space_constraint(operand, pltpu.HBM)
            for operand in (pressure, displacement, stiffness, borehole_id, flags, broken)
        )
    )
    z_low = sent(z_up, "gz", 1)
    z_high = sent(z_down, "gz", -1)
    rows_low = sent(rows_up, "gy", 1)
    rows_high = sent(rows_down, "gy", -1)
    x_broken = sent(x_up, "gx", 1)
    rows = (round_up(5 * size_x * REACH + 2 * REACH + 2 * size_x * REACH), LANES)
    y_up, y_down = call(
        part(y_rows_first_kernel, extent), [edges],
        [motion, stiffness, pore, z_low, z_high], [rows, rows], name="y_rows_first",
    )
    y_low = sent(y_up, "gy", 1)
    y_high = sent(y_down, "gy", -1)
    moves = 2 * REACH + 1
    early_slots = inner_plan(extent, False)[1]
    late_slots = inner_plan(extent, True)[1]
    outer_slots = outer_plan(extent)[1]
    weights_early, keeps = call(
        part(weights_early_kernel, extent), [edges], [stiffness, z_low, z_high],
        [(early_slots, 8, LANES), (late_slots, 8, LANES)],
        [
            (moves, size_x, tall, LANES),
            (len(OFFSETS), size_x, tall, LANES),
            field,
            pltpu.VMEM(broken.shape, jnp.int32),
            pltpu.SemaphoreType.DMA((size_x,)),
        ], name="weights_early", far=[broken],
    )

    def force_early(motion, z_low, z_high):
        return call(
            part(force_early_kernel, extent), [edges], [motion, z_low, z_high, weights_early],
            [vector, (moves, 3, size_x, tall, LANES)], [vector], name="force_early",
        )

    def force_late(count, motion, early, early_shifts, y_low, y_high):
        return call(
            part(force_late_kernel, extent, count), [edges],
            [motion, early, early_shifts, y_low, y_high, weights_late], [vector],
            [(moves, 3, size_x, tall, LANES), (2 + 3 * size_x, 8, LANES), (3 * size_x, 8, LANES)], name="force_late",
        )[0]

    early, early_shifts = force_early(motion, z_low, z_high)
    y_low, y_high, x_broken, early = lax.optimization_barrier((y_low, y_high, x_broken, early))
    layers = x_place(4, REACH, size_y) + height + size_y
    layers = round_up(layers + 2 * NEAR * height + XY_UP_COUNT)
    wide_static, wide_pack, wide_broken, x_near, x_far = call(
        part(x_layers_first_kernel, extent), [edges],
        [motion, stiffness, pore, z_low, z_high, y_low, y_high, rows_low, rows_high],
        [
            (2, size_x, height, LANES),
            (2, height, LANES),
            (2, size_x, height, LANES),
            (layers, LANES),
            (layers, LANES),
        ], [(3, size_x, height, LANES)], name="x_layers_first",
    )
    x_near, x_far = swapped(x_near, x_far)
    (weights_late,) = call(
        part(weights_late_kernel, extent), [],
        [stiffness, wide_static, wide_pack, wide_broken, rows_low, rows_high, keeps],
        [(late_slots, 8, LANES)],
        [(moves, size_x, height, LANES), (size_x, height, LANES)], name="weights_late",
    )
    inner = force_late(5, motion, early, early_shifts, y_low, y_high)
    outer_weights, pressing = call(
        part(weights_outer_kernel, extent), [edges],
        [stiffness, pore, wide_static, wide_pack, x_up, x_broken, x_far, x_near],
        [(outer_slots, 8, LANES), vector],
        [
            (moves, 1, 2 * REACH, height, LANES),
            (X_UP_COUNT, height, LANES),
            (1, 2 * REACH, height, LANES),
        ], name="weights_outer",
    )

    def finish(stage, count, motion, speed, inner, x_near, x_far):
        columns = (size_y, LANES)
        shapes = [vector] * 3 if stage == "last" else [vector, vector, columns, columns]
        return call(
            part(finish_kernel, extent, count, stage), [edges],
            [motion, speed, pressing, inner, outer_weights, x_far, x_near],
            shapes,
            [
                vector,
                (moves, 3, 2 * REACH, height, LANES),
                (3, 2 * REACH, height, LANES),
            ], name="finish_" + stage,
            results=(0, 1, 2) if stage == "last" else (),
        )

    motion, speed, z_up, z_down = finish(
        "first", 4, motion, velocity, inner, x_near, x_far
    )
    for step_index in range(STEPS):
        z_low = sent(z_up, "gz", 1)
        z_high = sent(z_down, "gz", -1)
        rows = (round_up(3 * size_x * REACH + 2 * REACH), LANES)
        y_up, y_down = call(
            part(y_rows_kernel, extent), [edges], [motion, z_low, z_high], [rows, rows],
            name="y_rows",
        )
        y_low = sent(y_up, "gy", 1)
        y_high = sent(y_down, "gy", -1)
        early, early_shifts = force_early(motion, z_low, z_high)
        y_low, y_high, early = lax.optimization_barrier((y_low, y_high, early))
        layers = round_up(x_place(3, REACH, size_y) + height)
        x_near, x_far = call(
            part(x_layers_kernel, extent), [edges],
            [motion, z_low, z_high, y_low, y_high],
            [(layers, LANES), (layers, LANES)],
            [(3, size_x, height, LANES), (2, height, LANES)], name="x_layers",
        )
        x_near, x_far = swapped(x_near, x_far)
        inner = force_late(3, motion, early, early_shifts, y_low, y_high)
        if step_index < STEPS - 1:
            motion, speed, z_up, z_down = finish("middle", 3, motion, speed, inner, x_near, x_far)
        else:
            motion, speed, accel = finish("last", 3, motion, speed, inner, x_near, x_far)
    return (motion, speed, accel)


def solution(mesh):
    in_specs = (
        P(None, "gx", "gy", "gz"),
        P(None, "gx", "gy", "gz"),
        P("gx", "gy", "gz"),
        P(None, "gx", "gy", "gz"),
        P("gx", "gy", "gz"),
        P("gx", "gy", "gz"),
        P(),
    )
    out_specs = (P(None, "gx", "gy", "gz"), P(None, "gx", "gy", "gz"), P(None, "gx", "gy", "gz"))
    return jax.shard_map(
        on_device, mesh=mesh, in_specs=in_specs, out_specs=out_specs, check_vma=False
    )
```

```python
import functools
import math

import jax
import jax.numpy as jnp
from jax import lax
from jax.experimental import pallas as pl
from jax.experimental.pallas import tpu as pltpu
from jax.sharding import PartitionSpec as P

STEPS = 2
C_BOND = 3.0
DT_STEP = 0.04
REACH = 3
NEAR = 2
LANES = 128
SLOT = 16
PAD = 8
UNROLL = 2
UNROLL_FILL = 2
FIRST = 8
HALF_DT = 0.5 * DT_STEP


def half_offsets():
    result = []
    for step_x in range(0, 4):
        for step_y in range(-3, 4):
            for step_z in range(-3, 4):
                square = step_x * step_x + step_y * step_y + step_z * step_z
                if square == 0 or square > 9:
                    continue
                if step_x > 0 or (step_x == 0 and (step_y > 0 or (step_y == 0 and step_z > 0))):
                    result.append((step_x, step_y, step_z))
    return result


OFFSETS = half_offsets()
BONDS = {step: [] for step in range(-REACH, REACH + 1)}
for _plane, (_a, _b, _c) in enumerate(OFFSETS):
    BONDS[_a].append((_b, _c, _plane, True))
    BONDS[-_a].append((-_b, -_c, _plane, False))


def inner_layers(step, extent):
    return max(0, -step), min(extent, extent - step)


def outer_layers(step, extent):
    return (extent - step, extent) if step > 0 else (0, -step)


STEPS_ALL = list(range(-REACH, REACH + 1))
STEPS_OUT = [step for step in STEPS_ALL if step != 0]


def tiled_bonds(step, tiles):
    early, late = [], []
    for tile in range(tiles):
        for bond in BONDS[step]:
            low, high = 8 * tile + bond[0], 8 * tile + 8 + bond[0]
            (early if low >= 0 and high <= 8 * tiles else late).append((tile, *bond))
    return early, late


def inner_plan(extent, late):
    plan, total = [], 0
    for step in STEPS_ALL:
        bonds = tiled_bonds(step, extent[1] // 8)[int(late)]
        first, last = inner_layers(step, extent[0])
        plan.append((step, first, last, bonds, total))
        total += (last - first) * len(bonds)
    return plan, total


def outer_plan(extent):
    plan, total = [], 0
    for step in STEPS_OUT:
        bonds = [(tile, *bond) for tile in range(extent[1] // 8) for bond in BONDS[step]]
        first, last = outer_layers(step, extent[0])
        plan.append((step, first, last, bonds, total))
        total += (last - first) * len(bonds)
    return plan, total


def reach_beside(distance):
    return max(max(abs(b), abs(c)) for a, b, c in OFFSETS if a >= distance)


def x_span(distance, size_y):
    return REACH - reach_beside(distance), REACH + size_y + reach_beside(distance)


def x_place(field, distance, size_y):
    lengths = [high - low for low, high in (x_span(far, size_y) for far in (3, 2, 1))]
    return field * sum(lengths) + sum(lengths[: REACH - distance])


def round_up(count):
    return (count + 7) // 8 * 8


def running(amounts):
    places, total = {}, 0
    for plane, amount in amounts:
        places[plane] = total
        total += amount
    return places, total


Z_UP, Z_UP_COUNT = running([(k, c) for k, (a, b, c) in enumerate(OFFSETS) if c > 0])
Z_DOWN, Z_DOWN_COUNT = running([(k, -c) for k, (a, b, c) in enumerate(OFFSETS) if c < 0])
Y_UP, Y_UP_COUNT = running([(k, b) for k, (a, b, c) in enumerate(OFFSETS) if b > 0])
Y_DOWN, Y_DOWN_COUNT = running([(k, -b) for k, (a, b, c) in enumerate(OFFSETS) if b < 0])
X_UP, X_UP_COUNT = running([(k, a) for k, (a, b, c) in enumerate(OFFSETS) if a > 0])
XY_UP, XY_UP_COUNT = running([(k, a * abs(b)) for k, (a, b, c) in enumerate(OFFSETS) if a * abs(b) > 0])


def lanes_like(value):
    return lax.broadcasted_iota(jnp.int32, value.shape, value.ndim - 1)


def rolled(value, shift):
    shift = shift % LANES
    return value if shift == 0 else pltpu.roll(value, shift, value.ndim - 1)


def beside_columns(low_pack, high_pack, lane_of, high_lanes=0):
    lanes = lanes_like(low_pack)
    return jnp.where(
        lanes < REACH,
        rolled(high_pack, -lane_of - high_lanes),
        rolled(low_pack, LANES - REACH - lane_of),
    )


def moved(main, beside, step):
    if step == 0:
        return main
    lanes = lanes_like(main)
    if step > 0:
        return rolled(jnp.where(lanes < step, beside, main), -step)
    return rolled(jnp.where(lanes >= LANES + step, beside, main), -step)


def pack_columns(field_of, count, extent, height):
    lanes = lax.broadcasted_iota(jnp.int32, (height, LANES), 1)
    up = jnp.zeros((height, LANES), jnp.float32)
    down = up
    for layer in range(extent):
        for field in range(count):
            lane_of = layer * SLOT + field * REACH
            value = field_of(field, layer)
            here = (lanes >= lane_of) & (lanes < lane_of + REACH)
            up = jnp.where(here, rolled(value, lane_of - (LANES - REACH)), up)
            down = jnp.where(here, rolled(value, lane_of), down)
    return up, down


class Either:
    def __init__(self, odd, if_odd, if_even):
        self.odd, self.if_odd, self.if_even = odd, if_odd, if_even

    def __getitem__(self, rows):
        return jnp.where(self.odd > 0, self.if_odd[rows], self.if_even[rows])


def by_parity(odd, near, far, write):
    @pl.when(odd > 0)
    def _():
        write(far, near)

    @pl.when(odd == 0)
    def _():
        write(near, far)


def kept(flag, value):
    return jnp.where(flag > 0, value, 0.0)


def start_kernel(
    extent, pressure_in, motion_in, stiffness_in, borehole_in, flags_in, broken_in,
    motion, stiffness, pore, z_up, z_down, rows_up, rows_down, x_up,
    broken, pressure, borehole, flags, field_sems, layer_sems,
):
    size_x, size_y, _ = extent
    pairs = (
        (pressure_in, pressure), (borehole_in, borehole), (flags_in, flags),
        (motion_in, motion), (stiffness_in, stiffness),
    )
    copies = [
        pltpu.make_async_copy(source, target, field_sems.at[place])
        for place, (source, target) in enumerate(pairs)
    ]

    def layer_copy(layer):
        return pltpu.make_async_copy(
            broken_in.at[:, layer], broken.at[:, layer], layer_sems.at[layer]
        )

    for copy in copies:
        copy.start()
    for layer in range(size_x):
        layer_copy(layer).start()
    for copy in copies:
        copy.wait()
    ids = borehole[...]
    level = jnp.zeros(ids.shape, jnp.float32)
    for label in range(pressure.shape[0]):
        level = jnp.where(ids == label, pressure[label], level)
    pore[...] = flags[...].astype(jnp.float32) * level

    def field_of(field, layer):
        if field < 3:
            return motion[field, layer]
        return stiffness[layer] if field == 3 else pore[layer]

    up, down = pack_columns(field_of, 5, size_x, size_y)
    z_up[0:size_y] = up
    z_down[0:size_y] = down

    def one_layer(layer, carry):
        layer_copy(layer).wait()
        lanes = lax.broadcasted_iota(jnp.int32, (size_y, LANES), 1)
        rows = pl.ds(size_y + layer * size_y, size_y)
        up = jnp.zeros((size_y, LANES), jnp.float32)
        down = up
        for plane, (_, _, c) in enumerate(OFFSETS):
            if c > 0:
                at = Z_UP[plane]
                value = broken[plane, layer].astype(jnp.float32)
                up = jnp.where((lanes >= at) & (lanes < at + c), rolled(value, at + c), up)
            if c < 0:
                at = Z_DOWN[plane]
                value = broken[plane, layer].astype(jnp.float32)
                down = jnp.where((lanes >= at) & (lanes < at - c), rolled(value, at), down)
        z_up[rows] = up
        z_down[rows] = down
        return carry

    lax.fori_loop(0, size_x, one_layer, 0)
    for plane, (a, _, _) in enumerate(OFFSETS):
        for layer in range(a):
            at = (X_UP[plane] + layer) * size_y
            x_up[at : at + size_y] = broken[plane, size_x - a + layer].astype(jnp.float32)
    for plane, (_, b, _) in enumerate(OFFSETS):
        for layer in range(size_x):
            if b > 0:
                at = PAD + Y_UP[plane] * size_x + layer * b
                rows_up[at : at + b] = broken[plane, layer, size_y - b : size_y].astype(jnp.float32)
            if b < 0:
                at = PAD + Y_DOWN[plane] * size_x - layer * b
                rows_down[at : at - b] = broken[plane, layer, 0:-b].astype(jnp.float32)


def copy_y_rows(field_of, count, extent, low_pack, high_pack, y_up, y_down):
    size_x, size_y, _ = extent
    for field in range(count):
        for layer in range(size_x):
            at = (field * size_x + layer) * REACH
            y_up[at : at + REACH] = field_of(field, layer, slice(size_y - REACH, size_y))
            y_down[at : at + REACH] = field_of(field, layer, slice(0, REACH))
    at = count * size_x * REACH
    for pack in (low_pack, high_pack):
        y_up[at : at + REACH] = pack[size_y - REACH : size_y]
        y_down[at : at + REACH] = pack[0:REACH]
        at += REACH
    return at


def y_rows_kernel(extent, edges, motion, z_low, z_high, y_up, y_down):
    size_y = extent[1]
    low_pack = kept(edges[0], z_low[0:size_y])
    high_pack = kept(edges[1], z_high[0:size_y])
    copy_y_rows(
        lambda field, layer, rows: motion[field, layer, rows],
        3, extent, low_pack, high_pack, y_up, y_down,
    )


def y_rows_first_kernel(extent, edges, motion, stiffness, pore, z_low, z_high, y_up, y_down):
    size_x, size_y, _ = extent
    low_pack = kept(edges[0], z_low[0:size_y])
    high_pack = kept(edges[1], z_high[0:size_y])

    def field_of(field, layer, rows):
        if field < 3:
            return motion[field, layer, rows]
        return stiffness[layer, rows] if field == 3 else pore[layer, rows]

    base = copy_y_rows(field_of, 5, extent, low_pack, high_pack, y_up, y_down)
    for order, pack in enumerate((z_low, z_high)):
        for layer in range(size_x):
            first = size_y + layer * size_y
            at = base + (order * size_x + layer) * REACH
            y_up[at : at + REACH] = pack[first + size_y - REACH : first + size_y]
            y_down[at : at + REACH] = pack[first : first + REACH]


def widen(target, low_rows, middle, high_rows):
    size_y = middle.shape[0]
    target[0:REACH] = low_rows
    target[REACH : REACH + size_y] = middle
    target[REACH + size_y : 2 * REACH + size_y] = high_rows
    height = target.shape[0]
    target[2 * REACH + size_y : height] = jnp.zeros((height - 2 * REACH - size_y, LANES), jnp.float32)


def widen_fields(edges, field_of, count, extent, z_low, z_high, y_low, y_high, target, wide_pack):
    size_x, size_y, _ = extent
    for field in range(count):
        for layer in range(size_x):
            at = (field * size_x + layer) * REACH
            widen(
                target(field).at[layer],
                kept(edges[2], y_low[at : at + REACH]),
                field_of(field, layer),
                kept(edges[3], y_high[at : at + REACH]),
            )
    at = count * size_x * REACH
    for order, pack in enumerate((z_low, z_high)):
        widen(
            wide_pack.at[order],
            kept(edges[2], y_low[at : at + REACH]),
            kept(edges[order], pack[0:size_y]),
            kept(edges[3], y_high[at : at + REACH]),
        )
        at += REACH
    return at


def copy_x_layers(count, extent, target, wide_pack, x_up, x_down):
    size_x, size_y, _ = extent
    height = wide_pack.shape[1]
    for field in range(count):
        for distance in (3, 2, 1):
            low, high = x_span(distance, size_y)
            at = x_place(field, distance, size_y)
            x_up[at : at + high - low] = target(field)[size_x - distance, low:high]
            x_down[at : at + high - low] = target(field)[distance - 1, low:high]
    at = x_place(count, REACH, size_y)
    low_pack, high_pack = wide_pack[0], wide_pack[1]
    half = lanes_like(low_pack) < LANES // 2
    other = rolled(high_pack, LANES // 2)
    x_up[at : at + height] = jnp.where(half, other, low_pack)
    x_down[at : at + height] = jnp.where(half, low_pack, other)
    return at + height


def x_layers_kernel(
    extent, edges, motion, z_low, z_high, y_low, y_high, x_near, x_far, wide, wide_pack
):
    widen_fields(
        edges, lambda field, layer: motion[field, layer],
        3, extent, z_low, z_high, y_low, y_high, lambda field: wide.at[field], wide_pack,
    )

    def write(x_up, x_down):
        copy_x_layers(3, extent, lambda field: wide.at[field], wide_pack, x_up, x_down)

    by_parity(edges[6], x_near, x_far, write)


def x_layers_first_kernel(
    extent, edges, motion, stiffness, pore, z_low, z_high, y_low, y_high, rows_low, rows_high,
    wide_static, wide_pack, wide_broken, x_near, x_far, wide,
):
    size_x, size_y, _ = extent

    def field_of(field, layer):
        if field < 3:
            return motion[field, layer]
        return stiffness[layer] if field == 3 else pore[layer]

    def target(field):
        return wide.at[field] if field < 3 else wide_static.at[field - 3]

    base = widen_fields(
        edges, field_of, 5, extent, z_low, z_high, y_low, y_high, target, wide_pack
    )
    for order, pack in enumerate((z_low, z_high)):
        for layer in range(size_x):
            first = size_y + layer * size_y
            at = base + (order * size_x + layer) * REACH
            widen(
                wide_broken.at[order, layer],
                y_low[at : at + REACH],
                pack[first : first + size_y],
                y_high[at : at + REACH],
            )

    def write(x_up, x_down):
        at = copy_x_layers(4, extent, target, wide_pack, x_up, x_down)
        height = wide.shape[2]
        x_up[at : at + size_y] = pore[size_x - 1]
        x_down[at : at + size_y] = pore[0]
        at += size_y
        for order in range(2):
            for layer in range(NEAR):
                x_up[at : at + height] = wide_broken[order, size_x - NEAR + layer]
                at += height
        for plane, (a, b, _) in enumerate(OFFSETS):
            if a * b == 0:
                continue
            rows, many = abs(b), a * abs(b)
            source = rows_low if b > 0 else rows_high
            first = PAD + (Y_UP if b > 0 else Y_DOWN)[plane] * size_x + (size_x - a) * rows
            x_up[at + XY_UP[plane] : at + XY_UP[plane] + many] = source[first : first + many]

    by_parity(edges[6], x_near, x_far, write)


def each_shift(main, beside, add_step, reach=REACH):
    for step in range(-reach, reach + 1):
        value = moved(main, beside, step)
        yield step + REACH, value + float(step) if add_step and step else value


def wanted_keep(value, low, high, plane, step_z):
    if step_z == 0:
        return 1.0 - value
    lanes = lanes_like(value)
    if step_z < 0:
        beside = rolled(low(), -Z_UP[plane])
        value = jnp.where(lanes < -step_z, beside, rolled(value, -step_z))
    else:
        beside = rolled(high(), LANES - step_z - Z_DOWN[plane])
        value = jnp.where(lanes >= LANES - step_z, beside, rolled(value, -step_z))
    return 1.0 - value


def fill_outer(extent, count, edges, fields, x_low, x_high, shifts, besides):
    size_x, size_y, _ = extent
    height = shifts.shape[3]
    at = x_place(count, REACH, size_y)
    sides = ((x_low, size_x - REACH, -LANES // 2), (x_high, 0, LANES // 2))
    for side, (source, first, high_lanes) in enumerate(sides):
        pack = kept(edges[4 + side], source[at : at + height])
        for layer in range(REACH):
            for order, field in enumerate(fields):
                lane_of = (first + layer) * SLOT + field * REACH
                besides[order, side * REACH + layer] = beside_columns(
                    pack, pack, lane_of, high_lanes
                )
    for side, (source, _, _) in enumerate(sides):
        for layer in range(REACH):
            distance = REACH - layer if side == 0 else layer + 1
            low, high = x_span(distance, size_y)
            for order, field in enumerate(fields):
                start = x_place(field, distance, size_y)
                for step, value in each_shift(
                    kept(edges[4 + side], source[start : start + high - low]),
                    besides[order, side * REACH + layer, low:high],
                    field == 2, reach_beside(distance),
                ):
                    shifts[step, order, side * REACH + layer, low:high] = value


def weights_early_kernel(
    extent, edges, broken_in, stiffness, z_low, z_high, weights, keeps,
    shifts, planes, besides, broken, sems,
):
    size_x, size_y, _ = extent

    def layer_copy(layer):
        return pltpu.make_async_copy(broken_in.at[:, layer], broken.at[:, layer], sems.at[layer])

    for layer in range(size_x):
        layer_copy(layer).start()
    low_pack = kept(edges[0], z_low[0:size_y])
    high_pack = kept(edges[1], z_high[0:size_y])
    for layer in range(size_x):
        besides[layer] = beside_columns(low_pack, high_pack, layer * SLOT + 3 * REACH)
    for layer in range(size_x):
        for order, value in each_shift(stiffness[layer], besides[layer], False):
            shifts[order, layer, FIRST : FIRST + size_y] = value

    def fill(layer, carry):
        layer_copy(layer).wait()
        for plane in range(len(OFFSETS)):
            planes[plane, layer, FIRST : FIRST + size_y] = broken[plane, layer].astype(jnp.float32)
        return carry

    lax.fori_loop(0, size_x, fill, 0)
    for late, target in ((False, weights), (True, keeps)):
        for step, first, last, bonds, base in inner_plan(extent, late)[0]:

            def one_layer(layer, carry, step=step, first=first, bonds=bonds, base=base):
                slot = base + (layer - first) * len(bonds)
                far_layer = layer + step
                for order, (tile, step_y, step_z, plane, owner) in enumerate(bonds):
                    rows = slice(8 * tile, 8 * tile + 8)
                    far_rows = slice(FIRST + step_y + 8 * tile, FIRST + step_y + 8 * tile + 8)
                    if owner:
                        keep = 1.0 - broken[plane, layer, rows].astype(jnp.float32)
                    else:
                        at = size_y + far_layer * size_y + step_y + 8 * tile
                        keep = wanted_keep(
                            planes[plane, far_layer, far_rows],
                            lambda: z_low[pl.ds(at, 8)],
                            lambda: z_high[pl.ds(at, 8)],
                            plane, step_z,
                        )
                    keep = (0.5 * C_BOND) * keep
                    if not late:
                        far = shifts[step_z + REACH, far_layer, far_rows]
                        keep = jnp.where(far > 0.0, keep * (stiffness[layer, rows] + far), 0.0)
                    target[slot + order] = keep
                return carry

            lax.fori_loop(first, last, one_layer, 0)


def pressed(inside, level, own, sign):
    return jnp.where(inside > 0.0, (-0.5 * sign) * (level - own), 0.0)


def weights_late_kernel(
    extent, stiffness, pore, wide, wide_pack, wide_broken, rows_low, rows_high, keeps,
    weights, pressing, shifts, besides,
):
    size_x, size_y, _ = extent
    middle = slice(REACH, REACH + size_y)
    for layer in range(size_x):
        own = pore[layer]
        besides_z = [
            beside_columns(wide_pack[0, middle], wide_pack[1, middle], layer * SLOT + field * REACH)
            for field in (3, 4)
        ]
        total = [jnp.zeros((size_y, LANES), jnp.float32) for axis in range(3)]
        for sign in (1, -1):
            if 0 <= layer + sign < size_x:
                pair = wide[0, layer + sign, middle], wide[1, layer + sign, middle]
                total[0] = total[0] + pressed(*pair, own, sign)
            rows = slice(REACH + sign, REACH + sign + size_y)
            total[1] = total[1] + pressed(wide[0, layer, rows], wide[1, layer, rows], own, sign)
            pair = [moved(wide[order, layer, middle], besides_z[order], sign) for order in range(2)]
            total[2] = total[2] + pressed(*pair, own, sign)
        for axis in range(3):
            pressing[axis, layer] = total[axis]
    for layer in range(size_x):
        besides[layer] = beside_columns(wide_pack[0], wide_pack[1], layer * SLOT + 3 * REACH)
    for layer in range(size_x):
        for order, value in each_shift(wide[0, layer], besides[layer], False):
            shifts[order, layer] = value
    for step, first, last, bonds, base in inner_plan(extent, True)[0]:

        def one_layer(layer, carry, step=step, first=first, bonds=bonds, base=base):
            slot = base + (layer - first) * len(bonds)
            far_layer = layer + step
            sublanes = lax.broadcasted_iota(jnp.int32, (8, LANES), 0)
            for order, (tile, step_y, step_z, plane, owner) in enumerate(bonds):
                rows = slice(8 * tile, 8 * tile + 8)
                far_rows = slice(REACH + step_y + 8 * tile, REACH + step_y + 8 * tile + 8)
                keep = keeps[slot + order]
                if not owner:
                    if step_y < 0:
                        at = PAD + Y_UP[plane] * size_x - far_layer * step_y
                        value = rows_low[pl.ds(at, 8)]
                        across = sublanes < -step_y
                    else:
                        at = PAD + Y_DOWN[plane] * size_x + far_layer * step_y + step_y - 8
                        value = rows_high[pl.ds(at, 8)]
                        across = sublanes >= 8 - step_y
                    halo = wanted_keep(
                        value,
                        lambda: wide_broken[0, far_layer, far_rows],
                        lambda: wide_broken[1, far_layer, far_rows],
                        plane, step_z,
                    )
                    keep = jnp.where(across, (0.5 * C_BOND) * halo, keep)
                far = shifts[step_z + REACH, far_layer, far_rows]
                weights[slot + order] = jnp.where(
                    far > 0.0, keep * (stiffness[layer, rows] + far), 0.0
                )
            return carry

        lax.fori_loop(first, last, one_layer, 0)


def weights_outer_kernel(
    extent, edges, stiffness, pore, wide, wide_pack, x_up, x_broken, x_far, x_near,
    pressing_inner, weights, pressing, shifts, planes, besides,
):
    size_x, size_y, _ = extent
    height = wide.shape[2]
    pore_at = x_place(4, REACH, size_y) + height
    broken_at = pore_at + size_y
    rows_at = broken_at + 2 * NEAR * height
    x_low = Either(edges[6], x_near, x_far)
    x_high = Either(edges[6], x_far, x_near)
    fill_outer(extent, 4, edges, (3,), x_low, x_high, shifts, besides)
    for plane, (a, b, _) in enumerate(OFFSETS):
        for layer in range(a):
            at = (X_UP[plane] + layer) * size_y
            place = X_UP[plane] + layer
            planes[place, REACH : REACH + size_y] = x_broken[at : at + size_y]
            at = rows_at + XY_UP.get(plane, 0) + layer * abs(b)
            if b > 0:
                planes[place, REACH - b : REACH] = x_low[at : at + b]
            if b < 0:
                planes[place, REACH + size_y : REACH + size_y - b] = x_low[at : at - b]
    for step, first, last, bonds, base in outer_plan(extent)[0]:
        for layer in range(first, last):
            slot = base + (layer - first) * len(bonds)
            far_layer = layer + step
            far_layer = far_layer + REACH if far_layer < 0 else far_layer - size_x + REACH
            for order, (tile, step_y, step_z, plane, owner) in enumerate(bonds):
                rows = slice(8 * tile, 8 * tile + 8)
                far_rows = slice(REACH + step_y + 8 * tile, REACH + step_y + 8 * tile + 8)
                far = shifts[step_z + REACH, 0, far_layer, far_rows]
                if owner:
                    at = (X_UP[plane] + layer - first) * size_y + 8 * tile
                    keep = 1.0 - x_up[at : at + 8]
                else:
                    low_at = broken_at + (far_layer + NEAR - REACH) * height
                    high_at = low_at + NEAR * height
                    keep = wanted_keep(
                        planes[X_UP[plane] + layer, far_rows],
                        lambda: x_low[far_rows.start + low_at : far_rows.stop + low_at],
                        lambda: x_low[far_rows.start + high_at : far_rows.stop + high_at],
                        plane, step_z,
                    )
                value = keep * (0.5 * C_BOND) * (stiffness[layer, rows] + far)
                weights[slot + order] = jnp.where(far > 0.0, value, 0.0)

    at = x_place(3, 1, size_y) + reach_beside(1)
    pressing[...] = pressing_inner[...]
    for source, flag, layer, sign in ((x_low, 4, 0, -1), (x_high, 5, size_x - 1, 1)):
        pressing[0, layer] += pressed(
            kept(edges[flag], source[at : at + size_y]),
            source[pore_at : pore_at + size_y], pore[layer], sign,
        )


def add_bonds(
    bonds, step, layer, far_layer, first_row, motion, shifts, weights, slot, total, level=None
):
    for tile in sorted({bond[0] for bond in bonds}):
        rows = slice(8 * tile, 8 * tile + 8)
        own = [motion[axis, layer, rows] for axis in range(3)]
        near_x = own[0] - float(step)
        near_y = {step_y: own[1] - float(step_y) for step_y in range(-REACH, REACH + 1)}
        force = [total[axis, layer, rows] for axis in range(3)]
        for order, (bond_tile, step_y, step_z, plane, _) in enumerate(bonds):
            if bond_tile != tile or level not in (None, step_z == 0):
                continue
            far_rows = slice(first_row + step_y + 8 * tile, first_row + step_y + 8 * tile + 8)
            if level:
                far = [motion[axis, far_layer, far_rows] for axis in range(3)]
            else:
                far = [shifts[step_z + REACH, axis, far_layer, far_rows] for axis in range(3)]
            radial = [far[0] - near_x, far[1] - near_y[step_y], far[2] - own[2]]
            square = radial[0] * radial[0] + radial[1] * radial[1] + radial[2] * radial[2]
            rest = math.sqrt(sum(part * part for part in OFFSETS[plane]))
            factor = weights[slot + order] * (1.0 / rest - lax.rsqrt(square))
            force = [force[axis] + factor * radial[axis] for axis in range(3)]
        for axis in range(3):
            total[axis, layer, rows] = force[axis]


def add_inner(extent, late, motion, shifts, weights, total, level=None):
    first_row = 0 if level else FIRST
    for step, first, last, bonds, base in inner_plan(extent, late)[0]:
        if not any(level in (None, bond[2] == 0) for bond in bonds):
            continue

        def one_layer(layer, carry, step=step, first=first, bonds=bonds, base=base):
            slot = base + (layer - first) * len(bonds)
            add_bonds(
                bonds, step, layer, layer + step, first_row, motion, shifts, weights, slot, total,
                level,
            )
            return carry

        lax.fori_loop(first, last, one_layer, 0, unroll=UNROLL if last - first > 1 else 1)


def force_level_kernel(extent, motion, weights, total):
    total[...] = jnp.zeros(total.shape, jnp.float32)
    add_inner(extent, False, motion, None, weights, total, True)


def force_early_kernel(extent, levelled, edges, motion, z_low, z_high, weights, *refs):
    size_x, size_y, _ = extent
    if levelled:
        level, total, shifts, besides = refs
        total[...] = level[...]
    else:
        total, shifts, besides = refs
        total[...] = jnp.zeros(total.shape, jnp.float32)
    low_pack = kept(edges[0], z_low[0:size_y])
    high_pack = kept(edges[1], z_high[0:size_y])
    for layer in range(size_x):
        for axis in range(3):
            besides[axis, layer] = beside_columns(
                low_pack, high_pack, layer * SLOT + axis * REACH
            )

    def fill(layer, carry):
        for axis in range(3):
            for order, value in each_shift(motion[axis, layer], besides[axis, layer], axis == 2):
                shifts[order, axis, layer, FIRST : FIRST + size_y] = value
        return carry

    lax.fori_loop(0, size_x, fill, 0, unroll=UNROLL_FILL)
    add_inner(extent, False, motion, shifts, weights, total, False if levelled else None)


def force_late_kernel(
    extent, count, edges, motion, early, early_shifts, y_low, y_high, weights,
    total, shifts, halo, besides,
):
    size_x, size_y, _ = extent
    total[...] = early[...]
    middle = slice(FIRST, FIRST + size_y)
    above = FIRST + size_y

    def across(place, at):
        halo[place, 0:REACH] = kept(edges[3], y_high[at : at + REACH])
        halo[place, REACH : 8 - REACH] = jnp.zeros((8 - 2 * REACH, LANES), jnp.float32)
        halo[place, 8 - REACH : 8] = kept(edges[2], y_low[at : at + REACH])

    packs = 3 * size_x
    for order in range(2):
        across(packs + order, (count * size_x + order) * REACH)
    for place in range(3 * size_x):
        across(place, place * REACH)
    low_pack, high_pack = halo[packs], halo[packs + 1]
    for layer in range(size_x):
        for axis in range(3):
            besides[axis * size_x + layer] = beside_columns(
                low_pack, high_pack, layer * SLOT + axis * REACH
            )

    def fill(layer, carry):
        for axis in range(3):
            place = axis * size_x + layer
            for order, value in each_shift(halo[place], besides[place], axis == 2):
                shifts[order, axis, layer, middle] = early_shifts[order, axis, layer, middle]
                shifts[order, axis, layer, FIRST - REACH : FIRST] = value[8 - REACH : 8]
                shifts[order, axis, layer, above : above + REACH] = value[0:REACH]
        return carry

    lax.fori_loop(0, size_x, fill, 0, unroll=UNROLL_FILL)
    add_inner(extent, True, motion, shifts, weights, total)


def finish_kernel(
    extent, count, stage, edges, motion, speed, pressing, inner, weights, x_far, x_near, *refs
):
    size_x, size_y, _ = extent
    if stage == "last":
        motion_out, speed_out, accel_out, total, shifts, besides = refs
    else:
        motion_out, speed_out, z_up, z_down, total, shifts, besides = refs
    total[...] = inner[...] + pressing[...]
    x_low = Either(edges[6], x_near, x_far)
    x_high = Either(edges[6], x_far, x_near)
    fill_outer(extent, count, edges, range(3), x_low, x_high, shifts, besides)
    for step, first, last, bonds, base in outer_plan(extent)[0]:
        for layer in range(first, last):
            slot = base + (layer - first) * len(bonds)
            far_layer = layer + step + (REACH if step < 0 else REACH - size_x)
            add_bonds(bonds, step, layer, far_layer, REACH, motion, shifts, weights, slot, total)
    accel = total[...]
    new_speed = speed[...] + HALF_DT * accel
    if stage == "last":
        motion_out[...] = motion[...]
        speed_out[...] = new_speed
        accel_out[...] = accel
        return
    if stage == "middle":
        new_speed = new_speed + HALF_DT * accel
    speed_out[...] = new_speed
    motion_out[...] = motion[...] + DT_STEP * new_speed
    up, down = pack_columns(lambda axis, layer: motion_out[axis, layer], 3, size_x, size_y)
    z_up[...] = up
    z_down[...] = down


VMEM = pl.BlockSpec(memory_space=pltpu.VMEM)
SMEM = pl.BlockSpec(memory_space=pltpu.SMEM)


def call(kernel, scalars, operands, shapes, scratch=(), name=None, results=(), far=()):
    operands = [pltpu.with_memory_space_constraint(operand, pltpu.HBM) for operand in far] + [
        pltpu.with_memory_space_constraint(operand, pltpu.VMEM) for operand in operands
    ]
    return pl.pallas_call(
        kernel,
        out_shape=[
            jax.ShapeDtypeStruct(shape, jnp.float32)
            if place in results
            else pltpu.VMEM(shape, jnp.float32)
            for place, shape in enumerate(shapes)
        ],
        in_specs=[SMEM] * len(scalars)
        + [pl.BlockSpec(memory_space=pltpu.HBM)] * len(far)
        + [VMEM] * (len(operands) - len(far)),
        out_specs=[VMEM] * len(shapes),
        scratch_shapes=[
            pltpu.VMEM(item, jnp.float32) if isinstance(item, tuple) else item for item in scratch
        ],
        compiler_params=pltpu.CompilerParams(vmem_limit_bytes=24 * 1024 * 1024),
        name=name,
    )(*scalars, *operands)


def sent(value, axis, distance):
    count = lax.axis_size(axis)
    return lax.ppermute(value, axis, [(i, (i + distance) % count) for i in range(count)])


def swapped(near, far):
    count = lax.axis_size("gx")
    side = [1 - 2 * (i % 2) for i in range(count)]
    far = lax.ppermute(far, "gx", [(i, (i - side[i]) % count) for i in range(count)])
    return lax.ppermute(near, "gx", [(i, i + side[i]) for i in range(count)]), far


def on_device(displacement, velocity, stiffness, broken, borehole_id, flags, pressure):
    extent = stiffness.shape
    size_x, size_y, _ = extent
    height = size_y + 8
    tall = size_y + 2 * FIRST
    edges = jnp.stack(
        [
            end
            for axis in ("gz", "gy", "gx")
            for end in (
                (lax.axis_index(axis) > 0).astype(jnp.int32),
                (lax.axis_index(axis) < lax.axis_size(axis) - 1).astype(jnp.int32),
            )
        ]
        + [lax.axis_index("gx") % 2]
    )
    field = (size_x, size_y, LANES)
    vector = (3,) + field
    part = functools.partial

    pack = (size_y + size_x * size_y + PAD, LANES)
    rows_shapes = [(count * size_x + 2 * PAD, LANES) for count in (Y_UP_COUNT, Y_DOWN_COUNT)]
    layers_shape = (X_UP_COUNT * size_y, LANES)
    motion, stiffness, pore, z_up, z_down, rows_up, rows_down, x_up = pl.pallas_call(
        part(start_kernel, extent),
        out_shape=[
            pltpu.VMEM(shape, kind)
            for shape, kind in (
                (vector, jnp.float32), (field, jnp.float32),
                (field, jnp.float32), (pack, jnp.float32), (pack, jnp.float32),
                (rows_shapes[0], jnp.float32), (rows_shapes[1], jnp.float32),
                (layers_shape, jnp.float32),
            )
        ],
        in_specs=[pl.BlockSpec(memory_space=pltpu.HBM)] * 6,
        out_specs=[VMEM] * 8,
        scratch_shapes=[
            pltpu.VMEM(broken.shape, jnp.int32),
            pltpu.SMEM(pressure.shape, jnp.float32),
            pltpu.VMEM(field, jnp.int32),
            pltpu.VMEM(field, jnp.int32),
            pltpu.SemaphoreType.DMA((5,)),
            pltpu.SemaphoreType.DMA((size_x,)),
        ],
        compiler_params=pltpu.CompilerParams(vmem_limit_bytes=24 * 1024 * 1024),
        name="start",
    )(
        *(
            pltpu.with_memory_space_constraint(operand, pltpu.HBM)
            for operand in (pressure, displacement, stiffness, borehole_id, flags, broken)
        )
    )
    z_low = sent(z_up, "gz", 1)
    z_high = sent(z_down, "gz", -1)
    rows_low = sent(rows_up, "gy", 1)
    rows_high = sent(rows_down, "gy", -1)
    x_broken = sent(x_up, "gx", 1)
    rows = (round_up(5 * size_x * REACH + 2 * REACH + 2 * size_x * REACH), LANES)
    y_up, y_down = call(
        part(y_rows_first_kernel, extent), [edges],
        [motion, stiffness, pore, z_low, z_high], [rows, rows], name="y_rows_first",
    )
    y_low = sent(y_up, "gy", 1)
    y_high = sent(y_down, "gy", -1)
    moves = 2 * REACH + 1
    early_slots = inner_plan(extent, False)[1]
    late_slots = inner_plan(extent, True)[1]
    outer_slots = outer_plan(extent)[1]
    weights_early, keeps = call(
        part(weights_early_kernel, extent), [edges], [stiffness, z_low, z_high],
        [(early_slots, 8, LANES), (late_slots, 8, LANES)],
        [
            (moves, size_x, tall, LANES),
            (len(OFFSETS), size_x, tall, LANES),
            field,
            pltpu.VMEM(broken.shape, jnp.int32),
            pltpu.SemaphoreType.DMA((size_x,)),
        ], name="weights_early", far=[broken],
    )

    def force_early(motion, z_low, z_high, *level):
        return call(
            part(force_early_kernel, extent, bool(level)), [edges],
            [motion, z_low, z_high, weights_early, *level],
            [vector, (moves, 3, size_x, tall, LANES)], [vector], name="force_early",
        )

    def force_late(count, motion, early, early_shifts, y_low, y_high):
        return call(
            part(force_late_kernel, extent, count), [edges],
            [motion, early, early_shifts, y_low, y_high, weights_late], [vector],
            [(moves, 3, size_x, tall, LANES), (2 + 3 * size_x, 8, LANES), (3 * size_x, 8, LANES)], name="force_late",
        )[0]

    early, early_shifts = force_early(motion, z_low, z_high)
    y_low, y_high, x_broken, early = lax.optimization_barrier((y_low, y_high, x_broken, early))
    layers = x_place(4, REACH, size_y) + height + size_y
    layers = round_up(layers + 2 * NEAR * height + XY_UP_COUNT)
    wide_static, wide_pack, wide_broken, x_near, x_far = call(
        part(x_layers_first_kernel, extent), [edges],
        [motion, stiffness, pore, z_low, z_high, y_low, y_high, rows_low, rows_high],
        [
            (2, size_x, height, LANES),
            (2, height, LANES),
            (2, size_x, height, LANES),
            (layers, LANES),
            (layers, LANES),
        ], [(3, size_x, height, LANES)], name="x_layers_first",
    )
    x_near, x_far = swapped(x_near, x_far)
    weights_late, pressing = call(
        part(weights_late_kernel, extent), [],
        [stiffness, pore, wide_static, wide_pack, wide_broken, rows_low, rows_high, keeps],
        [(late_slots, 8, LANES), vector],
        [(moves, size_x, height, LANES), (size_x, height, LANES)], name="weights_late",
    )
    inner = force_late(5, motion, early, early_shifts, y_low, y_high)
    outer_weights, pressing = call(
        part(weights_outer_kernel, extent), [edges],
        [stiffness, pore, wide_static, wide_pack, x_up, x_broken, x_far, x_near, pressing],
        [(outer_slots, 8, LANES), vector],
        [
            (moves, 1, 2 * REACH, height, LANES),
            (X_UP_COUNT, height, LANES),
            (1, 2 * REACH, height, LANES),
        ], name="weights_outer",
    )

    def finish(stage, count, motion, speed, inner, x_near, x_far):
        columns = (size_y, LANES)
        shapes = [vector] * 3 if stage == "last" else [vector, vector, columns, columns]
        return call(
            part(finish_kernel, extent, count, stage), [edges],
            [motion, speed, pressing, inner, outer_weights, x_far, x_near],
            shapes,
            [
                vector,
                (moves, 3, 2 * REACH, height, LANES),
                (3, 2 * REACH, height, LANES),
            ], name="finish_" + stage,
            results=(0, 1, 2) if stage == "last" else (),
        )

    motion, speed, z_up, z_down = finish(
        "first", 4, motion, velocity, inner, x_near, x_far
    )
    for step_index in range(STEPS):
        z_low = sent(z_up, "gz", 1)
        z_high = sent(z_down, "gz", -1)
        (level,) = call(
            part(force_level_kernel, extent), [], [motion, weights_early], [vector],
            name="force_level",
        )
        z_low, z_high, level = lax.optimization_barrier((z_low, z_high, level))
        rows = (round_up(3 * size_x * REACH + 2 * REACH), LANES)
        y_up, y_down = call(
            part(y_rows_kernel, extent), [edges], [motion, z_low, z_high], [rows, rows],
            name="y_rows",
        )
        y_low = sent(y_up, "gy", 1)
        y_high = sent(y_down, "gy", -1)
        early, early_shifts = force_early(motion, z_low, z_high, level)
        y_low, y_high, early = lax.optimization_barrier((y_low, y_high, early))
        layers = round_up(x_place(3, REACH, size_y) + height)
        x_near, x_far = call(
            part(x_layers_kernel, extent), [edges],
            [motion, z_low, z_high, y_low, y_high],
            [(layers, LANES), (layers, LANES)],
            [(3, size_x, height, LANES), (2, height, LANES)], name="x_layers",
        )
        x_near, x_far = swapped(x_near, x_far)
        inner = force_late(3, motion, early, early_shifts, y_low, y_high)
        if step_index < STEPS - 1:
            motion, speed, z_up, z_down = finish("middle", 3, motion, speed, inner, x_near, x_far)
        else:
            motion, speed, accel = finish("last", 3, motion, speed, inner, x_near, x_far)
    return (motion, speed, accel)


def solution(mesh):
    in_specs = (
        P(None, "gx", "gy", "gz"),
        P(None, "gx", "gy", "gz"),
        P("gx", "gy", "gz"),
        P(None, "gx", "gy", "gz"),
        P("gx", "gy", "gz"),
        P("gx", "gy", "gz"),
        P(),
    )
    out_specs = (P(None, "gx", "gy", "gz"), P(None, "gx", "gy", "gz"), P(None, "gx", "gy", "gz"))
    return jax.shard_map(
        on_device, mesh=mesh, in_specs=in_specs, out_specs=out_specs, check_vma=False
    )
```

```python
import functools
import math

import jax
import jax.numpy as jnp
from jax import lax
from jax.experimental import pallas as pl
from jax.experimental.pallas import tpu as pltpu
from jax.sharding import PartitionSpec as P

STEPS = 2
C_BOND = 3.0
DT_STEP = 0.04
REACH = 3
NEAR = 2
LANES = 128
SLOT = 16
PAD = 8
UNROLL = 2
UNROLL_FILL = 2
FIRST = 8
HALF_DT = 0.5 * DT_STEP


def half_offsets():
    result = []
    for step_x in range(0, 4):
        for step_y in range(-3, 4):
            for step_z in range(-3, 4):
                square = step_x * step_x + step_y * step_y + step_z * step_z
                if square == 0 or square > 9:
                    continue
                if step_x > 0 or (step_x == 0 and (step_y > 0 or (step_y == 0 and step_z > 0))):
                    result.append((step_x, step_y, step_z))
    return result


OFFSETS = half_offsets()
BONDS = {step: [] for step in range(-REACH, REACH + 1)}
for _plane, (_a, _b, _c) in enumerate(OFFSETS):
    BONDS[_a].append((_b, _c, _plane, True))
    BONDS[-_a].append((-_b, -_c, _plane, False))


def inner_layers(step, extent):
    return max(0, -step), min(extent, extent - step)


def outer_layers(step, extent):
    return (extent - step, extent) if step > 0 else (0, -step)


STEPS_ALL = list(range(-REACH, REACH + 1))
STEPS_OUT = [step for step in STEPS_ALL if step != 0]


def tiled_bonds(step, tiles):
    early, late = [], []
    for tile in range(tiles):
        for bond in BONDS[step]:
            low, high = 8 * tile + bond[0], 8 * tile + 8 + bond[0]
            (early if low >= 0 and high <= 8 * tiles else late).append((tile, *bond))
    return early, late


def inner_plan(extent, late):
    plan, total = [], 0
    for step in STEPS_ALL:
        bonds = tiled_bonds(step, extent[1] // 8)[int(late)]
        first, last = inner_layers(step, extent[0])
        plan.append((step, first, last, bonds, total))
        total += (last - first) * len(bonds)
    return plan, total


def outer_plan(extent):
    plan, total = [], 0
    for step in STEPS_OUT:
        bonds = [(tile, *bond) for tile in range(extent[1] // 8) for bond in BONDS[step]]
        first, last = outer_layers(step, extent[0])
        plan.append((step, first, last, bonds, total))
        total += (last - first) * len(bonds)
    return plan, total


def reach_beside(distance):
    return max(max(abs(b), abs(c)) for a, b, c in OFFSETS if a >= distance)


def x_span(distance, size_y):
    return REACH - reach_beside(distance), REACH + size_y + reach_beside(distance)


def x_place(field, distance, size_y):
    lengths = [high - low for low, high in (x_span(far, size_y) for far in (3, 2, 1))]
    return field * sum(lengths) + sum(lengths[: REACH - distance])


def round_up(count):
    return (count + 7) // 8 * 8


def running(amounts):
    places, total = {}, 0
    for plane, amount in amounts:
        places[plane] = total
        total += amount
    return places, total


Z_UP, Z_UP_COUNT = running([(k, c) for k, (a, b, c) in enumerate(OFFSETS) if c > 0])
Z_DOWN, Z_DOWN_COUNT = running([(k, -c) for k, (a, b, c) in enumerate(OFFSETS) if c < 0])
Y_UP, Y_UP_COUNT = running([(k, b) for k, (a, b, c) in enumerate(OFFSETS) if b > 0])
Y_DOWN, Y_DOWN_COUNT = running([(k, -b) for k, (a, b, c) in enumerate(OFFSETS) if b < 0])
X_UP, X_UP_COUNT = running([(k, a) for k, (a, b, c) in enumerate(OFFSETS) if a > 0])
XY_UP, XY_UP_COUNT = running([(k, a * abs(b)) for k, (a, b, c) in enumerate(OFFSETS) if a * abs(b) > 0])


def lanes_like(value):
    return lax.broadcasted_iota(jnp.int32, value.shape, value.ndim - 1)


def rolled(value, shift):
    shift = shift % LANES
    return value if shift == 0 else pltpu.roll(value, shift, value.ndim - 1)


def beside_columns(low_pack, high_pack, lane_of, high_lanes=0):
    lanes = lanes_like(low_pack)
    return jnp.where(
        lanes < REACH,
        rolled(high_pack, -lane_of - high_lanes),
        rolled(low_pack, LANES - REACH - lane_of),
    )


def moved(main, beside, step):
    if step == 0:
        return main
    lanes = lanes_like(main)
    if step > 0:
        return rolled(jnp.where(lanes < step, beside, main), -step)
    return rolled(jnp.where(lanes >= LANES + step, beside, main), -step)


def pack_columns(field_of, count, extent, height):
    lanes = lax.broadcasted_iota(jnp.int32, (height, LANES), 1)
    up = jnp.zeros((height, LANES), jnp.float32)
    down = up
    for layer in range(extent):
        for field in range(count):
            lane_of = layer * SLOT + field * REACH
            value = field_of(field, layer)
            here = (lanes >= lane_of) & (lanes < lane_of + REACH)
            up = jnp.where(here, rolled(value, lane_of - (LANES - REACH)), up)
            down = jnp.where(here, rolled(value, lane_of), down)
    return up, down


class Either:
    def __init__(self, odd, if_odd, if_even):
        self.odd, self.if_odd, self.if_even = odd, if_odd, if_even

    def __getitem__(self, rows):
        return jnp.where(self.odd > 0, self.if_odd[rows], self.if_even[rows])


def by_parity(odd, near, far, write):
    @pl.when(odd > 0)
    def _():
        write(far, near)

    @pl.when(odd == 0)
    def _():
        write(near, far)


def kept(flag, value):
    return jnp.where(flag > 0, value, 0.0)


def start_kernel(
    extent, pressure_in, motion_in, stiffness_in, borehole_in, flags_in, broken_in,
    motion, stiffness, pore, z_up, z_down, rows_up, rows_down, x_up,
    broken, pressure, borehole, flags, field_sems, layer_sems,
):
    size_x, size_y, _ = extent
    pairs = (
        (pressure_in, pressure), (borehole_in, borehole), (flags_in, flags),
        (motion_in, motion), (stiffness_in, stiffness),
    )
    copies = [
        pltpu.make_async_copy(source, target, field_sems.at[place])
        for place, (source, target) in enumerate(pairs)
    ]

    def layer_copy(layer):
        return pltpu.make_async_copy(
            broken_in.at[:, layer], broken.at[:, layer], layer_sems.at[layer]
        )

    for copy in copies:
        copy.start()
    for layer in range(size_x):
        layer_copy(layer).start()
    for copy in copies:
        copy.wait()
    ids = borehole[...]
    level = jnp.zeros(ids.shape, jnp.float32)
    for label in range(pressure.shape[0]):
        level = jnp.where(ids == label, pressure[label], level)
    pore[...] = flags[...].astype(jnp.float32) * level

    def field_of(field, layer):
        if field < 3:
            return motion[field, layer]
        return stiffness[layer] if field == 3 else pore[layer]

    up, down = pack_columns(field_of, 5, size_x, size_y)
    z_up[0:size_y] = up
    z_down[0:size_y] = down

    def one_layer(layer, carry):
        layer_copy(layer).wait()
        lanes = lax.broadcasted_iota(jnp.int32, (size_y, LANES), 1)
        rows = pl.ds(size_y + layer * size_y, size_y)
        up = jnp.zeros((size_y, LANES), jnp.float32)
        down = up
        for plane, (_, _, c) in enumerate(OFFSETS):
            if c > 0:
                at = Z_UP[plane]
                value = broken[plane, layer].astype(jnp.float32)
                up = jnp.where((lanes >= at) & (lanes < at + c), rolled(value, at + c), up)
            if c < 0:
                at = Z_DOWN[plane]
                value = broken[plane, layer].astype(jnp.float32)
                down = jnp.where((lanes >= at) & (lanes < at - c), rolled(value, at), down)
        z_up[rows] = up
        z_down[rows] = down
        return carry

    lax.fori_loop(0, size_x, one_layer, 0)
    for plane, (a, _, _) in enumerate(OFFSETS):
        for layer in range(a):
            at = (X_UP[plane] + layer) * size_y
            x_up[at : at + size_y] = broken[plane, size_x - a + layer].astype(jnp.float32)
    for plane, (_, b, _) in enumerate(OFFSETS):
        for layer in range(size_x):
            if b > 0:
                at = PAD + Y_UP[plane] * size_x + layer * b
                rows_up[at : at + b] = broken[plane, layer, size_y - b : size_y].astype(jnp.float32)
            if b < 0:
                at = PAD + Y_DOWN[plane] * size_x - layer * b
                rows_down[at : at - b] = broken[plane, layer, 0:-b].astype(jnp.float32)


def copy_y_rows(field_of, count, extent, low_pack, high_pack, y_up, y_down):
    size_x, size_y, _ = extent
    for field in range(count):
        for layer in range(size_x):
            at = (field * size_x + layer) * REACH
            y_up[at : at + REACH] = field_of(field, layer, slice(size_y - REACH, size_y))
            y_down[at : at + REACH] = field_of(field, layer, slice(0, REACH))
    at = count * size_x * REACH
    for pack in (low_pack, high_pack):
        y_up[at : at + REACH] = pack[size_y - REACH : size_y]
        y_down[at : at + REACH] = pack[0:REACH]
        at += REACH
    return at


def y_rows_kernel(extent, edges, motion, z_low, z_high, y_up, y_down):
    size_y = extent[1]
    low_pack = kept(edges[0], z_low[0:size_y])
    high_pack = kept(edges[1], z_high[0:size_y])
    copy_y_rows(
        lambda field, layer, rows: motion[field, layer, rows],
        3, extent, low_pack, high_pack, y_up, y_down,
    )


def y_rows_first_kernel(extent, edges, motion, stiffness, pore, z_low, z_high, y_up, y_down):
    size_x, size_y, _ = extent
    low_pack = kept(edges[0], z_low[0:size_y])
    high_pack = kept(edges[1], z_high[0:size_y])

    def field_of(field, layer, rows):
        if field < 3:
            return motion[field, layer, rows]
        return stiffness[layer, rows] if field == 3 else pore[layer, rows]

    base = copy_y_rows(field_of, 5, extent, low_pack, high_pack, y_up, y_down)
    for order, pack in enumerate((z_low, z_high)):
        for layer in range(size_x):
            first = size_y + layer * size_y
            at = base + (order * size_x + layer) * REACH
            y_up[at : at + REACH] = pack[first + size_y - REACH : first + size_y]
            y_down[at : at + REACH] = pack[first : first + REACH]


def widen(target, low_rows, middle, high_rows):
    size_y = middle.shape[0]
    target[0:REACH] = low_rows
    target[REACH : REACH + size_y] = middle
    target[REACH + size_y : 2 * REACH + size_y] = high_rows
    height = target.shape[0]
    target[2 * REACH + size_y : height] = jnp.zeros((height - 2 * REACH - size_y, LANES), jnp.float32)


def widen_fields(edges, field_of, count, extent, z_low, z_high, y_low, y_high, target, wide_pack):
    size_x, size_y, _ = extent
    for field in range(count):
        for layer in range(size_x):
            at = (field * size_x + layer) * REACH
            widen(
                target(field).at[layer],
                kept(edges[2], y_low[at : at + REACH]),
                field_of(field, layer),
                kept(edges[3], y_high[at : at + REACH]),
            )
    at = count * size_x * REACH
    for order, pack in enumerate((z_low, z_high)):
        widen(
            wide_pack.at[order],
            kept(edges[2], y_low[at : at + REACH]),
            kept(edges[order], pack[0:size_y]),
            kept(edges[3], y_high[at : at + REACH]),
        )
        at += REACH
    return at


def copy_x_layers(count, extent, target, wide_pack, x_up, x_down):
    size_x, size_y, _ = extent
    height = wide_pack.shape[1]
    for field in range(count):
        for distance in (3, 2, 1):
            low, high = x_span(distance, size_y)
            at = x_place(field, distance, size_y)
            x_up[at : at + high - low] = target(field)[size_x - distance, low:high]
            x_down[at : at + high - low] = target(field)[distance - 1, low:high]
    at = x_place(count, REACH, size_y)
    low_pack, high_pack = wide_pack[0], wide_pack[1]
    half = lanes_like(low_pack) < LANES // 2
    other = rolled(high_pack, LANES // 2)
    x_up[at : at + height] = jnp.where(half, other, low_pack)
    x_down[at : at + height] = jnp.where(half, low_pack, other)
    return at + height


def x_layers_kernel(
    extent, edges, motion, z_low, z_high, y_low, y_high, x_near, x_far, wide, wide_pack
):
    widen_fields(
        edges, lambda field, layer: motion[field, layer],
        3, extent, z_low, z_high, y_low, y_high, lambda field: wide.at[field], wide_pack,
    )

    def write(x_up, x_down):
        copy_x_layers(3, extent, lambda field: wide.at[field], wide_pack, x_up, x_down)

    by_parity(edges[6], x_near, x_far, write)


def x_layers_first_kernel(
    extent, edges, motion, stiffness, pore, z_low, z_high, y_low, y_high, rows_low, rows_high,
    wide_static, wide_pack, wide_broken, x_near, x_far, wide,
):
    size_x, size_y, _ = extent

    def field_of(field, layer):
        if field < 3:
            return motion[field, layer]
        return stiffness[layer] if field == 3 else pore[layer]

    def target(field):
        return wide.at[field] if field < 3 else wide_static.at[field - 3]

    base = widen_fields(
        edges, field_of, 5, extent, z_low, z_high, y_low, y_high, target, wide_pack
    )
    for order, pack in enumerate((z_low, z_high)):
        for layer in range(size_x):
            first = size_y + layer * size_y
            at = base + (order * size_x + layer) * REACH
            widen(
                wide_broken.at[order, layer],
                y_low[at : at + REACH],
                pack[first : first + size_y],
                y_high[at : at + REACH],
            )

    def write(x_up, x_down):
        at = copy_x_layers(4, extent, target, wide_pack, x_up, x_down)
        height = wide.shape[2]
        x_up[at : at + size_y] = pore[size_x - 1]
        x_down[at : at + size_y] = pore[0]
        at += size_y
        for order in range(2):
            for layer in range(NEAR):
                x_up[at : at + height] = wide_broken[order, size_x - NEAR + layer]
                at += height
        for plane, (a, b, _) in enumerate(OFFSETS):
            if a * b == 0:
                continue
            rows, many = abs(b), a * abs(b)
            source = rows_low if b > 0 else rows_high
            first = PAD + (Y_UP if b > 0 else Y_DOWN)[plane] * size_x + (size_x - a) * rows
            x_up[at + XY_UP[plane] : at + XY_UP[plane] + many] = source[first : first + many]

    by_parity(edges[6], x_near, x_far, write)


def each_shift(main, beside, add_step, reach=REACH):
    for step in range(-reach, reach + 1):
        value = moved(main, beside, step)
        yield step + REACH, value + float(step) if add_step and step else value


def wanted_keep(value, low, high, plane, step_z):
    if step_z == 0:
        return 1.0 - value
    lanes = lanes_like(value)
    if step_z < 0:
        beside = rolled(low(), -Z_UP[plane])
        value = jnp.where(lanes < -step_z, beside, rolled(value, -step_z))
    else:
        beside = rolled(high(), LANES - step_z - Z_DOWN[plane])
        value = jnp.where(lanes >= LANES - step_z, beside, rolled(value, -step_z))
    return 1.0 - value


def fill_outer(extent, count, edges, fields, x_low, x_high, shifts, besides):
    size_x, size_y, _ = extent
    height = shifts.shape[3]
    at = x_place(count, REACH, size_y)
    sides = ((x_low, size_x - REACH, -LANES // 2), (x_high, 0, LANES // 2))
    for side, (source, first, high_lanes) in enumerate(sides):
        pack = kept(edges[4 + side], source[at : at + height])
        for layer in range(REACH):
            for order, field in enumerate(fields):
                lane_of = (first + layer) * SLOT + field * REACH
                besides[order, side * REACH + layer] = beside_columns(
                    pack, pack, lane_of, high_lanes
                )
    for side, (source, _, _) in enumerate(sides):
        for layer in range(REACH):
            distance = REACH - layer if side == 0 else layer + 1
            low, high = x_span(distance, size_y)
            for order, field in enumerate(fields):
                start = x_place(field, distance, size_y)
                for step, value in each_shift(
                    kept(edges[4 + side], source[start : start + high - low]),
                    besides[order, side * REACH + layer, low:high],
                    field == 2, reach_beside(distance),
                ):
                    shifts[step, order, side * REACH + layer, low:high] = value


def weights_early_kernel(
    extent, edges, broken_in, stiffness, z_low, z_high, weights, keeps,
    shifts, planes, besides, broken, sems,
):
    size_x, size_y, _ = extent

    def layer_copy(layer):
        return pltpu.make_async_copy(broken_in.at[:, layer], broken.at[:, layer], sems.at[layer])

    for layer in range(size_x):
        layer_copy(layer).start()
    low_pack = kept(edges[0], z_low[0:size_y])
    high_pack = kept(edges[1], z_high[0:size_y])
    for layer in range(size_x):
        besides[layer] = beside_columns(low_pack, high_pack, layer * SLOT + 3 * REACH)
    for layer in range(size_x):
        for order, value in each_shift(stiffness[layer], besides[layer], False):
            shifts[order, layer, FIRST : FIRST + size_y] = value

    def fill(layer, carry):
        layer_copy(layer).wait()
        for plane in range(len(OFFSETS)):
            planes[plane, layer, FIRST : FIRST + size_y] = broken[plane, layer].astype(jnp.float32)
        return carry

    lax.fori_loop(0, size_x, fill, 0)
    for late, target in ((False, weights), (True, keeps)):
        for step, first, last, bonds, base in inner_plan(extent, late)[0]:

            def one_layer(layer, carry, step=step, first=first, bonds=bonds, base=base):
                slot = base + (layer - first) * len(bonds)
                far_layer = layer + step
                for order, (tile, step_y, step_z, plane, owner) in enumerate(bonds):
                    rows = slice(8 * tile, 8 * tile + 8)
                    far_rows = slice(FIRST + step_y + 8 * tile, FIRST + step_y + 8 * tile + 8)
                    if owner:
                        keep = 1.0 - broken[plane, layer, rows].astype(jnp.float32)
                    else:
                        at = size_y + far_layer * size_y + step_y + 8 * tile
                        keep = wanted_keep(
                            planes[plane, far_layer, far_rows],
                            lambda: z_low[pl.ds(at, 8)],
                            lambda: z_high[pl.ds(at, 8)],
                            plane, step_z,
                        )
                    keep = (0.5 * C_BOND) * keep
                    if not late:
                        far = shifts[step_z + REACH, far_layer, far_rows]
                        keep = jnp.where(far > 0.0, keep * (stiffness[layer, rows] + far), 0.0)
                    target[slot + order] = keep
                return carry

            lax.fori_loop(first, last, one_layer, 0, unroll=UNROLL if last - first > 1 else 1)


def pressed(inside, level, own, sign):
    return jnp.where(inside > 0.0, (-0.5 * sign) * (level - own), 0.0)


def weights_late_kernel(
    extent, stiffness, pore, wide, wide_pack, wide_broken, rows_low, rows_high, keeps,
    weights, pressing, shifts, besides,
):
    size_x, size_y, _ = extent
    middle = slice(REACH, REACH + size_y)
    for layer in range(size_x):
        own = pore[layer]
        besides_z = [
            beside_columns(wide_pack[0, middle], wide_pack[1, middle], layer * SLOT + field * REACH)
            for field in (3, 4)
        ]
        total = [jnp.zeros((size_y, LANES), jnp.float32) for axis in range(3)]
        for sign in (1, -1):
            if 0 <= layer + sign < size_x:
                pair = wide[0, layer + sign, middle], wide[1, layer + sign, middle]
                total[0] = total[0] + pressed(*pair, own, sign)
            rows = slice(REACH + sign, REACH + sign + size_y)
            total[1] = total[1] + pressed(wide[0, layer, rows], wide[1, layer, rows], own, sign)
            pair = [moved(wide[order, layer, middle], besides_z[order], sign) for order in range(2)]
            total[2] = total[2] + pressed(*pair, own, sign)
        for axis in range(3):
            pressing[axis, layer] = total[axis]
    for layer in range(size_x):
        besides[layer] = beside_columns(wide_pack[0], wide_pack[1], layer * SLOT + 3 * REACH)
    for layer in range(size_x):
        for order, value in each_shift(wide[0, layer], besides[layer], False):
            shifts[order, layer] = value
    for step, first, last, bonds, base in inner_plan(extent, True)[0]:

        def one_layer(layer, carry, step=step, first=first, bonds=bonds, base=base):
            slot = base + (layer - first) * len(bonds)
            far_layer = layer + step
            sublanes = lax.broadcasted_iota(jnp.int32, (8, LANES), 0)
            for order, (tile, step_y, step_z, plane, owner) in enumerate(bonds):
                rows = slice(8 * tile, 8 * tile + 8)
                far_rows = slice(REACH + step_y + 8 * tile, REACH + step_y + 8 * tile + 8)
                keep = keeps[slot + order]
                if not owner:
                    if step_y < 0:
                        at = PAD + Y_UP[plane] * size_x - far_layer * step_y
                        value = rows_low[pl.ds(at, 8)]
                        across = sublanes < -step_y
                    else:
                        at = PAD + Y_DOWN[plane] * size_x + far_layer * step_y + step_y - 8
                        value = rows_high[pl.ds(at, 8)]
                        across = sublanes >= 8 - step_y
                    halo = wanted_keep(
                        value,
                        lambda: wide_broken[0, far_layer, far_rows],
                        lambda: wide_broken[1, far_layer, far_rows],
                        plane, step_z,
                    )
                    keep = jnp.where(across, (0.5 * C_BOND) * halo, keep)
                far = shifts[step_z + REACH, far_layer, far_rows]
                weights[slot + order] = jnp.where(
                    far > 0.0, keep * (stiffness[layer, rows] + far), 0.0
                )
            return carry

        lax.fori_loop(first, last, one_layer, 0, unroll=UNROLL if last - first > 1 else 1)


def weights_outer_kernel(
    extent, edges, stiffness, pore, wide, wide_pack, x_up, x_broken, x_far, x_near,
    pressing_inner, weights, pressing, shifts, planes, besides,
):
    size_x, size_y, _ = extent
    height = wide.shape[2]
    pore_at = x_place(4, REACH, size_y) + height
    broken_at = pore_at + size_y
    rows_at = broken_at + 2 * NEAR * height
    x_low = Either(edges[6], x_near, x_far)
    x_high = Either(edges[6], x_far, x_near)
    fill_outer(extent, 4, edges, (3,), x_low, x_high, shifts, besides)
    for plane, (a, b, _) in enumerate(OFFSETS):
        for layer in range(a):
            at = (X_UP[plane] + layer) * size_y
            place = X_UP[plane] + layer
            planes[place, REACH : REACH + size_y] = x_broken[at : at + size_y]
            at = rows_at + XY_UP.get(plane, 0) + layer * abs(b)
            if b > 0:
                planes[place, REACH - b : REACH] = x_low[at : at + b]
            if b < 0:
                planes[place, REACH + size_y : REACH + size_y - b] = x_low[at : at - b]
    for step, first, last, bonds, base in outer_plan(extent)[0]:
        for layer in range(first, last):
            slot = base + (layer - first) * len(bonds)
            far_layer = layer + step
            far_layer = far_layer + REACH if far_layer < 0 else far_layer - size_x + REACH
            for order, (tile, step_y, step_z, plane, owner) in enumerate(bonds):
                rows = slice(8 * tile, 8 * tile + 8)
                far_rows = slice(REACH + step_y + 8 * tile, REACH + step_y + 8 * tile + 8)
                far = shifts[step_z + REACH, 0, far_layer, far_rows]
                if owner:
                    at = (X_UP[plane] + layer - first) * size_y + 8 * tile
                    keep = 1.0 - x_up[at : at + 8]
                else:
                    low_at = broken_at + (far_layer + NEAR - REACH) * height
                    high_at = low_at + NEAR * height
                    keep = wanted_keep(
                        planes[X_UP[plane] + layer, far_rows],
                        lambda: x_low[far_rows.start + low_at : far_rows.stop + low_at],
                        lambda: x_low[far_rows.start + high_at : far_rows.stop + high_at],
                        plane, step_z,
                    )
                value = keep * (0.5 * C_BOND) * (stiffness[layer, rows] + far)
                weights[slot + order] = jnp.where(far > 0.0, value, 0.0)

    at = x_place(3, 1, size_y) + reach_beside(1)
    pressing[...] = pressing_inner[...]
    for source, flag, layer, sign in ((x_low, 4, 0, -1), (x_high, 5, size_x - 1, 1)):
        pressing[0, layer] += pressed(
            kept(edges[flag], source[at : at + size_y]),
            source[pore_at : pore_at + size_y], pore[layer], sign,
        )


def add_bonds(
    bonds, step, layer, far_layer, first_row, motion, shifts, weights, slot, total, level=None
):
    for tile in sorted({bond[0] for bond in bonds}):
        rows = slice(8 * tile, 8 * tile + 8)
        own = [motion[axis, layer, rows] for axis in range(3)]
        near_x = own[0] - float(step)
        near_y = {step_y: own[1] - float(step_y) for step_y in range(-REACH, REACH + 1)}
        force = [total[axis, layer, rows] for axis in range(3)]
        for order, (bond_tile, step_y, step_z, plane, _) in enumerate(bonds):
            if bond_tile != tile or level not in (None, step_z == 0):
                continue
            far_rows = slice(first_row + step_y + 8 * tile, first_row + step_y + 8 * tile + 8)
            if level:
                far = [motion[axis, far_layer, far_rows] for axis in range(3)]
            else:
                far = [shifts[step_z + REACH, axis, far_layer, far_rows] for axis in range(3)]
            radial = [far[0] - near_x, far[1] - near_y[step_y], far[2] - own[2]]
            square = radial[0] * radial[0] + radial[1] * radial[1] + radial[2] * radial[2]
            rest = math.sqrt(sum(part * part for part in OFFSETS[plane]))
            factor = weights[slot + order] * (1.0 / rest - lax.rsqrt(square))
            force = [force[axis] + factor * radial[axis] for axis in range(3)]
        for axis in range(3):
            total[axis, layer, rows] = force[axis]


def add_inner(extent, late, motion, shifts, weights, total, level=None):
    first_row = 0 if level else FIRST
    for step, first, last, bonds, base in inner_plan(extent, late)[0]:
        if not any(level in (None, bond[2] == 0) for bond in bonds):
            continue

        def one_layer(layer, carry, step=step, first=first, bonds=bonds, base=base):
            slot = base + (layer - first) * len(bonds)
            add_bonds(
                bonds, step, layer, layer + step, first_row, motion, shifts, weights, slot, total,
                level,
            )
            return carry

        lax.fori_loop(first, last, one_layer, 0, unroll=UNROLL if last - first > 1 else 1)


def force_level_kernel(extent, motion, weights, total):
    total[...] = jnp.zeros(total.shape, jnp.float32)
    add_inner(extent, False, motion, None, weights, total, True)


def force_early_kernel(extent, levelled, edges, motion, z_low, z_high, weights, *refs):
    size_x, size_y, _ = extent
    if levelled:
        level, total, shifts, besides = refs
        total[...] = level[...]
    else:
        total, shifts, besides = refs
        total[...] = jnp.zeros(total.shape, jnp.float32)
    low_pack = kept(edges[0], z_low[0:size_y])
    high_pack = kept(edges[1], z_high[0:size_y])
    for layer in range(size_x):
        for axis in range(3):
            besides[axis, layer] = beside_columns(
                low_pack, high_pack, layer * SLOT + axis * REACH
            )

    def fill(layer, carry):
        for axis in range(3):
            for order, value in each_shift(motion[axis, layer], besides[axis, layer], axis == 2):
                shifts[order, axis, layer, FIRST : FIRST + size_y] = value
        return carry

    lax.fori_loop(0, size_x, fill, 0, unroll=UNROLL_FILL)
    add_inner(extent, False, motion, shifts, weights, total, False if levelled else None)


def force_late_kernel(
    extent, count, edges, motion, early, early_shifts, y_low, y_high, weights,
    total, shifts, halo, besides,
):
    size_x, size_y, _ = extent
    total[...] = early[...]
    middle = slice(FIRST, FIRST + size_y)
    above = FIRST + size_y

    def across(place, at):
        halo[place, 0:REACH] = kept(edges[3], y_high[at : at + REACH])
        halo[place, REACH : 8 - REACH] = jnp.zeros((8 - 2 * REACH, LANES), jnp.float32)
        halo[place, 8 - REACH : 8] = kept(edges[2], y_low[at : at + REACH])

    packs = 3 * size_x
    for order in range(2):
        across(packs + order, (count * size_x + order) * REACH)
    for place in range(3 * size_x):
        across(place, place * REACH)
    low_pack, high_pack = halo[packs], halo[packs + 1]
    for layer in range(size_x):
        for axis in range(3):
            besides[axis * size_x + layer] = beside_columns(
                low_pack, high_pack, layer * SLOT + axis * REACH
            )

    def fill(layer, carry):
        for axis in range(3):
            place = axis * size_x + layer
            for order, value in each_shift(halo[place], besides[place], axis == 2):
                shifts[order, axis, layer, middle] = early_shifts[order, axis, layer, middle]
                shifts[order, axis, layer, FIRST - REACH : FIRST] = value[8 - REACH : 8]
                shifts[order, axis, layer, above : above + REACH] = value[0:REACH]
        return carry

    lax.fori_loop(0, size_x, fill, 0, unroll=UNROLL_FILL)
    add_inner(extent, True, motion, shifts, weights, total)


def finish_kernel(
    extent, count, stage, edges, motion, speed, pressing, inner, weights, x_far, x_near, *refs
):
    size_x, size_y, _ = extent
    if stage == "last":
        motion_out, speed_out, accel_out, total, shifts, besides = refs
    else:
        motion_out, speed_out, z_up, z_down, total, shifts, besides = refs
    total[...] = inner[...] + pressing[...]
    x_low = Either(edges[6], x_near, x_far)
    x_high = Either(edges[6], x_far, x_near)
    fill_outer(extent, count, edges, range(3), x_low, x_high, shifts, besides)
    for step, first, last, bonds, base in outer_plan(extent)[0]:
        for layer in range(first, last):
            slot = base + (layer - first) * len(bonds)
            far_layer = layer + step + (REACH if step < 0 else REACH - size_x)
            add_bonds(bonds, step, layer, far_layer, REACH, motion, shifts, weights, slot, total)
    accel = total[...]
    new_speed = speed[...] + HALF_DT * accel
    if stage == "last":
        motion_out[...] = motion[...]
        speed_out[...] = new_speed
        accel_out[...] = accel
        return
    if stage == "middle":
        new_speed = new_speed + HALF_DT * accel
    speed_out[...] = new_speed
    motion_out[...] = motion[...] + DT_STEP * new_speed
    up, down = pack_columns(lambda axis, layer: motion_out[axis, layer], 3, size_x, size_y)
    z_up[...] = up
    z_down[...] = down


VMEM = pl.BlockSpec(memory_space=pltpu.VMEM)
SMEM = pl.BlockSpec(memory_space=pltpu.SMEM)


def call(kernel, scalars, operands, shapes, scratch=(), name=None, results=(), far=()):
    operands = [pltpu.with_memory_space_constraint(operand, pltpu.HBM) for operand in far] + [
        pltpu.with_memory_space_constraint(operand, pltpu.VMEM) for operand in operands
    ]
    return pl.pallas_call(
        kernel,
        out_shape=[
            jax.ShapeDtypeStruct(shape, jnp.float32)
            if place in results
            else pltpu.VMEM(shape, jnp.float32)
            for place, shape in enumerate(shapes)
        ],
        in_specs=[SMEM] * len(scalars)
        + [pl.BlockSpec(memory_space=pltpu.HBM)] * len(far)
        + [VMEM] * (len(operands) - len(far)),
        out_specs=[VMEM] * len(shapes),
        scratch_shapes=[
            pltpu.VMEM(item, jnp.float32) if isinstance(item, tuple) else item for item in scratch
        ],
        compiler_params=pltpu.CompilerParams(vmem_limit_bytes=24 * 1024 * 1024),
        name=name,
    )(*scalars, *operands)


def sent(value, axis, distance):
    count = lax.axis_size(axis)
    return lax.ppermute(value, axis, [(i, (i + distance) % count) for i in range(count)])


def swapped(near, far):
    count = lax.axis_size("gx")
    side = [1 - 2 * (i % 2) for i in range(count)]
    far = lax.ppermute(far, "gx", [(i, (i - side[i]) % count) for i in range(count)])
    return lax.ppermute(near, "gx", [(i, i + side[i]) for i in range(count)]), far


def on_device(displacement, velocity, stiffness, broken, borehole_id, flags, pressure):
    extent = stiffness.shape
    size_x, size_y, _ = extent
    height = size_y + 8
    tall = size_y + 2 * FIRST
    edges = jnp.stack(
        [
            end
            for axis in ("gz", "gy", "gx")
            for end in (
                (lax.axis_index(axis) > 0).astype(jnp.int32),
                (lax.axis_index(axis) < lax.axis_size(axis) - 1).astype(jnp.int32),
            )
        ]
        + [lax.axis_index("gx") % 2]
    )
    field = (size_x, size_y, LANES)
    vector = (3,) + field
    part = functools.partial

    pack = (size_y + size_x * size_y + PAD, LANES)
    rows_shapes = [(count * size_x + 2 * PAD, LANES) for count in (Y_UP_COUNT, Y_DOWN_COUNT)]
    layers_shape = (X_UP_COUNT * size_y, LANES)
    motion, stiffness, pore, z_up, z_down, rows_up, rows_down, x_up = pl.pallas_call(
        part(start_kernel, extent),
        out_shape=[
            pltpu.VMEM(shape, kind)
            for shape, kind in (
                (vector, jnp.float32), (field, jnp.float32),
                (field, jnp.float32), (pack, jnp.float32), (pack, jnp.float32),
                (rows_shapes[0], jnp.float32), (rows_shapes[1], jnp.float32),
                (layers_shape, jnp.float32),
            )
        ],
        in_specs=[pl.BlockSpec(memory_space=pltpu.HBM)] * 6,
        out_specs=[VMEM] * 8,
        scratch_shapes=[
            pltpu.VMEM(broken.shape, jnp.int32),
            pltpu.SMEM(pressure.shape, jnp.float32),
            pltpu.VMEM(field, jnp.int32),
            pltpu.VMEM(field, jnp.int32),
            pltpu.SemaphoreType.DMA((5,)),
            pltpu.SemaphoreType.DMA((size_x,)),
        ],
        compiler_params=pltpu.CompilerParams(vmem_limit_bytes=24 * 1024 * 1024),
        name="start",
    )(
        *(
            pltpu.with_memory_space_constraint(operand, pltpu.HBM)
            for operand in (pressure, displacement, stiffness, borehole_id, flags, broken)
        )
    )
    z_low = sent(z_up, "gz", 1)
    z_high = sent(z_down, "gz", -1)
    rows_low = sent(rows_up, "gy", 1)
    rows_high = sent(rows_down, "gy", -1)
    x_broken = sent(x_up, "gx", 1)
    rows = (round_up(5 * size_x * REACH + 2 * REACH + 2 * size_x * REACH), LANES)
    y_up, y_down = call(
        part(y_rows_first_kernel, extent), [edges],
        [motion, stiffness, pore, z_low, z_high], [rows, rows], name="y_rows_first",
    )
    y_low = sent(y_up, "gy", 1)
    y_high = sent(y_down, "gy", -1)
    moves = 2 * REACH + 1
    early_slots = inner_plan(extent, False)[1]
    late_slots = inner_plan(extent, True)[1]
    outer_slots = outer_plan(extent)[1]
    weights_early, keeps = call(
        part(weights_early_kernel, extent), [edges], [stiffness, z_low, z_high],
        [(early_slots, 8, LANES), (late_slots, 8, LANES)],
        [
            (moves, size_x, tall, LANES),
            (len(OFFSETS), size_x, tall, LANES),
            field,
            pltpu.VMEM(broken.shape, jnp.int32),
            pltpu.SemaphoreType.DMA((size_x,)),
        ], name="weights_early", far=[broken],
    )

    def force_early(motion, z_low, z_high, *level):
        return call(
            part(force_early_kernel, extent, bool(level)), [edges],
            [motion, z_low, z_high, weights_early, *level],
            [vector, (moves, 3, size_x, tall, LANES)], [vector], name="force_early",
        )

    def force_late(count, motion, early, early_shifts, y_low, y_high):
        return call(
            part(force_late_kernel, extent, count), [edges],
            [motion, early, early_shifts, y_low, y_high, weights_late], [vector],
            [(moves, 3, size_x, tall, LANES), (2 + 3 * size_x, 8, LANES), (3 * size_x, 8, LANES)], name="force_late",
        )[0]

    early, early_shifts = force_early(motion, z_low, z_high)
    y_low, y_high, x_broken, early = lax.optimization_barrier((y_low, y_high, x_broken, early))
    layers = x_place(4, REACH, size_y) + height + size_y
    layers = round_up(layers + 2 * NEAR * height + XY_UP_COUNT)
    wide_static, wide_pack, wide_broken, x_near, x_far = call(
        part(x_layers_first_kernel, extent), [edges],
        [motion, stiffness, pore, z_low, z_high, y_low, y_high, rows_low, rows_high],
        [
            (2, size_x, height, LANES),
            (2, height, LANES),
            (2, size_x, height, LANES),
            (layers, LANES),
            (layers, LANES),
        ], [(3, size_x, height, LANES)], name="x_layers_first",
    )
    x_near, x_far = swapped(x_near, x_far)
    weights_late, pressing = call(
        part(weights_late_kernel, extent), [],
        [stiffness, pore, wide_static, wide_pack, wide_broken, rows_low, rows_high, keeps],
        [(late_slots, 8, LANES), vector],
        [(moves, size_x, height, LANES), (size_x, height, LANES)], name="weights_late",
    )
    inner = force_late(5, motion, early, early_shifts, y_low, y_high)
    outer_weights, pressing = call(
        part(weights_outer_kernel, extent), [edges],
        [stiffness, pore, wide_static, wide_pack, x_up, x_broken, x_far, x_near, pressing],
        [(outer_slots, 8, LANES), vector],
        [
            (moves, 1, 2 * REACH, height, LANES),
            (X_UP_COUNT, height, LANES),
            (1, 2 * REACH, height, LANES),
        ], name="weights_outer",
    )

    def finish(stage, count, motion, speed, inner, x_near, x_far):
        columns = (size_y, LANES)
        shapes = [vector] * 3 if stage == "last" else [vector, vector, columns, columns]
        return call(
            part(finish_kernel, extent, count, stage), [edges],
            [motion, speed, pressing, inner, outer_weights, x_far, x_near],
            shapes,
            [
                vector,
                (moves, 3, 2 * REACH, height, LANES),
                (3, 2 * REACH, height, LANES),
            ], name="finish_" + stage,
            results=(0, 1, 2) if stage == "last" else (),
        )

    motion, speed, z_up, z_down = finish(
        "first", 4, motion, velocity, inner, x_near, x_far
    )
    for step_index in range(STEPS):
        z_low = sent(z_up, "gz", 1)
        z_high = sent(z_down, "gz", -1)
        (level,) = call(
            part(force_level_kernel, extent), [], [motion, weights_early], [vector],
            name="force_level",
        )
        z_low, z_high, level = lax.optimization_barrier((z_low, z_high, level))
        rows = (round_up(3 * size_x * REACH + 2 * REACH), LANES)
        y_up, y_down = call(
            part(y_rows_kernel, extent), [edges], [motion, z_low, z_high], [rows, rows],
            name="y_rows",
        )
        y_low = sent(y_up, "gy", 1)
        y_high = sent(y_down, "gy", -1)
        early, early_shifts = force_early(motion, z_low, z_high, level)
        y_low, y_high, early = lax.optimization_barrier((y_low, y_high, early))
        layers = round_up(x_place(3, REACH, size_y) + height)
        x_near, x_far = call(
            part(x_layers_kernel, extent), [edges],
            [motion, z_low, z_high, y_low, y_high],
            [(layers, LANES), (layers, LANES)],
            [(3, size_x, height, LANES), (2, height, LANES)], name="x_layers",
        )
        x_near, x_far = swapped(x_near, x_far)
        inner = force_late(3, motion, early, early_shifts, y_low, y_high)
        if step_index < STEPS - 1:
            motion, speed, z_up, z_down = finish("middle", 3, motion, speed, inner, x_near, x_far)
        else:
            motion, speed, accel = finish("last", 3, motion, speed, inner, x_near, x_far)
    return (motion, speed, accel)


def solution(mesh):
    in_specs = (
        P(None, "gx", "gy", "gz"),
        P(None, "gx", "gy", "gz"),
        P("gx", "gy", "gz"),
        P(None, "gx", "gy", "gz"),
        P("gx", "gy", "gz"),
        P("gx", "gy", "gz"),
        P(),
    )
    out_specs = (P(None, "gx", "gy", "gz"), P(None, "gx", "gy", "gz"), P(None, "gx", "gy", "gz"))
    return jax.shard_map(
        on_device, mesh=mesh, in_specs=in_specs, out_specs=out_specs, check_vma=False
    )
```
